32 devices in a mesh: dp: 8 (over y, x, core), tp: 4 (over z).
Axes of the slice: x: 2, y: 2, z: 4, core: 2. Of those that a mesh axis runs over, the one named last changes fastest.
Arguments:
- hidden_in: bfloat16 [8, 2048, 2048], P('dp', 'tp'), may hold values from -6 to 6
- triple_projection_weight: bfloat16 [2048, 3, 2048], P('dp', None, 'tp'), may hold values from -0.125 to 0.125
- triple_projection_bias: bfloat16 [3, 256, 8], P(None, 'tp', 'dp'), may hold values from -1 to 1
- attention_out_weight: bfloat16 [2048, 2048], P('tp', 'dp'), may hold values from -1.5 to 1.5
- b_dense: bfloat16 [2048], P('dp'), may hold values from -1 to 1
- feedforward_in_weight: bfloat16 [2048, 8192], P('dp', 'tp'), may hold values from -0.125 to 0.125
- feedforward_in_bias: bfloat16 [1024, 8], P('tp', 'dp'), may hold values from -1 to 1
- feedforward_out_weight: bfloat16 [8192, 2048], P('tp', 'dp'), may hold values from -0.0625 to 0.0625
- b_fc2: bfloat16 [2048], P('dp'), may hold values from -1 to 1
- ln1_gain: bfloat16 [2048], P('dp'), may hold values from 0.5 to 1.5
- ln1_bias: bfloat16 [2048], P('dp'), may hold values from -1 to 1
- ln2_gain: bfloat16 [2048], P('dp'), may hold values from 0.5 to 1.5
- ln2_bias: bfloat16 [2048], P('dp'), may hold values from -1 to 1
- grad_out: bfloat16 [8, 2048, 2048], P('dp', 'tp'), may hold values from -6 to 6
Outputs:
- hidden_out: bfloat16 [8, 2048, 2048], P('dp', 'tp')
- grad_in: float32 [8, 2048, 2048], P('dp', 'tp')
- grad_w_qkv: float32 [2048, 3, 2048], P('dp', None, 'tp')
- grad_b_qkv: float32 [3, 256, 8], P(None, 'tp', 'dp')
- grad_w_dense: float32 [2048, 2048], P('tp', 'dp')
- grad_b_dense: float32 [2048], P('dp')
- grad_w_fc1: float32 [2048, 8192], P('dp', 'tp')
- grad_b_fc1: float32 [1024, 8], P('tp', 'dp')
- grad_w_fc2: float32 [8192, 2048], P('tp', 'dp')
- grad_b_fc2: float32 [2048], P('dp')
- grad_ln1_gain: float32 [2048], P('dp')
- grad_ln1_bias: float32 [2048], P('dp')
- grad_ln2_gain: float32 [2048], P('dp')
- grad_ln2_bias: float32 [2048], P('dp')
The draws below stay inside these ranges and needn't reach their ends.
All inputs are finite; a program needn't handle non-finite values.
Results may differ from the reference program's by a relative error of at most 0.0097.
Values may be sent and summed in bfloat16 or wider, within the bound.
A program may use at most 320 MiB of HBM per device.

```python
import math
import jax
import jax.numpy as jnp
from jax import lax

D = 2048
HEADS = 8
ROT = 64
FF = 8192
LEN = 2048
BATCH = 8
N_DP = 8


def level_of(own_key, dims, cuts, low, largest):
    loudness = 1.0
    for dim, blocks in cuts:
        heights = jax.random.uniform(jax.random.fold_in(jax.random.fold_in(own_key, 6), dim), (blocks,), jnp.float32, low / len(cuts), largest / len(cuts))
        loudness = loudness * jnp.repeat(jnp.exp(heights), dims[dim] // blocks).reshape((-1,) + (1,) * (len(dims) - 1 - dim))
    return loudness


def gaussian(stream_key, extent, spread, most, pieces=(), kind=jnp.bfloat16):
    entries = jax.random.normal(stream_key, extent, jnp.float32) * spread
    if len(pieces) > 0:
        entries = level_of(stream_key, extent, pieces, -0.22, 0.18) * entries
    return jnp.clip(entries, min=-most, max=most).astype(kind)


def setup_inputs(seed: int = 0) -> dict:
    keys = jax.random.split(jax.random.key(seed), 15)
    hidden_in = gaussian(keys[0], (BATCH, LEN, D), 1.0, 6.0, ((0, 8), (1, 4)))
    triple_projection_weight = gaussian(keys[1], (D, 3, D), D ** -0.5, 0.125, ((0, 8), (2, 4)))
    triple_projection_bias = gaussian(keys[2], (3, D // N_DP, N_DP), 0.2, 1.0, ((1, 4), (2, 8)))
    attention_out_weight = gaussian(keys[3], (D, D), (D // 128) ** -0.5, 1.5, ((0, 4), (1, 8)))
    b_dense = gaussian(keys[4], (D,), 0.2, 1.0, ((0, 8),))
    feedforward_in_weight = gaussian(keys[5], (D, FF), D ** -0.5, 0.125, ((0, 8), (1, 4)))
    feedforward_in_bias = gaussian(keys[6], (FF // N_DP, N_DP), 0.2, 1.0, ((0, 4), (1, 8)))
    feedforward_out_weight = gaussian(keys[7], (FF, D), FF ** -0.5, 0.0625, ((0, 4), (1, 8)))
    b_fc2 = gaussian(keys[8], (D,), 0.2, 1.0, ((0, 8),))
    ln1_gain = jnp.clip(1.0 + 0.1 * jax.random.normal(keys[9], (D,), jnp.float32), 0.5, 1.5).astype(jnp.bfloat16)
    ln1_bias = gaussian(keys[10], (D,), 0.2, 1.0, ((0, 8),))
    ln2_gain = jnp.clip(1.0 + 0.1 * jax.random.normal(keys[11], (D,), jnp.float32), 0.5, 1.5).astype(jnp.bfloat16)
    ln2_bias = gaussian(keys[12], (D,), 0.2, 1.0, ((0, 8),))
    grad_out = gaussian(keys[13], (BATCH, LEN, D), 1.0, 6.0, ((0, 8), (1, 4)))
    return {"hidden_in": hidden_in, "triple_projection_weight": triple_projection_weight, "triple_projection_bias": triple_projection_bias, "attention_out_weight": attention_out_weight, "b_dense": b_dense, "feedforward_in_weight": feedforward_in_weight, "feedforward_in_bias": feedforward_in_bias, "feedforward_out_weight": feedforward_out_weight, "b_fc2": b_fc2, "ln1_gain": ln1_gain, "ln1_bias": ln1_bias, "ln2_gain": ln2_gain, "ln2_bias": ln2_bias, "grad_out": grad_out}


EPSILON = 1e-05
MASKED = -1e+30
BEST_PRECISION = lax.Precision.HIGHEST

@jax.custom_vjp
def low(v):
    return lax.optimization_barrier(v.astype(jnp.bfloat16)).astype(jnp.float32)

@jax.custom_vjp
def reduced_backward(v):
    return v

def low_keep(v):
    return (low(v), None)

def low_pass(kept, grad):
    return (grad,)

def back_keep(v):
    return (v, None)

def back_low(kept, grad):
    return (low(grad),)
low.defvjp(low_keep, low_pass)
reduced_backward.defvjp(back_keep, back_low)

def norm_rows(resid, gain_vec, shift_vec):
    row_mean = lax.optimization_barrier(jnp.mean(resid, axis=-1, keepdims=True))
    centered = resid - row_mean
    variance = lax.optimization_barrier(jnp.mean(centered * centered, axis=-1, keepdims=True))
    return centered * lax.rsqrt(variance + EPSILON) * gain_vec + shift_vec

def rotary_tables(length, rot_dims):
    half_rot = rot_dims // 2
    exponent = jnp.arange(half_rot, dtype=jnp.float32) * (2.0 / rot_dims)
    inverse = jnp.exp(exponent * -math.log(10000.0))
    position = jnp.arange(length, dtype=jnp.float32)
    angle = position[:, None] * inverse[None, :]
    angle = jnp.concatenate([angle, angle], axis=1)
    return (jnp.cos(angle), jnp.sin(angle))

def rotate(part, cosine, sine_tab):
    rot_dims = cosine.shape[1]
    half_rot = rot_dims // 2
    rot_part = part[..., :rot_dims]
    turned = jnp.concatenate([-rot_part[..., half_rot:], rot_part[..., :half_rot]], axis=-1)
    moved = rot_part * cosine[:, None, :] + turned * sine_tab[:, None, :]
    return jnp.concatenate([moved, part[..., rot_dims:]], axis=-1)

def gelu_exact(value):
    return 0.5 * value * (1.0 + lax.erf(value * (1.0 / math.sqrt(2.0))))

def attend_block(query_blk, row_start, key_rows, value_rows):
    score_scale = query_blk.shape[-1] ** (-0.5)
    scores = jnp.einsum('sqhd,skhd->shqk', query_blk, key_rows, precision=BEST_PRECISION) * score_scale
    scores = reduced_backward(scores)
    row_pos = row_start + jnp.arange(query_blk.shape[1], dtype=jnp.int32)
    col_pos = jnp.arange(key_rows.shape[1], dtype=jnp.int32)
    scores = jnp.where(col_pos[None, None, None, :] <= row_pos[None, None, :, None], scores, MASKED)
    row_max = lax.optimization_barrier(jnp.max(scores, axis=-1, keepdims=True))
    exp_scores = jnp.exp(scores - row_max)
    probabilities = exp_scores / lax.optimization_barrier(jnp.sum(exp_scores, axis=-1, keepdims=True))
    return jnp.einsum('shqk,skhd->sqhd', low(probabilities), value_rows, precision=BEST_PRECISION)

def layer_fn(params, resid_in):
    triple_projection_weight, triple_projection_bias, attention_out_weight, b_dense, feedforward_in_weight, feedforward_in_bias, feedforward_out_weight, b_fc2, ln1_gain, ln1_bias, ln2_gain, ln2_bias = params
    seq_count, length, hidden_width = resid_in.shape
    head_dim = hidden_width // HEADS
    attention_norm = low(norm_rows(resid_in, ln1_gain, ln1_bias))
    feedforward_norm = low(norm_rows(resid_in, ln2_gain, ln2_bias))
    triple_linear = jnp.einsum('bfk,kie->bfie', attention_norm, triple_projection_weight, precision=BEST_PRECISION) + triple_projection_bias.reshape(3, hidden_width)
    triple_linear = reduced_backward(triple_linear).reshape(seq_count, length, 3, HEADS, head_dim)
    cosine, sine_tab = rotary_tables(length, ROT)
    query_rows = low(rotate(triple_linear[:, :, 0], cosine, sine_tab))
    key_rows = low(rotate(triple_linear[:, :, 1], cosine, sine_tab))
    value_rows = low(triple_linear[:, :, 2])
    block_rows = min(512, length)
    block_count = length // block_rows
    query_blocks = query_rows.reshape(seq_count, block_count, block_rows, HEADS, head_dim).transpose(1, 0, 2, 3, 4)
    starts = jnp.arange(block_count, dtype=jnp.int32) * block_rows

    def one_block(block_item):
        return attend_block(block_item[0], block_item[1], key_rows, value_rows)
    attended = lax.map(jax.checkpoint(one_block), (query_blocks, starts))
    attended = attended.transpose(1, 0, 2, 3, 4).reshape(seq_count, length, hidden_width)
    head_output_rows = low(reduced_backward(attended))
    feedforward_entry = reduced_backward(jnp.einsum('wqt,tn->wqn', feedforward_norm, feedforward_in_weight, precision=BEST_PRECISION) + feedforward_in_bias.reshape(-1))
    activation_result = low(gelu_exact(feedforward_entry))
    parallel_branch = jnp.einsum('iox,xe->ioe', head_output_rows, attention_out_weight, precision=BEST_PRECISION)
    parallel_branch = parallel_branch + jnp.einsum('azv,vx->azx', activation_result, feedforward_out_weight, precision=BEST_PRECISION)
    return resid_in + parallel_branch + b_dense + b_fc2

def reference(hidden_in, triple_projection_weight, triple_projection_bias, attention_out_weight, b_dense, feedforward_in_weight, feedforward_in_bias, feedforward_out_weight, b_fc2, ln1_gain, ln1_bias, ln2_gain, ln2_bias, grad_out):
    params = tuple((source.astype(jnp.float32) for source in (triple_projection_weight, triple_projection_bias, attention_out_weight, b_dense, feedforward_in_weight, feedforward_in_bias, feedforward_out_weight, b_fc2, ln1_gain, ln1_bias, ln2_gain, ln2_bias)))
    batch_size, length, hidden_width = hidden_in.shape
    group_size = math.gcd(batch_size, max(1, 4096 // length))
    resid_all = hidden_in.astype(jnp.float32).reshape(batch_size // group_size, group_size, length, hidden_width)
    cot_all = grad_out.astype(jnp.float32).reshape(batch_size // group_size, group_size, length, hidden_width)

    def scan_step(totals, block_item):
        layer_out, pullback = jax.vjp(layer_fn, params, block_item[0])
        param_grads, input_grad = pullback(block_item[1])
        totals = jax.tree.map(lambda first_sum, second_sum: first_sum + second_sum, totals, param_grads)
        return (totals, (layer_out.astype(jnp.bfloat16), input_grad))
    start_totals = jax.tree.map(jnp.zeros_like, params)
    totals, (layer_outs, input_grads) = lax.scan(scan_step, start_totals, (resid_all, cot_all))
    hidden_out = layer_outs.reshape(batch_size, length, hidden_width)
    grad_in = input_grads.reshape(batch_size, length, hidden_width)
    return (hidden_out, grad_in, totals[0], totals[1], totals[2], totals[3], totals[4], totals[5], totals[6], totals[7], totals[8], totals[9], totals[10], totals[11])
```

```python
import math

import jax
import jax.numpy as jnp
from jax import lax
from jax.sharding import PartitionSpec as P

HD = 256
ROT = 64


EPSILON = 1e-05
MASKED = -1e30


def norm_rows(resid, gain_vec, shift_vec):
    row_mean = jnp.mean(resid, axis=-1, keepdims=True)
    centered = resid - row_mean
    variance = jnp.mean(centered * centered, axis=-1, keepdims=True)
    return centered * lax.rsqrt(variance + EPSILON) * gain_vec + shift_vec


def norm_pull(resid, gain_vec, shift_vec, upstream):
    _, pullback = jax.vjp(norm_rows, resid, gain_vec, shift_vec)
    return pullback(upstream)


def rotary_tables(length, rot_dims):
    half_rot = rot_dims // 2
    exponent = jnp.arange(half_rot, dtype=jnp.float32) * (2.0 / rot_dims)
    inverse = jnp.exp(exponent * -math.log(10000.0))
    position = jnp.arange(length, dtype=jnp.float32)
    angle = position[:, None] * inverse[None, :]
    angle = jnp.concatenate([angle, angle], axis=1)
    return (jnp.cos(angle), jnp.sin(angle))


def rotate(part, cosine, sine_tab):
    rot_dims = cosine.shape[1]
    half_rot = rot_dims // 2
    rot_part = part[..., :rot_dims]
    turned = jnp.concatenate([-rot_part[..., half_rot:], rot_part[..., :half_rot]], axis=-1)
    moved = rot_part * cosine[:, None, :] + turned * sine_tab[:, None, :]
    return jnp.concatenate([moved, part[..., rot_dims:]], axis=-1)


def rotate_back(upstream, cosine, sine_tab):
    rot_dims = cosine.shape[1]
    half_rot = rot_dims // 2
    rot_part = upstream[..., :rot_dims]
    turned = rot_part * sine_tab[:, None, :]
    swapped = jnp.concatenate([turned[..., half_rot:], -turned[..., :half_rot]], axis=-1)
    moved = rot_part * cosine[:, None, :] + swapped
    return jnp.concatenate([moved, upstream[..., rot_dims:]], axis=-1)


def gelu_exact(value):
    return 0.5 * value * (1.0 + lax.erf(value * (1.0 / math.sqrt(2.0))))


def mask_scores(scores, row_start, key_count):
    row_pos = row_start + jnp.arange(scores.shape[1], dtype=jnp.int32)
    col_pos = jnp.arange(key_count, dtype=jnp.int32)
    return jnp.where(col_pos[None, None, :] <= row_pos[None, :, None], scores, MASKED)


def attend_forward(query_rows, key_rows, value_rows, block_rows, score_scale):
    head_parts = []
    log_parts = []
    for row_start in range(0, query_rows.shape[0], block_rows):
        query_blk = query_rows[row_start : row_start + block_rows]
        scores = (
            jnp.einsum("qhd,khd->hqk", query_blk, key_rows, preferred_element_type=jnp.float32)
            * score_scale
        )
        scores = mask_scores(scores, row_start, key_rows.shape[0])
        row_max = jnp.max(scores, axis=-1, keepdims=True)
        exp_scores = jnp.exp(scores - row_max)
        row_total = jnp.sum(exp_scores, axis=-1, keepdims=True)
        probabilities = (exp_scores / row_total).astype(jnp.bfloat16)
        attended = jnp.einsum(
            "hqk,khd->qhd", probabilities, value_rows, preferred_element_type=jnp.float32
        )
        head_parts.append(attended.astype(jnp.bfloat16))
        log_parts.append(row_max + jnp.log(row_total))
    return (jnp.concatenate(head_parts, axis=0), jnp.concatenate(log_parts, axis=1))


def attend_backward(query_rows, key_rows, value_rows, log_total, d_heads, block_rows, score_scale):
    query_parts = []
    d_keys = jnp.zeros(key_rows.shape, jnp.float32)
    d_values = jnp.zeros(value_rows.shape, jnp.float32)
    for row_start in range(0, query_rows.shape[0], block_rows):
        query_blk = query_rows[row_start : row_start + block_rows]
        grad_blk = d_heads[row_start : row_start + block_rows]
        scores = (
            jnp.einsum("qhd,khd->hqk", query_blk, key_rows, preferred_element_type=jnp.float32)
            * score_scale
        )
        scores = mask_scores(scores, row_start, key_rows.shape[0])
        probabilities = jnp.exp(scores - log_total[:, row_start : row_start + block_rows])
        low_probs = probabilities.astype(jnp.bfloat16)
        d_probs = jnp.einsum(
            "qhd,khd->hqk", grad_blk, value_rows, preferred_element_type=jnp.float32
        )
        inner = jnp.sum(probabilities * d_probs, axis=-1, keepdims=True)
        d_scores = (probabilities * (d_probs - inner)).astype(jnp.bfloat16)
        query_parts.append(
            jnp.einsum("hqk,khd->qhd", d_scores, key_rows, preferred_element_type=jnp.float32)
            * score_scale
        )
        d_keys = (
            d_keys
            + jnp.einsum("hqk,qhd->khd", d_scores, query_blk, preferred_element_type=jnp.float32)
            * score_scale
        )
        d_values = d_values + jnp.einsum(
            "hqk,qhd->khd", low_probs, grad_blk, preferred_element_type=jnp.float32
        )
    return (jnp.concatenate(query_parts, axis=0), d_keys, d_values)


def low(value):
    return value.astype(jnp.bfloat16)


def gather_small(parts):
    flat = jnp.concatenate([part.reshape(-1) for part in parts])
    every = lax.all_gather(flat, "dp", axis=0, tiled=False)
    out = []
    start = 0
    for part in parts:
        out.append(every[:, start : start + part.size])
        start += part.size
    return out


def body(
    hidden_in,
    triple_projection_weight,
    triple_projection_bias,
    attention_out_weight,
    b_dense,
    feedforward_in_weight,
    feedforward_in_bias,
    feedforward_out_weight,
    b_fc2,
    ln1_gain,
    ln1_bias,
    ln2_gain,
    ln2_bias,
    grad_out,
):
    seq_count, piece_len, hidden_width = hidden_in.shape
    tp_count = lax.axis_size("tp")
    dp_count = lax.axis_size("dp")
    length = piece_len * tp_count
    local_heads = triple_projection_weight.shape[2] // HD
    block_rows = min(512, length)
    score_scale = HD ** (-0.5)
    cosine, sine_tab = rotary_tables(length, ROT)
    small = gather_small(
        [
            triple_projection_bias,
            feedforward_in_bias,
            b_dense,
            b_fc2,
            ln1_gain,
            ln1_bias,
            ln2_gain,
            ln2_bias,
        ]
    )
    full_bqkv = small[0].T.reshape(-1).astype(jnp.float32)
    full_bfc1 = small[1].T.reshape(-1).astype(jnp.float32)
    full_bdense, full_bfc2, gain_one, shift_one, gain_two, shift_two = [
        part.reshape(-1).astype(jnp.float32) for part in small[2:]
    ]
    x_seq = lax.all_gather(hidden_in, "tp", axis=1, tiled=True)[0]
    full_qkv = lax.all_gather(triple_projection_weight, "dp", axis=0, tiled=True)
    full_qkv = full_qkv.reshape(hidden_width, -1)
    full_fc1 = lax.all_gather(feedforward_in_weight, "dp", axis=0, tiled=True)
    full_dense = lax.all_gather(attention_out_weight, "dp", axis=1, tiled=True)
    full_fc2 = lax.all_gather(feedforward_out_weight, "dp", axis=1, tiled=True)
    cot_seq = lax.all_gather(grad_out, "tp", axis=1, tiled=True)[0]

    x_f32 = x_seq.astype(jnp.float32)
    mean = jnp.mean(x_f32, axis=-1, keepdims=True)
    centered = x_f32 - mean
    rstd = lax.rsqrt(jnp.mean(centered * centered, axis=-1, keepdims=True) + EPSILON)
    xhat = centered * rstd
    attention_norm = low(xhat * gain_one + shift_one)
    feedforward_norm = low(xhat * gain_two + shift_two)

    triple_linear = (
        jnp.dot(attention_norm, full_qkv, preferred_element_type=jnp.float32) + full_bqkv
    )
    triple_linear = triple_linear.reshape(length, 3, local_heads, HD)
    query_rows = low(rotate(triple_linear[:, 0], cosine, sine_tab))
    key_rows = low(rotate(triple_linear[:, 1], cosine, sine_tab))
    value_rows = low(triple_linear[:, 2])
    head_output_rows, log_total = attend_forward(
        query_rows, key_rows, value_rows, block_rows, score_scale
    )
    heads_flat = head_output_rows.reshape(length, -1)
    feedforward_entry = (
        jnp.dot(feedforward_norm, full_fc1, preferred_element_type=jnp.float32) + full_bfc1
    )
    activation_result = low(gelu_exact(feedforward_entry))
    partial_value = jnp.dot(heads_flat, full_dense, preferred_element_type=jnp.float32)
    partial_value = partial_value + jnp.dot(
        activation_result, full_fc2, preferred_element_type=jnp.float32
    )
    summed = lax.psum_scatter(low(partial_value), "tp", scatter_dimension=0, tiled=True)
    layer_out = (
        hidden_in[0].astype(jnp.float32) + summed.astype(jnp.float32) + full_bdense + full_bfc2
    )
    hidden_out = low(layer_out)[None]

    d_heads = low(
        jnp.einsum("ld,jd->lj", cot_seq, full_dense, preferred_element_type=jnp.float32)
    )
    d_act = jnp.einsum("ld,fd->lf", cot_seq, full_fc2, preferred_element_type=jnp.float32)
    _, gelu_pull = jax.vjp(gelu_exact, feedforward_entry)
    d_fc = low(gelu_pull(d_act)[0])
    d_norm_two = jnp.einsum("lf,df->ld", d_fc, full_fc1, preferred_element_type=jnp.float32)
    d_query, d_keys, d_values = attend_backward(
        query_rows,
        key_rows,
        value_rows,
        log_total,
        d_heads.reshape(length, local_heads, HD),
        block_rows,
        score_scale,
    )
    d_qkv = jnp.stack(
        [rotate_back(d_query, cosine, sine_tab), rotate_back(d_keys, cosine, sine_tab), d_values],
        axis=1,
    )
    d_qkv = low(d_qkv).reshape(length, -1)
    d_norm_one = jnp.einsum("lj,dj->ld", d_qkv, full_qkv, preferred_element_type=jnp.float32)
    e_sum = low(d_norm_one * gain_one + d_norm_two * gain_two)
    ln_sums = jnp.stack(
        [
            jnp.sum(d_norm_one * xhat, axis=0),
            jnp.sum(d_norm_one, axis=0),
            jnp.sum(d_norm_two * xhat, axis=0),
            jnp.sum(d_norm_two, axis=0),
        ]
    )
    e_piece = lax.psum_scatter(e_sum, "tp", scatter_dimension=0, tiled=True).astype(jnp.float32)

    sum_fc2 = low(
        jnp.einsum("lf,ld->fd", activation_result, cot_seq, preferred_element_type=jnp.float32)
    )
    sum_dense = low(
        jnp.einsum("lj,ld->jd", heads_flat, cot_seq, preferred_element_type=jnp.float32)
    )
    sum_fc1 = low(
        jnp.einsum("ld,lf->df", feedforward_norm, d_fc, preferred_element_type=jnp.float32)
    )
    sum_wqkv = low(
        jnp.einsum("ld,lj->dj", attention_norm, d_qkv, preferred_element_type=jnp.float32)
    )
    own_fc2 = lax.psum_scatter(sum_fc2, "dp", scatter_dimension=1, tiled=True)
    own_dense = lax.psum_scatter(sum_dense, "dp", scatter_dimension=1, tiled=True)
    own_fc1 = lax.psum_scatter(sum_fc1, "dp", scatter_dimension=0, tiled=True)
    own_wqkv = lax.psum_scatter(
        sum_wqkv.reshape(hidden_width, 3, -1), "dp", scatter_dimension=0, tiled=True
    )

    cot_piece = grad_out[0].astype(jnp.float32)
    x_own = hidden_in[0].astype(jnp.float32)
    own_mean = jnp.mean(x_own, axis=-1, keepdims=True)
    own_centered = x_own - own_mean
    own_rstd = lax.rsqrt(
        jnp.mean(own_centered * own_centered, axis=-1, keepdims=True) + EPSILON
    )
    own_xhat = own_centered * own_rstd
    back = (
        e_piece
        - jnp.mean(e_piece, axis=-1, keepdims=True)
        - own_xhat * jnp.mean(e_piece * own_xhat, axis=-1, keepdims=True)
    ) * own_rstd
    grad_in = (cot_piece + back)[None]

    me = lax.axis_index("dp")
    sum_bias_out = jnp.sum(cot_piece, axis=0)
    shared = jnp.concatenate([ln_sums.reshape(-1), sum_bias_out])
    shared = lax.psum(shared, ("dp", "tp")).reshape(5, dp_count, -1)
    shared = lax.dynamic_index_in_dim(shared, me, axis=1, keepdims=False)
    sum_bqkv = jnp.sum(d_qkv.astype(jnp.float32), axis=0)
    sum_bfc1 = jnp.sum(d_fc.astype(jnp.float32), axis=0)
    split = sum_bqkv.size
    mine = lax.psum(jnp.concatenate([sum_bqkv, sum_bfc1]), "dp").reshape(-1, dp_count)
    mine = lax.dynamic_index_in_dim(mine, me, axis=1, keepdims=True)
    own_bqkv = mine[: split // dp_count].reshape(3, -1, 1)
    own_bfc1 = mine[split // dp_count :]
    wide = jnp.float32
    return (
        hidden_out,
        grad_in,
        own_wqkv.astype(wide),
        own_bqkv,
        own_dense.astype(wide),
        shared[4],
        own_fc1.astype(wide),
        own_bfc1,
        own_fc2.astype(wide),
        shared[4],
        shared[0],
        shared[1],
        shared[2],
        shared[3],
    )


def solution(mesh):
    return jax.shard_map(
        body,
        mesh=mesh,
        in_specs=(
            P("dp", "tp", None),
            P("dp", None, "tp"),
            P(None, "tp", "dp"),
            P("tp", "dp"),
            P("dp"),
            P("dp", "tp"),
            P("tp", "dp"),
            P("tp", "dp"),
            P("dp"),
            P("dp"),
            P("dp"),
            P("dp"),
            P("dp"),
            P("dp", "tp", None),
        ),
        out_specs=(
            P("dp", "tp", None),
            P("dp", "tp", None),
            P("dp", None, "tp"),
            P(None, "tp", "dp"),
            P("tp", "dp"),
            P("dp"),
            P("dp", "tp"),
            P("tp", "dp"),
            P("tp", "dp"),
            P("dp"),
            P("dp"),
            P("dp"),
            P("dp"),
            P("dp"),
        ),
        check_vma=False,
    )
```

```python
import functools
import math

import jax
import jax.numpy as jnp
import numpy as np
from jax import lax
from jax.experimental import pallas as pl
from jax.experimental.pallas import tpu as pltpu
from jax.sharding import PartitionSpec as P

MESH = pl.DeviceIdType.MESH
EPSILON = 1e-05
MASKED = -1e30
HD = 256
ROT = 64
VMEM_LIMIT = 60 * 1024 * 1024
LOG2E = 1.4426950408889634


def low(value):
    return value.astype(jnp.bfloat16)


def dot_nn(a, b):
    return lax.dot_general(a, b, (((1,), (0,)), ((), ())), preferred_element_type=jnp.float32)


def dot_nt(a, b):
    return lax.dot_general(a, b, (((1,), (1,)), ((), ())), preferred_element_type=jnp.float32)


def dot_tn(a, b):
    return lax.dot_general(a, b, (((0,), (0,)), ((), ())), preferred_element_type=jnp.float32)


def rotary_tables(length):
    half = ROT // 2
    exponent = np.arange(half, dtype=np.float32) * np.float32(2.0 / ROT)
    inverse = np.exp(exponent * np.float32(-math.log(10000.0)), dtype=np.float32)
    angle = np.arange(length, dtype=np.float32)[:, None] * inverse[None, :]
    cosine = np.ones((length, 128), np.float32)
    sine = np.zeros((length, 128), np.float32)
    cosine[:, :half] = cosine[:, half:ROT] = np.cos(angle)
    sine[:, :half] = -np.sin(angle)
    sine[:, half:ROT] = np.sin(angle)
    return jnp.asarray(cosine), jnp.asarray(sine)


def turned(part):
    half = ROT // 2
    lane = lax.broadcasted_iota(jnp.int32, part.shape, 1)
    return jnp.where(
        lane < half, pltpu.roll(part, 128 - half, 1), pltpu.roll(part, half, 1)
    )


def front_kernel(
    heads, x_ref, gains_ref, wq_ref, bq_ref, w1_ref, b1_ref, cos_ref, sin_ref,
    n1_ref, n2_ref, q_ref, k_ref, v_ref, act_ref, slope_ref, stat_ref,
):
    x = x_ref[...].astype(jnp.float32)
    mean = jnp.mean(x, axis=1, keepdims=True)
    centered = x - mean
    rstd = lax.rsqrt(jnp.mean(centered * centered, axis=1, keepdims=True) + EPSILON)
    xhat = centered * rstd
    n1_ref[...] = low(xhat * gains_ref[0:1] + gains_ref[1:2])
    n2_ref[...] = low(xhat * gains_ref[2:3] + gains_ref[3:4])
    lane = lax.broadcasted_iota(jnp.int32, stat_ref.shape, 1)
    stat_ref[...] = jnp.where(lane == 0, mean, rstd)
    width = heads * HD
    cosine, sine = cos_ref[...], sin_ref[...]
    for which, out in enumerate((q_ref, k_ref, v_ref)):
        for head in range(heads):
            at = which * width + head * HD
            raw = dot_nn(n1_ref[...], wq_ref[:, at : at + HD]) + bq_ref[:, at : at + HD]
            if which < 2:
                first = raw[:, :128]
                first = first * cosine + turned(first) * sine
                out[:, head * HD : head * HD + 128] = low(first)
                out[:, head * HD + 128 : (head + 1) * HD] = low(raw[:, 128:])
            else:
                out[:, head * HD : (head + 1) * HD] = low(raw)
    step = 256
    for at in range(0, w1_ref.shape[1], step):
        u = dot_nn(n2_ref[...], w1_ref[:, at : at + step]) + b1_ref[:, at : at + step]
        cdf = 0.5 * (1.0 + lax.erf(u * (1.0 / math.sqrt(2.0))))
        pdf = jnp.exp(-0.5 * u * u) * (1.0 / math.sqrt(2.0 * math.pi))
        act_ref[:, at : at + step] = low(u * cdf)
        slope_ref[:, at : at + step] = low(cdf + u * pdf)


def front(x, gains, wq, bq, w1, b1, cosine, sine, heads, rows=256):
    length, width = x.shape
    ff = w1.shape[1]
    qw = heads * HD
    bf = jnp.bfloat16
    whole = lambda *shape: pl.BlockSpec(shape, lambda i: (0,) * len(shape), pipeline_mode=pl.Buffered(1))
    row = lambda n: pl.BlockSpec((rows, n), lambda i: (i, 0))
    sds = lambda n, t: jax.ShapeDtypeStruct((length, n), t)
    return pl.pallas_call(
        functools.partial(front_kernel, heads),
        grid=(length // rows,),
        in_specs=[
            row(width), whole(*gains.shape), whole(*wq.shape), whole(*bq.shape),
            whole(*w1.shape), whole(*b1.shape), row(128), row(128),
        ],
        out_specs=[row(width), row(width), row(qw), row(qw), row(qw), row(ff), row(ff), row(128)],
        out_shape=[
            sds(width, bf), sds(width, bf), sds(qw, bf), sds(qw, bf), sds(qw, bf),
            sds(ff, bf), sds(ff, bf), sds(128, jnp.float32),
        ],
        compiler_params=pltpu.CompilerParams(vmem_limit_bytes=VMEM_LIMIT),
        cost_estimate=pl.CostEstimate(
            flops=2 * length * width * (3 * qw + ff), bytes_accessed=60_000_000,
            transcendentals=2 * length * ff),
        name="front",
    )(x, gains, wq, bq, w1, b1, cosine, sine)


def attend_kernel(heads, block, q_ref, k_ref, v_ref, o_ref, lse_ref):
    i = pl.program_id(0)
    scale = LOG2E * HD ** -0.5
    qs = [q_ref[:, h * HD : (h + 1) * HD] for h in range(heads)]

    def one(h, j, state, diagonal):
        top, total, acc = state
        rows = pl.ds(pl.multiple_of(j * block, block), block)
        key = k_ref[rows, h * HD : (h + 1) * HD]
        value = v_ref[rows, h * HD : (h + 1) * HD]
        s = dot_nt(key, qs[h]) * scale
        if diagonal:
            kp = lax.broadcasted_iota(jnp.int32, s.shape, 0)
            qp = lax.broadcasted_iota(jnp.int32, s.shape, 1)
            s = jnp.where(kp <= qp, s, MASKED)
        new_top = jnp.maximum(top, jnp.max(s, axis=0, keepdims=True))
        p = jnp.exp2(s - new_top)
        shrink = jnp.exp2(top - new_top)
        total = total * shrink + jnp.sum(p, axis=0, keepdims=True)
        acc = acc * shrink + dot_tn(value, low(p))
        return new_top, total, acc

    def start():
        return (
            jnp.full((1, block), MASKED, jnp.float32),
            jnp.zeros((1, block), jnp.float32),
            jnp.zeros((HD, block), jnp.float32),
        )

    def step(j, states):
        return tuple(one(h, j, states[h], False) for h in range(heads))

    states = lax.fori_loop(0, i, step, tuple(start() for _ in range(heads)))
    states = [one(h, i, states[h], True) for h in range(heads)]
    for h in range(heads):
        top, total, acc = states[h]
        o_ref[:, h * HD : (h + 1) * HD] = low((acc / total).T)
        lse_ref[h : h + 1, :] = top + jnp.log2(total)


def attend(q, k, v, heads, block=512):
    length, width = q.shape
    block = min(block, length)
    whole = pl.BlockSpec((length, width), lambda i: (0, 0), pipeline_mode=pl.Buffered(1))
    row = pl.BlockSpec((block, width), lambda i: (i, 0))
    return pl.pallas_call(
        functools.partial(attend_kernel, heads, block),
        grid=(length // block,),
        in_specs=[row, whole, whole],
        out_specs=[row, pl.BlockSpec((heads, block), lambda i: (0, i))],
        out_shape=[
            jax.ShapeDtypeStruct((length, width), jnp.bfloat16),
            jax.ShapeDtypeStruct((heads, length), jnp.float32),
        ],
        compiler_params=pltpu.CompilerParams(vmem_limit_bytes=VMEM_LIMIT),
        cost_estimate=pl.CostEstimate(
            flops=2 * length * length * width, bytes_accessed=8 * length * width,
            transcendentals=length * length * heads // 2),
        name="attend",
    )(q, k, v)


def attend_back_kernel(
    heads, block, q_ref, k_ref, v_ref, o_ref, do_ref, lse_ref, cos_ref, sin_ref,
    dqkv_ref, sums_ref, dq_acc, dk_acc, dv_acc, delta_ref,
):
    length = q_ref.shape[0]
    blocks = length // block
    scale = HD ** -0.5
    width = heads * HD
    for i in range(blocks):
        rows = slice(i * block, (i + 1) * block)
        for h in range(heads):
            cols = slice(h * HD, (h + 1) * HD)
            inner = jnp.sum(
                do_ref[rows, cols].astype(jnp.float32) * o_ref[rows, cols].astype(jnp.float32),
                axis=1, keepdims=True)
            delta_ref[h : h + 1, rows] = jnp.broadcast_to(inner, (block, 128)).T[0:1]
    dq_acc[...] = jnp.zeros_like(dq_acc)

    def one(h, i, j, diagonal):
        cols = slice(h * HD, (h + 1) * HD)
        qrows = pl.ds(pl.multiple_of(i * block, block), block)
        krows = pl.ds(pl.multiple_of(j * block, block), block)
        query, grad = q_ref[qrows, cols], do_ref[qrows, cols]
        key, value = k_ref[krows, cols], v_ref[krows, cols]
        s = dot_nt(key, query) * (scale * LOG2E)
        p = jnp.exp2(s - lse_ref[h : h + 1, qrows])
        if diagonal:
            kp = lax.broadcasted_iota(jnp.int32, s.shape, 0)
            qp = lax.broadcasted_iota(jnp.int32, s.shape, 1)
            p = jnp.where(kp <= qp, p, 0.0)
        dp = dot_nt(value, grad)
        ds = low(p * (dp - delta_ref[h : h + 1, qrows]))
        dv = dot_nn(low(p), grad)
        dk = dot_nn(ds, query)
        dq_acc[qrows, cols] += dot_tn(ds, key)
        if diagonal:
            dv_acc[krows, cols] = dv
            dk_acc[krows, cols] = dk
        else:
            dv_acc[krows, cols] += dv
            dk_acc[krows, cols] += dk

    def outer(j, carry):
        for h in range(heads):
            one(h, j, j, True)

        def inner(i, c):
            for h in range(heads):
                one(h, i, j, False)
            return c

        lax.fori_loop(j + 1, blocks, inner, 0)
        return carry

    lax.fori_loop(0, blocks, outer, 0)
    sums_ref[...] = jnp.zeros_like(sums_ref)

    def finish(i, carry):
        rows = pl.ds(pl.multiple_of(i * block, block), block)
        cosine, sine = cos_ref[rows, :], sin_ref[rows, :]
        for which, acc in enumerate((dq_acc, dk_acc, dv_acc)):
            for h in range(heads):
                at = which * width + h * HD
                g = acc[rows, h * HD : (h + 1) * HD]
                if which < 2:
                    g = g * scale
                    first = g[:, :128]
                    first = low(first * cosine - turned(first) * sine)
                    rest = low(g[:, 128:])
                    dqkv_ref[rows, at : at + 128] = first
                    dqkv_ref[rows, at + 128 : at + HD] = rest
                    sums_ref[:, at : at + 128] += jnp.sum(first.astype(jnp.float32), axis=0, keepdims=True)
                    sums_ref[:, at + 128 : at + HD] += jnp.sum(rest.astype(jnp.float32), axis=0, keepdims=True)
                else:
                    g = low(g)
                    dqkv_ref[rows, at : at + HD] = g
                    sums_ref[:, at : at + HD] += jnp.sum(g.astype(jnp.float32), axis=0, keepdims=True)
        return carry

    lax.fori_loop(0, blocks, finish, 0)


def attend_back(q, k, v, o, do, lse, cosine, sine, heads, block=512):
    length, width = q.shape
    block = min(block, length)
    vm = pl.BlockSpec(memory_space=pltpu.VMEM)
    f32 = jnp.float32
    return pl.pallas_call(
        functools.partial(attend_back_kernel, heads, block),
        in_specs=[vm] * 8,
        out_specs=[vm, vm],
        out_shape=[
            jax.ShapeDtypeStruct((length, 3 * width), jnp.bfloat16),
            jax.ShapeDtypeStruct((1, 3 * width), f32),
        ],
        scratch_shapes=[
            pltpu.VMEM((length, width), f32), pltpu.VMEM((length, width), f32),
            pltpu.VMEM((length, width), f32), pltpu.VMEM((heads, length), f32),
        ],
        compiler_params=pltpu.CompilerParams(vmem_limit_bytes=VMEM_LIMIT),
        cost_estimate=pl.CostEstimate(
            flops=5 * length * length * width, bytes_accessed=20 * length * width,
            transcendentals=length * length * heads // 2),
        name="attend_back",
    )(q, k, v, o, do, lse, cosine, sine)


def out_kernel(h_ref, a_ref, wd_ref, w2_ref, o_ref):
    step = 512
    for at in range(0, o_ref.shape[1], step):
        o_ref[:, at : at + step] = low(
            dot_nn(h_ref[...], wd_ref[:, at : at + step])
            + dot_nn(a_ref[...], w2_ref[:, at : at + step]))


def out_proj(h, a, wd, w2, rows=512):
    length = h.shape[0]
    width = wd.shape[1]
    whole = lambda w: pl.BlockSpec(w.shape, lambda i: (0, 0), pipeline_mode=pl.Buffered(1))
    row = lambda n: pl.BlockSpec((rows, n), lambda i: (i, 0))
    return pl.pallas_call(
        out_kernel,
        grid=(length // rows,),
        in_specs=[row(h.shape[1]), row(a.shape[1]), whole(wd), whole(w2)],
        out_specs=row(width),
        out_shape=jax.ShapeDtypeStruct((length, width), jnp.bfloat16),
        compiler_params=pltpu.CompilerParams(vmem_limit_bytes=VMEM_LIMIT),
        cost_estimate=pl.CostEstimate(
            flops=2 * length * width * (h.shape[1] + a.shape[1]), bytes_accessed=30_000_000,
            transcendentals=0),
        name="out_proj",
    )(h, a, wd, w2)


def back_in_kernel(c_ref, slope_ref, wd_ref, w2_ref, dh_ref, dfc_ref, sums_ref):
    @pl.when(pl.program_id(0) == 0)
    def _():
        sums_ref[...] = jnp.zeros_like(sums_ref)

    dh_ref[...] = low(dot_nt(c_ref[...], wd_ref[...]))
    step = 512
    for at in range(0, dfc_ref.shape[1], step):
        d = low(dot_nt(c_ref[...], w2_ref[at : at + step, :])
                * slope_ref[:, at : at + step].astype(jnp.float32))
        dfc_ref[:, at : at + step] = d
        sums_ref[:, at : at + step] += jnp.sum(d.astype(jnp.float32), axis=0, keepdims=True)


def back_in(cot, slope, wd, w2, rows=512):
    length, width = cot.shape
    qw, ff = wd.shape[0], w2.shape[0]
    whole = lambda w: pl.BlockSpec(w.shape, lambda i: (0, 0), pipeline_mode=pl.Buffered(1))
    row = lambda n: pl.BlockSpec((rows, n), lambda i: (i, 0))
    return pl.pallas_call(
        back_in_kernel,
        grid=(length // rows,),
        in_specs=[row(width), row(ff), whole(wd), whole(w2)],
        out_specs=[row(qw), row(ff), pl.BlockSpec((1, ff), lambda i: (0, 0))],
        out_shape=[
            jax.ShapeDtypeStruct((length, qw), jnp.bfloat16),
            jax.ShapeDtypeStruct((length, ff), jnp.bfloat16),
            jax.ShapeDtypeStruct((1, ff), jnp.float32),
        ],
        compiler_params=pltpu.CompilerParams(vmem_limit_bytes=VMEM_LIMIT),
        cost_estimate=pl.CostEstimate(
            flops=2 * length * width * (qw + ff), bytes_accessed=40_000_000, transcendentals=0),
        name="back_in",
    )(cot, slope, wd, w2)


def back_out_kernel(dqkv_ref, dfc_ref, x_ref, stat_ref, gains_ref, wq_ref, w1_ref, e_ref, sums_ref):
    @pl.when(pl.program_id(0) == 0)
    def _():
        sums_ref[...] = jnp.zeros_like(sums_ref)

    mean, rstd = stat_ref[:, 0:1], stat_ref[:, 1:2]
    step = 512
    for at in range(0, e_ref.shape[1], step):
        cols = slice(at, at + step)
        d1 = dot_nt(dqkv_ref[...], wq_ref[cols, :])
        d2 = dot_nt(dfc_ref[...], w1_ref[cols, :])
        xhat = (x_ref[:, cols].astype(jnp.float32) - mean) * rstd
        e_ref[:, cols] = low(d1 * gains_ref[0:1, cols] + d2 * gains_ref[2:3, cols])
        sums_ref[0:1, cols] += jnp.sum(d1 * xhat, axis=0, keepdims=True)
        sums_ref[1:2, cols] += jnp.sum(d1, axis=0, keepdims=True)
        sums_ref[2:3, cols] += jnp.sum(d2 * xhat, axis=0, keepdims=True)
        sums_ref[3:4, cols] += jnp.sum(d2, axis=0, keepdims=True)


def back_out(dqkv, dfc, x, stat, gains, wq, w1, rows=512):
    length, width = x.shape
    whole = lambda w: pl.BlockSpec(w.shape, lambda i: (0, 0), pipeline_mode=pl.Buffered(1))
    row = lambda n: pl.BlockSpec((rows, n), lambda i: (i, 0))
    return pl.pallas_call(
        back_out_kernel,
        grid=(length // rows,),
        in_specs=[row(dqkv.shape[1]), row(dfc.shape[1]), row(width), row(128), whole(gains), whole(wq), whole(w1)],
        out_specs=[row(width), pl.BlockSpec((4, width), lambda i: (0, 0))],
        out_shape=[
            jax.ShapeDtypeStruct((length, width), jnp.bfloat16),
            jax.ShapeDtypeStruct((4, width), jnp.float32),
        ],
        compiler_params=pltpu.CompilerParams(vmem_limit_bytes=VMEM_LIMIT),
        cost_estimate=pl.CostEstimate(
            flops=2 * length * width * (dqkv.shape[1] + dfc.shape[1]), bytes_accessed=50_000_000,
            transcendentals=0),
        name="back_out",
    )(dqkv, dfc, x, stat, gains, wq, w1)


def weight_grad_kernel(split, a_ref, b_ref, o_ref):
    if split == 1:
        o_ref[...] = low(dot_tn(a_ref[...], b_ref[...]))
        return
    cols = o_ref.shape[2]
    for shard in range(split):
        o_ref[shard] = low(dot_tn(a_ref[...], b_ref[:, shard * cols : (shard + 1) * cols]))


def weight_grad(a, b, split=1, tile_m=512):
    length, m = a.shape
    n = b.shape[1]
    tile_m = min(tile_m, m)
    if split == 1:
        out_spec = pl.BlockSpec((tile_m, n), lambda i: (i, 0))
        out_shape = jax.ShapeDtypeStruct((m, n), jnp.bfloat16)
    else:
        out_spec = pl.BlockSpec((split, tile_m, n // split), lambda i: (0, i, 0))
        out_shape = jax.ShapeDtypeStruct((split, m, n // split), jnp.bfloat16)
    return pl.pallas_call(
        functools.partial(weight_grad_kernel, split),
        grid=(m // tile_m,),
        in_specs=[
            pl.BlockSpec((length, tile_m), lambda i: (0, i)),
            pl.BlockSpec((length, n), lambda i: (0, 0), pipeline_mode=pl.Buffered(1)),
        ],
        out_specs=out_spec,
        out_shape=out_shape,
        compiler_params=pltpu.CompilerParams(vmem_limit_bytes=VMEM_LIMIT),
        cost_estimate=pl.CostEstimate(
            flops=2 * length * m * n, bytes_accessed=2 * (length * (m + n) + m * n), transcendentals=0),
        name="weight_grad",
    )(a, b)


def ring_place(chip, chips):
    half = chips // 2
    return jnp.where(chip < half, chip, 3 * half - 1 - chip)


def shard_view(ref, kind, owner, part, extent):
    if kind == "row":
        rows = extent[0]
        if part == 0:
            return ref.at[pl.ds(owner * rows, rows)]
        half = rows // 2
        return ref.at[pl.ds(owner * rows + (part - 1) * half, half)]
    rows, cols = extent
    if part == 0:
        return ref.at[:, pl.ds(owner * cols, cols)]
    half = rows // 2
    return ref.at[pl.ds((part - 1) * half, half), pl.ds(owner * cols, cols)]


def own_view(ref, part, extent):
    if part == 0:
        return ref
    half = extent[0] // 2
    return ref.at[pl.ds((part - 1) * half, half)]


def gather_kernel(kinds, extents, pieces, chips, line, *refs):
    count = len(kinds)
    shards = refs[:count]
    rows_in = refs[count : count + pieces]
    fulls = refs[count + pieces : 2 * count + pieces]
    rows_all = refs[2 * count + pieces : 2 * count + 2 * pieces]
    ring_send, ring_recv, pair_send, pair_recv, line_send, line_recv, local = refs[
        2 * count + 2 * pieces :
    ]
    dp = lax.axis_index("dp")
    tp = lax.axis_index("tp")
    core = lax.rem(dp, 2)
    place = ring_place(lax.div(dp, 2), chips)
    hops = chips // 2

    def device(ring_pos):
        pos = lax.rem(ring_pos + chips, chips)
        return ring_place(pos, chips) * 2 + core

    right, left = device(place + 1), device(place - 1)
    sibling = dp + 1 - 2 * core
    barrier = pltpu.get_barrier_semaphore()
    for partner in (right, left, sibling):
        pl.semaphore_signal(barrier, 1, device_id={"dp": partner}, device_id_type=MESH)
    peers = 3
    if pieces:
        @pl.when(tp > 0)
        def _():
            pl.semaphore_signal(barrier, 1, device_id={"tp": tp - 1}, device_id_type=MESH)

        @pl.when(tp < line - 1)
        def _():
            pl.semaphore_signal(barrier, 1, device_id={"tp": tp + 1}, device_id_type=MESH)

        peers = peers + jnp.where(tp > 0, 1, 0) + jnp.where(tp < line - 1, 1, 0)
    pl.semaphore_wait(barrier, peers)

    def ring_copy(a, way, hop):
        owner = device(place - hop) if way == 0 else device(place + hop)
        part = 0 if hop < hops - 1 else 1 + way
        if hop == 0:
            src = own_view(shards[a], part, extents[a])
        else:
            src = shard_view(fulls[a], kinds[a], owner, part, extents[a])
        return pltpu.make_async_remote_copy(
            src_ref=src,
            dst_ref=shard_view(fulls[a], kinds[a], owner, part, extents[a]),
            send_sem=ring_send.at[a, way, hop],
            recv_sem=ring_recv.at[a, way, hop],
            device_id={"dp": right if way == 0 else left},
            device_id_type=MESH,
        )

    def ring_arrival(a, way, hop):
        owner = device(place - 1 - hop) if way == 0 else device(place + 1 + hop)
        part = 0 if hop < hops - 1 else 1 + way
        view = shard_view(fulls[a], kinds[a], owner, part, extents[a])
        return pltpu.make_async_remote_copy(
            src_ref=view,
            dst_ref=view,
            send_sem=ring_send.at[a, way, hop],
            recv_sem=ring_recv.at[a, way, hop],
            device_id={"dp": right if way == 0 else left},
            device_id_type=MESH,
        )

    def pair_copy(a, slot, owner_here, owner_there, part, arriving):
        owner = owner_there if arriving else owner_here
        view = shard_view(fulls[a], kinds[a], owner, part, extents[a])
        src = own_view(shards[a], part, extents[a]) if slot == 0 and not arriving else view
        return pltpu.make_async_remote_copy(
            src_ref=src,
            dst_ref=view,
            send_sem=pair_send.at[a, slot],
            recv_sem=pair_recv.at[a, slot],
            device_id={"dp": sibling},
            device_id_type=MESH,
        )

    def other(owner):
        return owner + 1 - 2 * core

    def line_copy(b, way, hop):
        length = rows_in[b].shape[0]
        piece = tp - hop if way == 0 else tp + hop
        view = rows_all[b].at[pl.ds(piece * length, length)]
        return pltpu.make_async_remote_copy(
            src_ref=rows_in[b] if hop == 0 else view,
            dst_ref=view,
            send_sem=line_send.at[b, way, hop],
            recv_sem=line_recv.at[b, way, hop],
            device_id={"tp": tp + 1 if way == 0 else tp - 1},
            device_id_type=MESH,
        )

    def line_arrival(b, way, hop):
        length = rows_in[b].shape[0]
        piece = tp - 1 - hop if way == 0 else tp + 1 + hop
        view = rows_all[b].at[pl.ds(piece * length, length)]
        return pltpu.make_async_remote_copy(
            src_ref=view,
            dst_ref=view,
            send_sem=line_send.at[b, way, hop],
            recv_sem=line_recv.at[b, way, hop],
            device_id={"tp": tp - 1 if way == 0 else tp + 1},
            device_id_type=MESH,
        )

    def sends(way, hop):
        if way == 0:
            return (tp < line - 1) & (tp - hop >= 0)
        return (tp > 0) & (tp + hop <= line - 1)

    def arrives(way, hop):
        if way == 0:
            return tp - 1 - hop >= 0
        return tp + 1 + hop <= line - 1

    def start_line(hop):
        for b in range(pieces):
            for way in range(2):
                @pl.when(sends(way, hop))
                def _():
                    line_copy(b, way, hop).start()

    def step_line(hop):
        for b in range(pieces):
            for way in range(2):
                @pl.when(arrives(way, hop))
                def _():
                    line_arrival(b, way, hop).wait_recv()

                if hop + 1 < line - 1:
                    @pl.when(sends(way, hop + 1))
                    def _():
                        line_copy(b, way, hop + 1).start()

    start_line(0)
    for a in range(count):
        for way in range(2):
            ring_copy(a, way, 0).start()
        pair_copy(a, 0, dp, sibling, 0, False).start()
    locals_ = []
    for a in range(count):
        locals_.append(
            pltpu.make_async_copy(
                shards[a], shard_view(fulls[a], kinds[a], dp, 0, extents[a]), local.at[a]
            )
        )
    for b in range(pieces):
        length = rows_in[b].shape[0]
        locals_.append(
            pltpu.make_async_copy(
                rows_in[b], rows_all[b].at[pl.ds(tp * length, length)], local.at[count + b]
            )
        )
    for copy in locals_:
        copy.start()
    line_hop = 0
    for hop in range(hops):
        for a in range(count):
            for way in range(2):
                ring_arrival(a, way, hop).wait_recv()
                if hop + 1 < hops:
                    ring_copy(a, way, hop + 1).start()
                owner = device(place - 1 - hop) if way == 0 else device(place + 1 + hop)
                part = 0 if hop < hops - 1 else 1 + way
                pair_copy(a, 1 + 2 * hop + way, owner, other(owner), part, False).start()
            if a == count // 2 and line_hop < line - 1:
                step_line(line_hop)
                line_hop += 1
    for hop in range(line_hop, line - 1):
        step_line(hop)
    for a in range(count):
        own = pair_copy(a, 0, dp, sibling, 0, False)
        own.wait_send()
        pair_copy(a, 0, dp, sibling, 0, True).wait_recv()
        for hop in range(hops):
            for way in range(2):
                owner = device(place - 1 - hop) if way == 0 else device(place + 1 + hop)
                part = 0 if hop < hops - 1 else 1 + way
                slot = 1 + 2 * hop + way
                pair_copy(a, slot, owner, other(owner), part, False).wait_send()
                pair_copy(a, slot, owner, other(owner), part, True).wait_recv()
                ring_copy(a, way, hop).wait_send()
    for b in range(pieces):
        for hop in range(line - 1):
            for way in range(2):
                @pl.when(sends(way, hop))
                def _():
                    line_copy(b, way, hop).wait_send()
    for copy in locals_:
        copy.wait()


def gather_all(shards, kinds, rows, dp_count, tp_count, collective_id):
    extents = [shard.shape for shard in shards]
    full_shapes = []
    for kind, extent in zip(kinds, extents):
        if kind == "row":
            full_shapes.append((extent[0] * dp_count,) + tuple(extent[1:]))
        else:
            full_shapes.append((extent[0], extent[1] * dp_count))
    chips = dp_count // 2
    hops = chips // 2
    count, pieces = len(shards), len(rows)
    out_shape = [jax.ShapeDtypeStruct(shape, s.dtype) for shape, s in zip(full_shapes, shards)]
    out_shape += [
        jax.ShapeDtypeStruct((r.shape[0] * tp_count, r.shape[1]), r.dtype) for r in rows
    ]
    dma = pltpu.SemaphoreType.DMA
    return pl.pallas_call(
        functools.partial(gather_kernel, kinds, extents, pieces, chips, tp_count),
        out_shape=out_shape,
        in_specs=[pl.BlockSpec(memory_space=pl.ANY)] * (count + pieces),
        out_specs=[pl.BlockSpec(memory_space=pl.ANY)] * (count + pieces),
        scratch_shapes=[
            dma((max(count, 1), 2, hops)),
            dma((max(count, 1), 2, hops)),
            dma((max(count, 1), 1 + 2 * hops)),
            dma((max(count, 1), 1 + 2 * hops)),
            dma((max(pieces, 1), 2, max(tp_count - 1, 1))),
            dma((max(pieces, 1), 2, max(tp_count - 1, 1))),
            dma((count + pieces,)),
        ],
        compiler_params=pltpu.CompilerParams(
            collective_id=collective_id, has_side_effects=True
        ),
        name="gather_all",
    )(*shards, *rows)


def scatter_kernel(count, chips, line, *refs):
    hops = chips // 2
    refs = list(refs)

    def take(n):
        out, refs[:n] = refs[:n], []
        return out

    grads = take(count - 1)
    line_ref, flat_ref = take(2)
    outs = take(count)
    held = take(count)
    paired = take(count)
    landed = take(count)
    small, line_land = take(2)
    pair_send, pair_recv, load_sem, ring_send, ring_recv, line_send, line_recv = refs
    dp = lax.axis_index("dp")
    tp = lax.axis_index("tp")
    core = lax.rem(dp, 2)
    place = ring_place(lax.div(dp, 2), chips)

    def chip_at(ring_pos):
        return ring_place(lax.rem(ring_pos + chips, chips), chips)

    right, left = chip_at(place + 1) * 2 + core, chip_at(place - 1) * 2 + core
    sibling = dp + 1 - 2 * core
    barrier = pltpu.get_barrier_semaphore()
    for partner in (right, left, sibling):
        pl.semaphore_signal(barrier, 1, device_id={"dp": partner}, device_id_type=MESH)
    for n in range(1, line):
        pl.semaphore_signal(
            barrier, 1, device_id={"tp": lax.rem(tp + n, line)}, device_id_type=MESH)
    pl.semaphore_wait(barrier, 3 + line - 1)

    def line_copy(n):
        return pltpu.make_async_remote_copy(
            src_ref=line_ref, dst_ref=line_land.at[n - 1],
            send_sem=line_send.at[n - 1], recv_sem=line_recv.at[n - 1],
            device_id={"tp": lax.rem(tp + n, line)}, device_id_type=MESH)

    for n in range(1, line):
        line_copy(n).start()

    offsets = [hops]
    for near in range(hops - 1, 0, -1):
        offsets += [near, -near]
    offsets.append(0)

    def source(a):
        return small if a == count - 1 else grads[a]

    def pair_copy(a, slot):
        chip = chip_at(place + offsets[slot])
        return pltpu.make_async_remote_copy(
            src_ref=source(a).at[chip * 2 + 1 - core], dst_ref=paired[a].at[slot],
            send_sem=pair_send.at[a, slot], recv_sem=pair_recv.at[a, slot],
            device_id={"dp": sibling}, device_id_type=MESH)

    def load(a, slot):
        chip = chip_at(place + offsets[slot])
        return pltpu.make_async_copy(
            source(a).at[chip * 2 + core], held[a].at[slot], load_sem.at[a, slot])

    big = range(count - 1)
    for slot in range(chips):
        for a in big:
            load(a, slot).start()
            pair_copy(a, slot).start()
    for n in range(1, line):
        line_copy(n).wait_recv()
    total = line_ref[...]
    for n in range(1, line):
        total = total + line_land[n - 1]
    rows_z = line_ref.shape[1]
    small[:, :rows_z] = total
    small[:, rows_z:] = flat_ref[...]
    last = count - 1
    for slot in range(chips):
        load(last, slot).start()
        pair_copy(last, slot).start()

    def tiles(a, rows, body):
        cols = held[a].shape[2]
        step = min(rows, max(16, 1 << ((32768 // cols).bit_length() - 1)))

        def run(t, carry):
            body(pl.ds(pl.multiple_of(t * step, step), step))
            return carry

        lax.fori_loop(0, rows // step, run, 0)

    def f32(value):
        return value.astype(jnp.float32)

    def pair_sum(a, slot):
        load(a, slot).wait()
        pair_copy(a, slot).wait_recv()

        def body(at):
            held[a][slot, at] = (f32(held[a][slot, at]) + f32(paired[a][slot, at])).astype(
                held[a].dtype)

        tiles(a, held[a].shape[1], body)

    def part_of(a, way, step):
        rows = held[a].shape[1]
        if step == 0:
            return way * (rows // 2), rows // 2
        return 0, rows

    def ring_copy(a, way, step):
        slot = offsets.index((hops - step) * (1 if way == 0 or step == 0 else -1))
        first, rows = part_of(a, way, step)
        return pltpu.make_async_remote_copy(
            src_ref=held[a].at[slot, pl.ds(first, rows)],
            dst_ref=landed[a].at[way, step, pl.ds(first, rows)],
            send_sem=ring_send.at[a, way, step], recv_sem=ring_recv.at[a, way, step],
            device_id={"dp": right if way == 0 else left}, device_id_type=MESH)

    def add_landed(a, way, step, slot):
        first, rows = part_of(a, way, step)
        ring_copy(a, way, step).wait_recv()

        def body(at):
            at = pl.ds(pl.multiple_of(at.start + first, 16), at.size)
            held[a][slot, at] = (f32(held[a][slot, at]) + f32(landed[a][way, step, at])).astype(
                held[a].dtype)

        tiles(a, rows, body)

    for a in range(count):
        pair_sum(a, 0)
        for way in range(2):
            ring_copy(a, way, 0).start()
    for step in range(1, hops):
        for a in range(count):
            for way in range(2):
                slot = offsets.index((hops - step) * (1 if way == 0 else -1))
                pair_sum(a, slot)
                add_landed(a, way, step - 1, slot)
                ring_copy(a, way, step).start()
    own = chips - 1
    for a in range(count):
        pair_sum(a, own)
        for way in range(2):
            ring_copy(a, way, hops - 1).wait_recv()

        def body(at):
            outs[a][at] = (
                f32(held[a][own, at]) + f32(landed[a][0, hops - 1, at]) + f32(landed[a][1, hops - 1, at]))

        tiles(a, held[a].shape[1], body)
    for a in range(count):
        for slot in range(chips):
            pair_copy(a, slot).wait_send()
        for way in range(2):
            for step in range(hops):
                ring_copy(a, way, step).wait_send()
    for n in range(1, line):
        line_copy(n).wait_send()


def scatter_grads(grads, line_sums, flat_sums, dp_count, tp_count, collective_id):
    chips = dp_count // 2
    hops = chips // 2
    count = len(grads) + 1
    rows_z, rows_d = line_sums.shape[1], flat_sums.shape[1]
    shapes = [g.shape[1:] for g in grads] + [(rows_z + rows_d, line_sums.shape[2])]
    dtypes = [g.dtype for g in grads] + [jnp.float32]
    dma = pltpu.SemaphoreType.DMA
    vm = pl.BlockSpec(memory_space=pltpu.VMEM)
    per = lambda lead: [pltpu.VMEM(lead + tuple(s), t) for s, t in zip(shapes, dtypes)]
    return pl.pallas_call(
        functools.partial(scatter_kernel, count, chips, tp_count),
        out_shape=[jax.ShapeDtypeStruct(s, jnp.float32) for s in shapes],
        in_specs=[pl.BlockSpec(memory_space=pl.ANY)] * len(grads) + [vm, vm],
        out_specs=[vm] * count,
        scratch_shapes=per((chips,)) + per((chips,)) + per((2, hops)) + [
            pltpu.VMEM((dp_count, rows_z + rows_d, line_sums.shape[2]), jnp.float32),
            pltpu.VMEM((max(tp_count - 1, 1),) + line_sums.shape, jnp.float32),
            dma((count, chips)), dma((count, chips)), dma((count, chips)),
            dma((count, 2, hops)), dma((count, 2, hops)),
            dma((max(tp_count - 1, 1),)), dma((max(tp_count - 1, 1),)),
        ],
        compiler_params=pltpu.CompilerParams(
            collective_id=collective_id, has_side_effects=True,
            vmem_limit_bytes=60 * 1024 * 1024),
        name="scatter_grads",
    )(*grads, line_sums, flat_sums)


def pack_small(parts):
    flat = jnp.concatenate([part.reshape(-1) for part in parts])
    rows = -(-flat.size // 4096) * 32
    return jnp.pad(flat, (0, rows * 128 - flat.size)).reshape(rows, 128)


def unpack_small(full, parts, dp_count):
    full = full.reshape(dp_count, -1).astype(jnp.float32)
    out, start = [], 0
    for part in parts:
        out.append(full[:, start : start + part.size])
        start += part.size
    return out


def by_owner(rows, dp_count):
    count = -(-rows.shape[1] // 2048) * 16
    padded = jnp.pad(rows, ((0, 0), (0, count * 128 - rows.shape[1])))
    return padded.reshape(dp_count, count, 128)


def body(
    hidden_in,
    triple_projection_weight,
    triple_projection_bias,
    attention_out_weight,
    b_dense,
    feedforward_in_weight,
    feedforward_in_bias,
    feedforward_out_weight,
    b_fc2,
    ln1_gain,
    ln1_bias,
    ln2_gain,
    ln2_bias,
    grad_out,
):
    _, piece_len, width = hidden_in.shape
    tp_count = lax.axis_size("tp")
    dp_count = lax.axis_size("dp")
    length = piece_len * tp_count
    heads = triple_projection_weight.shape[2] // HD
    cosine, sine = rotary_tables(length)
    small = [
        triple_projection_bias,
        feedforward_in_bias,
        b_dense,
        b_fc2,
        ln1_gain,
        ln1_bias,
        ln2_gain,
        ln2_bias,
    ]
    small_all, full_qkv, full_fc1, full_dense, full_fc2, x_seq = gather_all(
        [
            pack_small(small),
            triple_projection_weight.reshape(width // dp_count, -1),
            feedforward_in_weight,
            attention_out_weight,
            feedforward_out_weight,
        ],
        ["row", "row", "row", "col", "col"],
        [hidden_in[0]],
        dp_count,
        tp_count,
        0,
    )
    grad_own, x_seq = lax.optimization_barrier((grad_out, x_seq))
    cot_seq = lax.all_gather(grad_own, "tp", axis=1, tiled=True)[0]
    vectors = unpack_small(small_all, small, dp_count)
    bqkv = vectors[0].T.reshape(1, -1)
    bfc1 = vectors[1].T.reshape(1, -1)
    full_bdense, full_bfc2 = vectors[2].reshape(-1), vectors[3].reshape(-1)
    gains = jnp.stack([part.reshape(-1) for part in vectors[4:]])

    norm_one, norm_two, query, key, value, act, slope, stat = front(
        x_seq, gains, full_qkv, bqkv, full_fc1, bfc1, cosine, sine, heads
    )
    head_out, lse = attend(query, key, value, heads)
    partial_value = out_proj(head_out, act, full_dense, full_fc2)
    summed = lax.psum_scatter(partial_value, "tp", scatter_dimension=0, tiled=True)
    layer_out = (
        hidden_in[0].astype(jnp.float32) + summed.astype(jnp.float32) + full_bdense + full_bfc2
    )
    hidden_out = low(layer_out)[None]

    d_heads, d_fc, sum_bfc1 = back_in(cot_seq, slope, full_dense, full_fc2)
    d_qkv, sum_bqkv = attend_back(query, key, value, head_out, d_heads, lse, cosine, sine, heads)
    e_sum, ln_sums = back_out(d_qkv, d_fc, x_seq, stat, gains, full_qkv, full_fc1)
    e_piece = lax.psum_scatter(e_sum, "tp", scatter_dimension=0, tiled=True).astype(jnp.float32)

    grad_fc2 = weight_grad(act, cot_seq, dp_count)
    grad_dense = weight_grad(head_out, cot_seq, dp_count)
    grad_fc1 = weight_grad(norm_two, d_fc).reshape(dp_count, -1, d_fc.shape[1])
    grad_qkv = weight_grad(norm_one, d_qkv).reshape(dp_count, -1, d_qkv.shape[1])

    cot_piece = grad_out[0].astype(jnp.float32)
    sum_out = jnp.sum(cot_piece, axis=0, keepdims=True)
    line_sums = jnp.concatenate([ln_sums, sum_out], axis=0)
    line_sums = line_sums.reshape(5, dp_count, -1).transpose(1, 0, 2).reshape(dp_count, -1)
    flat_sums = jnp.concatenate([sum_bqkv, sum_bfc1], axis=1).reshape(-1, dp_count).T
    line_rows, flat_rows = by_owner(line_sums, dp_count), by_owner(flat_sums, dp_count)
    own_fc2, own_dense, own_fc1, own_qkv, own_small = scatter_grads(
        [grad_fc2, grad_dense, grad_fc1, grad_qkv], line_rows, flat_rows, dp_count, tp_count, 1
    )
    own_line = own_small[: line_rows.shape[1]].reshape(-1)[: line_sums.shape[1]].reshape(5, -1)
    own_flat = own_small[line_rows.shape[1] :].reshape(-1)[: flat_sums.shape[1]]
    split = sum_bqkv.size // dp_count

    x_own = hidden_in[0].astype(jnp.float32)
    mean = jnp.mean(x_own, axis=-1, keepdims=True)
    centered = x_own - mean
    rstd = lax.rsqrt(jnp.mean(centered * centered, axis=-1, keepdims=True) + EPSILON)
    xhat = centered * rstd
    back = (
        e_piece
        - jnp.mean(e_piece, axis=-1, keepdims=True)
        - xhat * jnp.mean(e_piece * xhat, axis=-1, keepdims=True)
    ) * rstd
    grad_in = (cot_piece + back)[None]
    return (
        hidden_out,
        grad_in,
        own_qkv.reshape(triple_projection_weight.shape),
        own_flat[:split].reshape(triple_projection_bias.shape),
        own_dense,
        own_line[4],
        own_fc1,
        own_flat[split:].reshape(feedforward_in_bias.shape),
        own_fc2,
        own_line[4],
        own_line[0],
        own_line[1],
        own_line[2],
        own_line[3],
    )


def solution(mesh):
    return jax.shard_map(
        body,
        mesh=mesh,
        in_specs=(
            P("dp", "tp", None),
            P("dp", None, "tp"),
            P(None, "tp", "dp"),
            P("tp", "dp"),
            P("dp"),
            P("dp", "tp"),
            P("tp", "dp"),
            P("tp", "dp"),
            P("dp"),
            P("dp"),
            P("dp"),
            P("dp"),
            P("dp"),
            P("dp", "tp", None),
        ),
        out_specs=(
            P("dp", "tp", None),
            P("dp", "tp", None),
            P("dp", None, "tp"),
            P(None, "tp", "dp"),
            P("tp", "dp"),
            P("dp"),
            P("dp", "tp"),
            P("tp", "dp"),
            P("tp", "dp"),
            P("dp"),
            P("dp"),
            P("dp"),
            P("dp"),
            P("dp"),
        ),
        check_vma=False,
    )
```

```python
import functools
import math

import jax
import jax.numpy as jnp
import numpy as np
from jax import lax
from jax.experimental import pallas as pl
from jax.experimental.pallas import tpu as pltpu
from jax.sharding import PartitionSpec as P

MESH = pl.DeviceIdType.MESH
EPSILON = 1e-05
MASKED = -1e30
HD = 256
ROT = 64
VMEM_LIMIT = 60 * 1024 * 1024
LOG2E = 1.4426950408889634


def low(value):
    return value.astype(jnp.bfloat16)


def dot_nn(a, b):
    return lax.dot_general(a, b, (((1,), (0,)), ((), ())), preferred_element_type=jnp.float32)


def dot_nt(a, b):
    return lax.dot_general(a, b, (((1,), (1,)), ((), ())), preferred_element_type=jnp.float32)


def dot_tn(a, b):
    return lax.dot_general(a, b, (((0,), (0,)), ((), ())), preferred_element_type=jnp.float32)


def rotary_tables(length):
    half = ROT // 2
    exponent = np.arange(half, dtype=np.float32) * np.float32(2.0 / ROT)
    inverse = np.exp(exponent * np.float32(-math.log(10000.0)), dtype=np.float32)
    angle = np.arange(length, dtype=np.float32)[:, None] * inverse[None, :]
    cosine = np.ones((length, 128), np.float32)
    sine = np.zeros((length, 128), np.float32)
    cosine[:, :half] = cosine[:, half:ROT] = np.cos(angle)
    sine[:, :half] = -np.sin(angle)
    sine[:, half:ROT] = np.sin(angle)
    return jnp.asarray(cosine), jnp.asarray(sine)


def turned(part):
    half = ROT // 2
    lane = lax.broadcasted_iota(jnp.int32, part.shape, 1)
    return jnp.where(
        lane < half, pltpu.roll(part, 128 - half, 1), pltpu.roll(part, half, 1)
    )


def ring_place(chip, chips):
    half = chips // 2
    return jnp.where(chip < half, chip, 3 * half - 1 - chip)


def shard_view(ref, kind, owner, part, extent):
    axis = 1 if kind == "mid" else 0
    rows = extent[axis]
    first, size = (0, rows) if part == 0 else ((part - 1) * (rows // 2), rows // 2)
    if kind == "row":
        return ref.at[pl.ds(owner * rows + first, size)]
    if kind == "mid":
        return ref.at[:, pl.ds(owner * rows + first, size)]
    return ref.at[pl.ds(first, size), pl.ds(owner * extent[1], extent[1])]


def own_view(ref, kind, part, extent):
    if part == 0:
        return ref
    axis = 1 if kind == "mid" else 0
    half = extent[axis] // 2
    at = pl.ds((part - 1) * half, half)
    return ref.at[:, at] if kind == "mid" else ref.at[at]


def picked(tp, values):
    out = values[0]
    for i in range(1, len(values)):
        out = jnp.where(tp == i, values[i], out)
    return out


def order_of(line):
    return [sorted(range(line), key=lambda p: (abs(p - z), p)) for z in range(line)]


def head_kernel(cfg, *refs):
    chips, line, heads, n_q, n_b = cfg
    hops = chips // 2
    refs = list(refs)

    def take(n):
        out, refs[:n] = refs[:n], []
        return out

    shards = take(5)
    x_ref, cot_ref, cos_ref, sin_ref = take(4)
    (x_all, cot_all, n1_out, n2_out, q_out, k_out, v_out, act_out, slope_out,
     stat_out, head_out, lse_out, part_out, dh_out, dfc_out, land_out, acc_out, dqkv_out, e_out,
     hidden_out, vec_out, sfc_out, sq_out, ln_out) = take(24)
    fulls = take(5)
    small_ref, wq_ref, w1_ref, wd_ref, w2_ref = fulls
    kvec, bq_ref, b1_ref, k_buf, v_buf, sq_ref, ln_ref = take(7)
    (ring_send, ring_recv, pair_send, pair_recv, line_send, line_recv, local,
     sum_send, sum_recv, keep) = refs
    kinds = ["row", "mid", "row", "col", "col"]
    extents = [s.shape for s in shards]
    count = 5
    dp = lax.axis_index("dp")
    tp = lax.axis_index("tp")
    dp_count = 2 * chips
    core = lax.rem(dp, 2)
    place = ring_place(lax.div(dp, 2), chips)
    length = x_ref.shape[0]
    total_len = length * line
    width = x_ref.shape[1]

    def device(ring_pos):
        return ring_place(lax.rem(ring_pos + chips, chips), chips) * 2 + core

    right, left = device(place + 1), device(place - 1)
    sibling = dp + 1 - 2 * core
    barrier = pltpu.get_barrier_semaphore()
    for partner in (right, left, sibling):
        pl.semaphore_signal(barrier, 1, device_id={"dp": partner}, device_id_type=MESH)

    @pl.when(tp > 0)
    def _():
        pl.semaphore_signal(barrier, 1, device_id={"tp": tp - 1}, device_id_type=MESH)

    @pl.when(tp < line - 1)
    def _():
        pl.semaphore_signal(barrier, 1, device_id={"tp": tp + 1}, device_id_type=MESH)

    pl.semaphore_wait(barrier, 3 + jnp.where(tp > 0, 1, 0) + jnp.where(tp < line - 1, 1, 0))

    def ring_copy(a, way, hop, arriving=False):
        back = hop + 1 if arriving else hop
        owner = device(place - back) if way == 0 else device(place + back)
        part = 0 if hop < hops - 1 else 1 + way
        view = shard_view(fulls[a], kinds[a], owner, part, extents[a])
        own = hop == 0 and not arriving
        return pltpu.make_async_remote_copy(
            src_ref=own_view(shards[a], kinds[a], part, extents[a]) if own else view,
            dst_ref=view,
            send_sem=ring_send.at[a, way, hop],
            recv_sem=ring_recv.at[a, way, hop],
            device_id={"dp": right if way == 0 else left},
            device_id_type=MESH,
        )

    def pair_copy(a, slot, arriving=False):
        if slot == 0:
            owner, part = dp, 0
        else:
            hop, way = divmod(slot - 1, 2)
            owner = device(place - 1 - hop) if way == 0 else device(place + 1 + hop)
            part = 0 if hop < hops - 1 else 1 + way
        if arriving:
            owner = owner + 1 - 2 * core
        view = shard_view(fulls[a], kinds[a], owner, part, extents[a])
        return pltpu.make_async_remote_copy(
            src_ref=shards[a] if slot == 0 and not arriving else view,
            dst_ref=view,
            send_sem=pair_send.at[a, slot],
            recv_sem=pair_recv.at[a, slot],
            device_id={"dp": sibling},
            device_id_type=MESH,
        )

    def rows_of(piece):
        return pl.ds(pl.multiple_of(piece * length, length), length)

    def line_copy(b, way, hop, arriving=False):
        back = hop + 1 if arriving else hop
        piece = tp - back if way == 0 else tp + back
        view = (x_all, cot_all)[b].at[rows_of(piece)]
        to = tp + 1 if way == 0 else tp - 1
        if arriving:
            to = tp - 1 if way == 0 else tp + 1
        return pltpu.make_async_remote_copy(
            src_ref=(x_ref, cot_ref)[b] if hop == 0 and not arriving else view,
            dst_ref=view,
            send_sem=line_send.at[b, way, hop],
            recv_sem=line_recv.at[b, way, hop],
            device_id={"tp": to},
            device_id_type=MESH,
        )

    def sends(way, hop):
        return (tp < line - 1) & (tp >= hop) if way == 0 else (tp > 0) & (tp + hop < line)

    def arrives(way, hop):
        return tp - 1 - hop >= 0 if way == 0 else tp + 1 + hop < line

    def start_line(b, hop):
        for way in range(2):
            @pl.when(sends(way, hop))
            def _():
                line_copy(b, way, hop).start()

    def step_line(b, hop):
        for way in range(2):
            @pl.when(arrives(way, hop))
            def _():
                line_copy(b, way, hop, True).wait_recv()

            if hop + 1 < line - 1:
                @pl.when(sends(way, hop + 1))
                def _():
                    line_copy(b, way, hop + 1).start()

    start_line(0, 0)
    for a in range(count):
        for way in range(2):
            ring_copy(a, way, 0).start()
        pair_copy(a, 0).start()
    locals_ = [
        pltpu.make_async_copy(
            shards[a], shard_view(fulls[a], kinds[a], dp, 0, extents[a]), local.at[a])
        for a in range(count)
    ]
    locals_.append(pltpu.make_async_copy(x_ref, x_all.at[rows_of(tp)], local.at[count]))
    locals_.append(pltpu.make_async_copy(cot_ref, cot_all.at[rows_of(tp)], local.at[count + 1]))
    for copy in locals_:
        copy.start()
    line_hop = 0
    for hop in range(hops):
        for a in range(count):
            for way in range(2):
                ring_copy(a, way, hop, True).wait_recv()
                if hop + 1 < hops:
                    ring_copy(a, way, hop + 1).start()
                pair_copy(a, 1 + 2 * hop + way).start()
            if a == count // 2 and line_hop < line - 2:
                step_line(0, line_hop)
                line_hop += 1
    for a in range(count):
        locals_[a].wait()
        for slot in range(1 + 2 * hops):
            pair_copy(a, slot, True).wait_recv()

    small_rows = extents[0][0]
    per = width // dp_count // 128
    for d in range(dp_count):
        block = small_ref[d * small_rows : (d + 1) * small_rows].astype(jnp.float32)
        for vec in range(6):
            for r in range(per):
                at = (d * per + r) * 128
                row = vec * per + r
                kvec[vec : vec + 1, at : at + 128] = block[row : row + 1]
    span = 128 * dp_count
    lane = lax.broadcasted_iota(jnp.int32, (128, span), 0)
    col = lax.broadcasted_iota(jnp.int32, (128, span), 1)
    mixed = jnp.zeros((16, span), jnp.float32)
    for d in range(dp_count):
        hot = jnp.where(col == lane * dp_count + d, 1.0, 0.0).astype(jnp.bfloat16)
        mixed += dot_nn(small_ref[d * small_rows + 16 : d * small_rows + 32], hot)
    for ref, first, n in ((bq_ref, 0, n_q), (b1_ref, n_q, n_b)):
        for r in range(n):
            wide = min(span, ref.shape[1] - r * span)
            ref[0:1, r * span : r * span + wide] = mixed[first + r : first + r + 1, :wide]

    def front_body(x_blk, cos_blk, sin_blk, n1, n2, q, k, v, act, slope, stat):
        x = x_blk[...].astype(jnp.float32)
        mean = jnp.mean(x, axis=1, keepdims=True)
        centered = x - mean
        rstd = lax.rsqrt(jnp.mean(centered * centered, axis=1, keepdims=True) + EPSILON)
        xhat = centered * rstd
        n1[...] = low(xhat * kvec[2:3] + kvec[3:4])
        n2[...] = low(xhat * kvec[4:5] + kvec[5:6])
        lanes = lax.broadcasted_iota(jnp.int32, stat.shape, 1)
        stat[...] = jnp.where(lanes == 0, mean, rstd)
        cosine, sine = cos_blk[...], sin_blk[...]
        qw = heads * HD
        for which, out in enumerate((q, k, v)):
            for head in range(heads):
                cols = slice(head * HD, (head + 1) * HD)
                bias = slice(which * qw + head * HD, which * qw + (head + 1) * HD)
                raw = dot_nn(n1[...], wq_ref[which, :, cols]) + bq_ref[:, bias]
                if which < 2:
                    first = raw[:, :128]
                    first = first * cosine + turned(first) * sine
                    out[:, head * HD : head * HD + 128] = low(first)
                    out[:, head * HD + 128 : (head + 1) * HD] = low(raw[:, 128:])
                else:
                    out[:, cols] = low(raw)
        step = 256
        for at in range(0, w1_ref.shape[1], step):
            u = dot_nn(n2[...], w1_ref[:, at : at + step]) + b1_ref[:, at : at + step]
            cdf = 0.5 * (1.0 + lax.erf(u * (1.0 / math.sqrt(2.0))))
            pdf = jnp.exp(-0.5 * u * u) * (1.0 / math.sqrt(2.0 * math.pi))
            act[:, at : at + step] = low(u * cdf)
            slope[:, at : at + step] = low(cdf + u * pdf)

    block = min(256, length)
    wblock = min(512, length)

    def spec(n):
        return pl.BlockSpec((block, n), lambda i: (i, 0))

    qw, ff = heads * HD, w1_ref.shape[1]
    front_outs = (n1_out, n2_out, q_out, k_out, v_out, act_out, slope_out, stat_out)
    front_pipe = pltpu.emit_pipeline(
        front_body,
        grid=(length // block,),
        in_specs=[spec(width), spec(128), spec(128)],
        out_specs=[spec(ref.shape[1]) for ref in front_outs],
    )
    table = order_of(line)

    def piece_at(k):
        return picked(tp, [table[z][k] for z in range(line)])

    locals_[count].wait()
    for k in range(line):
        if k > 0:
            for hop in range(line_hop, k):
                step_line(0, hop)
                line_hop = hop + 1
        if k == line - 1:
            start_line(1, 0)
        at = rows_of(piece_at(k))
        front_pipe(
            x_all.at[at], cos_ref.at[at], sin_ref.at[at], *[ref.at[at] for ref in front_outs])

    kv_copies = [
        pltpu.make_async_copy(k_out, k_buf, local.at[0]),
        pltpu.make_async_copy(v_out, v_buf, local.at[1]),
    ]
    for copy in kv_copies:
        copy.start()
    for copy in kv_copies:
        copy.wait()
    qblock = min(512, total_len)
    scale = LOG2E * HD ** -0.5

    def attend_body(q_blk, o_blk, lse_blk):
        i = pl.program_id(0)
        qs = [q_blk[:, h * HD : (h + 1) * HD] for h in range(heads)]

        def one(h, j, state, diagonal):
            top, total, acc = state
            rows = pl.ds(pl.multiple_of(j * qblock, qblock), qblock)
            key = k_buf[rows, h * HD : (h + 1) * HD]
            value = v_buf[rows, h * HD : (h + 1) * HD]
            s = dot_nt(key, qs[h]) * scale
            if diagonal:
                kp = lax.broadcasted_iota(jnp.int32, s.shape, 0)
                qp = lax.broadcasted_iota(jnp.int32, s.shape, 1)
                s = jnp.where(kp <= qp, s, MASKED)
            new_top = jnp.maximum(top, jnp.max(s, axis=0, keepdims=True))
            p = jnp.exp2(s - new_top)
            shrink = jnp.exp2(top - new_top)
            total = total * shrink + jnp.sum(p, axis=0, keepdims=True)
            acc = acc * shrink + dot_tn(value, low(p))
            return new_top, total, acc

        def start():
            return (
                jnp.full((1, qblock), MASKED, jnp.float32),
                jnp.zeros((1, qblock), jnp.float32),
                jnp.zeros((HD, qblock), jnp.float32),
            )

        def step(j, states):
            return tuple(one(h, j, states[h], False) for h in range(heads))

        states = lax.fori_loop(0, i, step, tuple(start() for _ in range(heads)))
        states = [one(h, i, states[h], True) for h in range(heads)]
        for h in range(heads):
            top, total, acc = states[h]
            o_blk[:, h * HD : (h + 1) * HD] = low((acc / total).T)
            lse_blk[h : h + 1, :] = top + jnp.log2(total)

    pltpu.emit_pipeline(
        attend_body,
        grid=(total_len // qblock,),
        in_specs=[pl.BlockSpec((qblock, qw), lambda i: (i, 0))],
        out_specs=[
            pl.BlockSpec((qblock, qw), lambda i: (i, 0)),
            pl.BlockSpec((heads, qblock), lambda i: (0, i)),
        ],
    )(q_out, head_out, lse_out)
    step_line(1, 0)
    cot_hop = 1

    def out_body(h_blk, a_blk, o_blk):
        step = 512
        for at in range(0, o_blk.shape[1], step):
            o_blk[:, at : at + step] = low(
                dot_nn(h_blk[...], wd_ref[:, at : at + step])
                + dot_nn(a_blk[...], w2_ref[:, at : at + step]))

    out_pipe = pltpu.emit_pipeline(
        out_body, grid=(length // block,), in_specs=[spec(qw), spec(ff)], out_specs=[spec(width)])

    def sum_copy(way, step, from_acc):
        dist = line - step
        piece = tp + dist if way == 0 else tp - dist
        src = acc_out.at[way, step - 2] if from_acc else part_out.at[rows_of(piece)]
        return pltpu.make_async_remote_copy(
            src_ref=src,
            dst_ref=land_out.at[way, step - 1],
            send_sem=sum_send.at[way, step - 1],
            recv_sem=sum_recv.at[way, step - 1],
            device_id={"tp": tp + 1 if way == 0 else tp - 1},
            device_id_type=MESH,
        )

    def sum_sends(way, step):
        dist = line - step
        return tp + dist < line if way == 0 else tp - dist >= 0

    def sum_first(way):
        return tp == 0 if way == 0 else tp == line - 1

    def sum_arrival(way, step):
        view = land_out.at[way, step - 1]
        return pltpu.make_async_remote_copy(
            src_ref=view, dst_ref=view,
            send_sem=sum_send.at[way, step - 1], recv_sem=sum_recv.at[way, step - 1],
            device_id={"tp": tp - 1 if way == 0 else tp + 1}, device_id_type=MESH)

    def sum_arrives(way, step):
        dist = line - step
        if way == 0:
            return (tp >= 1) & (tp - 1 + dist < line)
        return (tp + 1 < line) & (tp + 1 - dist >= 0)

    def add_body(a_blk, b_blk, o_blk):
        o_blk[...] = low(a_blk[...].astype(jnp.float32) + b_blk[...].astype(jnp.float32))

    add_pipe = pltpu.emit_pipeline(
        add_body, grid=(length // block,), in_specs=[spec(width)] * 2, out_specs=[spec(width)])

    def start_sum(step):
        for way in range(2):
            dist = line - step
            piece = tp + dist if way == 0 else tp - dist

            @pl.when(sum_sends(way, step) & sum_first(way))
            def _():
                sum_copy(way, step, False).start()

            if step > 1:
                @pl.when(sum_arrives(way, step - 1))
                def _():
                    sum_arrival(way, step - 1).wait_recv()

                @pl.when(sum_sends(way, step) & jnp.logical_not(sum_first(way)))
                def _():
                    add_pipe(
                        part_out.at[rows_of(piece)], land_out.at[way, step - 2],
                        acc_out.at[way, step - 2])
                    sum_copy(way, step, True).start()

    for k in range(line - 1, -1, -1):
        at = rows_of(piece_at(k))
        out_pipe(head_out.at[at], act_out.at[at], part_out.at[at])
        if k == line - 1:
            start_sum(1)

    sfc_ref = b1_ref
    for row in range(1):
        sfc_ref[...] = jnp.zeros_like(sfc_ref)

    def back_body(c_blk, slope_blk, dh_blk, dfc_blk):
        dh_blk[...] = low(dot_nt(c_blk[...], wd_ref[...]))
        step = 512
        for at in range(0, ff, step):
            d = low(dot_nt(c_blk[...], w2_ref[at : at + step, :])
                    * slope_blk[:, at : at + step].astype(jnp.float32))
            dfc_blk[:, at : at + step] = d
            sfc_ref[0:1, at : at + step] += jnp.sum(d.astype(jnp.float32), axis=0, keepdims=True)

    back_pipe = pltpu.emit_pipeline(
        back_body, grid=(length // block,), in_specs=[spec(width), spec(ff)],
        out_specs=[spec(qw), spec(ff)])
    locals_[count + 1].wait()
    sum_step = 2
    ln_ref[...] = jnp.zeros_like(ln_ref)

    def cot_sum_body(c_blk):
        ln_ref[4:5] += jnp.sum(c_blk[...].astype(jnp.float32), axis=0, keepdims=True)

    pltpu.emit_pipeline(
        cot_sum_body, grid=(length // block,), in_specs=[spec(width)], out_specs=[])(cot_ref)
    for k in range(line):
        for hop in range(cot_hop, k):
            step_line(1, hop)
            cot_hop = hop + 1
        if k == line - 1:
            while sum_step < line - 1:
                start_sum(sum_step)
                sum_step += 1
            for hop in range(cot_hop, line - 1):
                step_line(1, hop)
        at = rows_of(piece_at(k))
        back_pipe(cot_all.at[at], slope_out.at[at], dh_out.at[at], dfc_out.at[at])
    def attend_back(q_buf, o_buf, do_buf, lse_buf, dq_acc, dk_acc, dv_acc, delta, loaded):
        copies = [
            pltpu.make_async_copy(q_out, q_buf, loaded.at[0]),
            pltpu.make_async_copy(head_out, o_buf, loaded.at[1]),
            pltpu.make_async_copy(dh_out, do_buf, loaded.at[2]),
            pltpu.make_async_copy(lse_out, lse_buf, loaded.at[3]),
        ]
        for copy in copies:
            copy.start()
        dq_acc[...] = jnp.zeros_like(dq_acc)
        for copy in copies:
            copy.wait()
        blocks = total_len // qblock
        scale = HD ** -0.5
        for i in range(blocks):
            rows = slice(i * qblock, (i + 1) * qblock)
            for h in range(heads):
                cols = slice(h * HD, (h + 1) * HD)
                inner = jnp.sum(
                    do_buf[rows, cols].astype(jnp.float32) * o_buf[rows, cols].astype(jnp.float32),
                    axis=1, keepdims=True)
                delta[h : h + 1, rows] = jnp.broadcast_to(inner, (qblock, 128)).T[0:1]

        def one(h, i, j, diagonal):
            cols = slice(h * HD, (h + 1) * HD)
            qrows = pl.ds(pl.multiple_of(i * qblock, qblock), qblock)
            krows = pl.ds(pl.multiple_of(j * qblock, qblock), qblock)
            query, grad = q_buf[qrows, cols], do_buf[qrows, cols]
            key, value = k_buf[krows, cols], v_buf[krows, cols]
            s = dot_nt(key, query) * (scale * LOG2E)
            p = jnp.exp2(s - lse_buf[h : h + 1, qrows])
            if diagonal:
                kp = lax.broadcasted_iota(jnp.int32, s.shape, 0)
                qp = lax.broadcasted_iota(jnp.int32, s.shape, 1)
                p = jnp.where(kp <= qp, p, 0.0)
            dp_blk = dot_nt(value, grad)
            ds = low(p * (dp_blk - delta[h : h + 1, qrows]))
            dv = dot_nn(low(p), grad)
            dk = dot_nn(ds, query)
            dq_acc[qrows, cols] += dot_tn(ds, key)
            if diagonal:
                dv_acc[krows, cols] = dv
                dk_acc[krows, cols] = dk
            else:
                dv_acc[krows, cols] += dv
                dk_acc[krows, cols] += dk

        def outer(j, carry):
            for h in range(heads):
                one(h, j, j, True)

            def inner(i, c):
                for h in range(heads):
                    one(h, i, j, False)
                return c

            lax.fori_loop(j + 1, blocks, inner, 0)
            return carry

        lax.fori_loop(0, blocks, outer, 0)
        sq_ref[...] = jnp.zeros_like(sq_ref)

        def finish_body(cos_blk, sin_blk, out_blk):
            rows = pl.ds(pl.multiple_of(pl.program_id(0) * block, block), block)
            cosine, sine = cos_blk[...], sin_blk[...]
            for which, acc in enumerate((dq_acc, dk_acc, dv_acc)):
                for h in range(heads):
                    at = which * qw + h * HD
                    g = acc[rows, h * HD : (h + 1) * HD]
                    if which < 2:
                        g = g * scale
                        first = g[:, :128]
                        first = first * cosine - turned(first) * sine
                        out_blk[:, at : at + 128] = low(first)
                        out_blk[:, at + 128 : at + HD] = low(g[:, 128:])
                    else:
                        out_blk[:, at : at + HD] = low(g)
                    sq_ref[:, at : at + HD] += jnp.sum(
                        out_blk[:, at : at + HD].astype(jnp.float32), axis=0, keepdims=True)

        pltpu.emit_pipeline(
            finish_body, grid=(total_len // block,), in_specs=[spec(128), spec(128)],
            out_specs=[spec(3 * qw)],
        )(cos_ref, sin_ref, dqkv_out)

    pl.run_scoped(
        attend_back,
        pltpu.VMEM((total_len, qw), jnp.bfloat16),
        pltpu.VMEM((total_len, qw), jnp.bfloat16),
        pltpu.VMEM((total_len, qw), jnp.bfloat16),
        pltpu.VMEM((heads, total_len), jnp.float32),
        pltpu.VMEM((total_len, qw), jnp.float32),
        pltpu.VMEM((total_len, qw), jnp.float32),
        pltpu.VMEM((total_len, qw), jnp.float32),
        pltpu.VMEM((heads, total_len), jnp.float32),
        pltpu.SemaphoreType.DMA((4,)),
    )
    while sum_step < line:
        start_sum(sum_step)
        sum_step += 1


    def e_body(dqkv_blk, dfc_blk, x_blk, stat_blk, e_blk):
        mean, rstd = stat_blk[:, 0:1], stat_blk[:, 1:2]
        step = 512
        for at in range(0, width, step):
            cols = slice(at, at + step)
            d1 = dot_nt(dqkv_blk[:, :qw], wq_ref[0, cols, :])
            d1 += dot_nt(dqkv_blk[:, qw : 2 * qw], wq_ref[1, cols, :])
            d1 += dot_nt(dqkv_blk[:, 2 * qw :], wq_ref[2, cols, :])
            d2 = dot_nt(dfc_blk[...], w1_ref[cols, :])
            xhat = (x_blk[:, cols].astype(jnp.float32) - mean) * rstd
            e_blk[:, cols] = low(d1 * kvec[2:3, cols] + d2 * kvec[4:5, cols])
            ln_ref[0:1, cols] += jnp.sum(d1 * xhat, axis=0, keepdims=True)
            ln_ref[1:2, cols] += jnp.sum(d1, axis=0, keepdims=True)
            ln_ref[2:3, cols] += jnp.sum(d2 * xhat, axis=0, keepdims=True)
            ln_ref[3:4, cols] += jnp.sum(d2, axis=0, keepdims=True)

    wspec = lambda n: pl.BlockSpec((wblock, n), lambda i: (i, 0))
    pltpu.emit_pipeline(
        e_body, grid=(total_len // wblock,),
        in_specs=[wspec(3 * qw), wspec(ff), wspec(width), wspec(128)], out_specs=[wspec(width)],
    )(dqkv_out, dfc_out, x_all, stat_out, e_out)
    ends = [
        pltpu.make_async_copy(kvec, vec_out, keep.at[0]),
        pltpu.make_async_copy(sfc_ref, sfc_out, keep.at[1]),
        pltpu.make_async_copy(sq_ref, sq_out, keep.at[2]),
        pltpu.make_async_copy(ln_ref, ln_out, keep.at[3]),
    ]
    for copy in ends:
        copy.start()

    def hidden_body(ways):
        def run(x_blk, part_blk, *blks):
            total = x_blk[...].astype(jnp.float32) + part_blk[...].astype(jnp.float32)
            for blk in blks[:-1]:
                total = total + blk[...].astype(jnp.float32)
            blks[-1][...] = low(total + kvec[0:1] + kvec[1:2])

        pltpu.emit_pipeline(
            run, grid=(length // block,), in_specs=[spec(width)] * (2 + len(ways)),
            out_specs=[spec(width)],
        )(x_ref, part_out.at[rows_of(tp)], *[land_out.at[w, line - 2] for w in ways], hidden_out)

    for way in range(2):
        @pl.when(sum_arrives(way, line - 1))
        def _():
            sum_arrival(way, line - 1).wait_recv()

    @pl.when(tp == 0)
    def _():
        hidden_body([1])

    @pl.when(tp == line - 1)
    def _():
        hidden_body([0])

    @pl.when((tp > 0) & (tp < line - 1))
    def _():
        hidden_body([0, 1])

    for step in range(1, line):
        for way in range(2):
            @pl.when(sum_sends(way, step))
            def _():
                sum_copy(way, step, False).wait_send()

    for a in range(count):
        for slot in range(1 + 2 * hops):
            pair_copy(a, slot).wait_send()
        for hop in range(hops):
            for way in range(2):
                ring_copy(a, way, hop).wait_send()
    for b in range(2):
        for hop in range(line - 1):
            for way in range(2):
                @pl.when(sends(way, hop))
                def _():
                    line_copy(b, way, hop).wait_send()
    for copy in ends:
        copy.wait()


def head(small, wq, w1, wd, w2, x, cot, cosine, sine, n_q, n_b, dp_count, tp_count, collective_id):
    piece, width = x.shape
    length = piece * tp_count
    qw, ff = wd.shape[0], w2.shape[0]
    heads = qw // HD
    chips = dp_count // 2
    hops = chips // 2
    bf, f32 = jnp.bfloat16, jnp.float32
    sds = jax.ShapeDtypeStruct
    steps = max(tp_count - 1, 1)
    out_shape = [
        sds((length, width), bf), sds((length, width), bf),
        sds((length, width), bf), sds((length, width), bf),
        sds((length, qw), bf), sds((length, qw), bf), sds((length, qw), bf),
        sds((length, ff), bf), sds((length, ff), bf), sds((length, 128), f32),
        sds((length, qw), bf), sds((heads, length), f32), sds((length, width), bf),
        sds((length, qw), bf), sds((length, ff), bf),
        sds((2, steps, piece, width), bf), sds((2, steps, piece, width), bf),
        sds((length, 3 * qw), bf), sds((length, width), bf), sds((piece, width), bf),
        sds((8, width), f32), sds((1, ff), f32), sds((1, 3 * qw), f32), sds((8, width), f32),
    ]
    dma = pltpu.SemaphoreType.DMA
    hbm = pl.BlockSpec(memory_space=pl.ANY)
    line = max(tp_count - 1, 1)
    return pl.pallas_call(
        functools.partial(head_kernel, (chips, tp_count, heads, n_q, n_b)),
        out_shape=out_shape,
        in_specs=[hbm] * 9,
        out_specs=[hbm] * len(out_shape),
        scratch_shapes=[
            pltpu.VMEM((small.shape[0] * dp_count, 128), bf),
            pltpu.VMEM((3, width, qw), bf),
            pltpu.VMEM((width, ff), bf),
            pltpu.VMEM((qw, width), bf),
            pltpu.VMEM((ff, width), bf),
            pltpu.VMEM((8, width), f32),
            pltpu.VMEM((1, 3 * qw), f32),
            pltpu.VMEM((1, ff), f32),
            pltpu.VMEM((length, qw), bf),
            pltpu.VMEM((length, qw), bf),
            pltpu.VMEM((1, 3 * qw), f32),
            pltpu.VMEM((8, width), f32),
            dma((5, 2, hops)), dma((5, 2, hops)),
            dma((5, 1 + 2 * hops)), dma((5, 1 + 2 * hops)),
            dma((2, 2, line)), dma((2, 2, line)), dma((7,)),
            dma((2, line)), dma((2, line)), dma((4,)),
        ],
        compiler_params=pltpu.CompilerParams(
            collective_id=collective_id, has_side_effects=True,
            vmem_limit_bytes=62 * 1024 * 1024),
        name="head",
    )(small, wq, w1, wd, w2, x, cot, cosine, sine)


def tail_kernel(cfg, *refs):
    chips, line = cfg
    hops = chips // 2
    refs = list(refs)

    def take(n):
        out, refs[:n] = refs[:n], []
        return out

    act, heads_in, cot, n1, n2, dfc, dqkv, line_ref, flat_ref = take(9)
    own_fc2, own_dense, own_fc1, own_qkv, own_small = take(5)
    held, paired, landed, first_landed = take(4)
    small, s_held, s_paired, s_landed, line_land = take(5)
    (pair_send, pair_recv, ring_send, ring_recv, s_load, s_pair_send, s_pair_recv, s_ring_send,
     s_ring_recv, line_send, line_recv) = refs
    ff, qw = act.shape[1], heads_in.shape[1]
    length = act.shape[0]
    rows = held.shape[1]
    dp = lax.axis_index("dp")
    tp = lax.axis_index("tp")
    core = lax.rem(dp, 2)
    place = ring_place(lax.div(dp, 2), chips)

    def chip_at(ring_pos):
        return ring_place(lax.rem(ring_pos + chips, chips), chips)

    right, left = chip_at(place + 1) * 2 + core, chip_at(place - 1) * 2 + core
    sibling = dp + 1 - 2 * core
    barrier = pltpu.get_barrier_semaphore()
    for partner in (right, left, sibling):
        pl.semaphore_signal(barrier, 1, device_id={"dp": partner}, device_id_type=MESH)
    for n in range(1, line):
        pl.semaphore_signal(
            barrier, 1, device_id={"tp": lax.rem(tp + n, line)}, device_id_type=MESH)
    pl.semaphore_wait(barrier, 3 + line - 1)

    def line_copy(n):
        return pltpu.make_async_remote_copy(
            src_ref=line_ref, dst_ref=line_land.at[n - 1],
            send_sem=line_send.at[n - 1], recv_sem=line_recv.at[n - 1],
            device_id={"tp": lax.rem(tp + n, line)}, device_id_type=MESH)

    for n in range(1, line):
        line_copy(n).start()

    offsets = [hops]
    for near in range(hops - 1, 0, -1):
        offsets += [near, -near]
    offsets.append(0)
    own = chips - 1
    spans = [(0, ff), (ff, qw), (ff + qw, ff), (2 * ff + qw, 3 * qw)]

    def f32(value):
        return value.astype(jnp.float32)

    def over_rows(count, body):
        step = min(count, 32)

        def run(t, carry):
            body(pl.multiple_of(t * step, step), step)
            return carry

        lax.fori_loop(0, count // step, run, 0)

    def pair_arrival(slot, unit):
        at, wide = spans[unit]
        view = paired.at[slot, :, pl.ds(at, wide)]
        return pltpu.make_async_remote_copy(
            src_ref=view, dst_ref=view,
            send_sem=pair_send.at[slot, unit], recv_sem=pair_recv.at[slot, unit],
            device_id={"dp": sibling}, device_id_type=MESH)

    def pair_sum(slot, unit):
        at, wide = spans[unit]
        cols = slice(at, at + wide)
        pair_arrival(slot, unit).wait_recv()

        def body(r, n):
            r = pl.ds(r, n)
            held[slot, r, cols] = low(f32(held[slot, r, cols]) + f32(paired[slot, r, cols]))

        over_rows(rows, body)

    def slot_of(way, step):
        return offsets.index((hops - step) * (1 if way == 0 or step == 0 else -1))

    def ring_rows(way, step):
        return (way * (rows // 2), rows // 2) if step == 0 else (0, rows)

    def ring_copy(way, step, unit):
        at, wide = spans[unit]
        first, n = ring_rows(way, step)
        view = held.at[slot_of(way, step), pl.ds(first, n), pl.ds(at, wide)]
        if step == 0:
            dst = first_landed.at[pl.ds(first, n), pl.ds(at, wide)]
        else:
            dst = landed.at[way, step - 1, :, pl.ds(at, wide)]
        return pltpu.make_async_remote_copy(
            src_ref=view, dst_ref=dst,
            send_sem=ring_send.at[way, step, unit], recv_sem=ring_recv.at[way, step, unit],
            device_id={"dp": right if way == 0 else left}, device_id_type=MESH)

    def add_landed(way, step, unit):
        at, wide = spans[unit]
        cols = slice(at, at + wide)
        slot = slot_of(way, step + 1)
        first, n = ring_rows(way, step)
        ring_copy(way, step, unit).wait_recv()

        def body(r, size):
            r = pl.ds(pl.multiple_of(r + first, 16), size)
            if step == 0:
                moved = first_landed[r, cols]
            else:
                moved = landed[way, step - 1, r, cols]
            held[slot, r, cols] = low(f32(held[slot, r, cols]) + f32(moved))

        over_rows(n, body)

    def ring_after(slot, units):
        for step in range(hops):
            for way in range(2):
                if slot_of(way, step) != slot or slot == own:
                    continue
                for unit in units:
                    if step > 0:
                        add_landed(way, step - 1, unit)
                    ring_copy(way, step, unit).start()

    def compute(big, mid, lhs, turn, out, lhs_sem, big_sem, mid_sem):
        loads = [(cot, 0, slot) for slot in range(chips)]
        loads += [(src, 2, slot) for slot in range(chips) for src in (n2, n1)]

        def lhs_load(i):
            src, _, slot = loads[i]
            chip = chip_at(place + offsets[slot])
            cols = pl.ds(pl.multiple_of(chip * 2 * rows, 128), 2 * rows)
            return pltpu.make_async_copy(src.at[:, cols], lhs.at[i % 2], lhs_sem.at[i % 2])

        phase_loads = (
            (pltpu.make_async_copy(act, big, big_sem.at[0]),
             pltpu.make_async_copy(heads_in, mid.at[:, pl.ds(0, qw)], mid_sem.at[0])),
            (pltpu.make_async_copy(dfc, big, big_sem.at[1]),
             pltpu.make_async_copy(dqkv, mid, mid_sem.at[1])),
        )
        lhs_load(0).start()
        for copy in phase_loads[0]:
            copy.start()
        busy = [None, None]
        counter = 0
        pending = []

        def product(i, slot, unit, rhs):
            nonlocal counter
            at, wide = spans[unit]
            which = counter % 2
            counter += 1
            if busy[which] is not None:
                busy[which].wait_send()
            step = 512 if wide % 512 == 0 else 256
            for col in range(0, wide, step):
                out[which, :, col : col + step] = low(
                    dot_nn(turn[...], rhs[:, col : col + step]))
            mine = pl.ds(pl.multiple_of(core * rows, 16), rows)
            held[slot, :, at : at + wide] = out[which, mine, :wide]
            theirs = pl.ds(pl.multiple_of((1 - core) * rows, 16), rows)
            copy = pltpu.make_async_remote_copy(
                src_ref=out.at[which, theirs, pl.ds(0, wide)],
                dst_ref=paired.at[slot, :, pl.ds(at, wide)],
                send_sem=pair_send.at[slot, unit], recv_sem=pair_recv.at[slot, unit],
                device_id={"dp": sibling}, device_id_type=MESH)
            copy.start()
            busy[which] = copy
            while pending:
                pair_sum(*pending.pop(0))
            pending.append((slot, unit))

        def settle():
            while pending:
                pair_sum(*pending.pop(0))

        def left_side(i):
            lhs_load(i).wait()
            if i + 1 < len(loads):
                lhs_load(i + 1).start()
            turn[...] = lhs[i % 2].T

        for phase in range(2):
            units = (0, 1) if phase == 0 else (2, 3)
            for slot in range(chips):
                if phase == 0:
                    left_side(slot)
                    if slot == 0:
                        for copy in phase_loads[0]:
                            copy.wait()
                    product(slot, slot, 0, big)
                    product(slot, slot, 1, mid)
                else:
                    i = chips + 2 * slot
                    left_side(i)
                    if slot == 0:
                        phase_loads[1][0].wait()
                    product(i, slot, 2, big)
                    left_side(i + 1)
                    if slot == 0:
                        phase_loads[1][1].wait()
                    product(i + 1, slot, 3, mid)
                if slot == 0:
                    settle()
                    ring_after(0, units)
                elif slot == chips - 2:
                    settle()
                    for ready in range(1, chips - 1):
                        ring_after(ready, units)
            if phase == 0:
                for copy in phase_loads[1]:
                    copy.start()
        settle()
        for copy in busy:
            copy.wait_send()

    pl.run_scoped(
        compute,
        pltpu.VMEM((length, ff), jnp.bfloat16),
        pltpu.VMEM((length, 3 * qw), jnp.bfloat16),
        pltpu.VMEM((2, length, 2 * rows), jnp.bfloat16),
        pltpu.VMEM((2 * rows, length), jnp.bfloat16),
        pltpu.VMEM((2, 2 * rows, max(ff, 3 * qw)), jnp.bfloat16),
        pltpu.SemaphoreType.DMA((2,)),
        pltpu.SemaphoreType.DMA((2,)),
        pltpu.SemaphoreType.DMA((2,)),
    )

    for n in range(1, line):
        line_copy(n).wait_recv()
    total = line_ref[...]
    for n in range(1, line):
        total = total + line_land[n - 1]
    rows_z = line_ref.shape[1]
    small[:, :rows_z] = total
    small[:, rows_z:] = flat_ref[...]
    s_rows = small.shape[1]

    def s_pair(slot):
        chip = chip_at(place + offsets[slot])
        return pltpu.make_async_remote_copy(
            src_ref=small.at[chip * 2 + 1 - core], dst_ref=s_paired.at[slot],
            send_sem=s_pair_send.at[slot], recv_sem=s_pair_recv.at[slot],
            device_id={"dp": sibling}, device_id_type=MESH)

    def s_keep(slot):
        chip = chip_at(place + offsets[slot])
        return pltpu.make_async_copy(small.at[chip * 2 + core], s_held.at[slot], s_load.at[slot])

    def s_ring(way, step):
        n = s_rows // 2 if step == 0 else s_rows
        first = way * n if step == 0 else 0
        return pltpu.make_async_remote_copy(
            src_ref=s_held.at[slot_of(way, step), pl.ds(first, n)],
            dst_ref=s_landed.at[way, step, pl.ds(first, n)],
            send_sem=s_ring_send.at[way, step], recv_sem=s_ring_recv.at[way, step],
            device_id={"dp": right if way == 0 else left}, device_id_type=MESH)

    for slot in range(chips):
        s_keep(slot).start()
        s_pair(slot).start()
    for slot in range(chips):
        s_keep(slot).wait()
        s_pair(slot).wait_recv()
        s_held[slot] += s_paired[slot]
        for step in range(hops):
            for way in range(2):
                if slot_of(way, step) != slot or slot == own:
                    continue
                if step > 0:
                    n = s_rows // 2 if step == 1 else s_rows
                    first = way * n if step == 1 else 0
                    s_ring(way, step - 1).wait_recv()
                    s_held[slot, first : first + n] += s_landed[way, step - 1, first : first + n]
                s_ring(way, step).start()
    for way in range(2):
        s_ring(way, hops - 1).wait_recv()
    own_small[...] = s_held[own] + s_landed[0, hops - 1] + s_landed[1, hops - 1]

    def finish(wide_buf, tall_buf, done):
        targets = [
            (0, [own_fc2]), (1, [own_dense]), (2, [own_fc1]),
            (3, [own_qkv.at[w] for w in range(3)]),
        ]
        last = {}

        def total_at(unit, at, size):
            cols = slice(at, at + size)
            value = f32(held[own, :, cols])
            if hops == 1:
                return value + f32(first_landed[:, cols])
            return value + f32(landed[0, hops - 2, :, cols]) + f32(landed[1, hops - 2, :, cols])

        for unit, outs in targets:
            at, wide = spans[unit]
            for way in range(2):
                ring_copy(way, hops - 1, unit).wait_recv()
            if unit < 2:
                if "tall" in last:
                    last["tall"].wait()
                for col in range(0, wide, 256):
                    tall_buf[col : col + 256, :] = total_at(unit, at + col, 256).T
                copy = pltpu.make_async_copy(tall_buf.at[pl.ds(0, wide)], outs[0], done.at[0])
                copy.start()
                last["tall"] = copy
            else:
                if "wide" in last:
                    for copy in last["wide"]:
                        copy.wait()
                for col in range(0, wide, 256):
                    wide_buf[:, col : col + 256] = total_at(unit, at + col, 256)
                each = wide // len(outs)
                copies = [
                    pltpu.make_async_copy(
                        wide_buf.at[:, pl.ds(w * each, each)], out, done.at[1 + w])
                    for w, out in enumerate(outs)
                ]
                for copy in copies:
                    copy.start()
                last["wide"] = copies
        last["tall"].wait()
        for copy in last["wide"]:
            copy.wait()

    pl.run_scoped(
        finish,
        pltpu.VMEM((rows, max(ff, 3 * qw)), jnp.float32),
        pltpu.VMEM((max(ff, qw), rows), jnp.float32),
        pltpu.SemaphoreType.DMA((4,)),
    )
    for way in range(2):
        for step in range(hops):
            for unit in range(4):
                ring_copy(way, step, unit).wait_send()
            s_ring(way, step).wait_send()
    for slot in range(chips):
        s_pair(slot).wait_send()
    for n in range(1, line):
        line_copy(n).wait_send()


def tail(act, heads_in, cot, n1, n2, dfc, dqkv, line_sums, flat_sums, dp_count, tp_count, collective_id):
    chips = dp_count // 2
    hops = chips // 2
    length, ff = act.shape
    qw = heads_in.shape[1]
    rows = cot.shape[1] // dp_count
    cols = 2 * ff + 4 * qw
    rows_s = line_sums.shape[1] + flat_sums.shape[1]
    bf, f32 = jnp.bfloat16, jnp.float32
    dma = pltpu.SemaphoreType.DMA
    hbm = pl.BlockSpec(memory_space=pl.ANY)
    vm = pl.BlockSpec(memory_space=pltpu.VMEM)
    line = max(tp_count - 1, 1)
    sds = jax.ShapeDtypeStruct
    return pl.pallas_call(
        functools.partial(tail_kernel, (chips, tp_count)),
        out_shape=[
            sds((ff, rows), f32), sds((qw, rows), f32), sds((rows, ff), f32),
            sds((3, rows, qw), f32), sds((rows_s, 128), f32),
        ],
        in_specs=[hbm] * 7 + [vm, vm],
        out_specs=[hbm] * 4 + [vm],
        scratch_shapes=[
            pltpu.VMEM((chips, rows, cols), bf),
            pltpu.VMEM((chips, rows, cols), bf),
            pltpu.VMEM((2, max(hops - 1, 1), rows, cols), bf),
            pltpu.VMEM((rows, cols), bf),
            pltpu.VMEM((dp_count, rows_s, 128), f32),
            pltpu.VMEM((chips, rows_s, 128), f32),
            pltpu.VMEM((chips, rows_s, 128), f32),
            pltpu.VMEM((2, hops, rows_s, 128), f32),
            pltpu.VMEM((line,) + line_sums.shape, f32),
            dma((chips, 4)), dma((chips, 4)), dma((2, hops, 4)), dma((2, hops, 4)),
            dma((chips,)), dma((chips,)), dma((chips,)), dma((2, hops)), dma((2, hops)),
            dma((line,)), dma((line,)),
        ],
        compiler_params=pltpu.CompilerParams(
            collective_id=collective_id, has_side_effects=True,
            vmem_limit_bytes=62 * 1024 * 1024),
        cost_estimate=pl.CostEstimate(
            flops=2 * length * cot.shape[1] * cols, bytes_accessed=400_000_000, transcendentals=0),
        name="tail",
    )(act, heads_in, cot, n1, n2, dfc, dqkv, line_sums, flat_sums)


def pack_small(wide, narrow):
    rows = []
    first = jnp.concatenate([part.reshape(-1, 128) for part in wide], axis=0)
    rows.append(jnp.pad(first, ((0, 16 - first.shape[0]), (0, 0))))
    count = 0
    for part in narrow:
        flat = part.reshape(-1)
        need = -(-flat.size // 128)
        rows.append(jnp.pad(flat, (0, need * 128 - flat.size)).reshape(need, 128))
        count += need
    rows.append(jnp.zeros((16 - count, 128), jnp.bfloat16))
    return jnp.concatenate(rows, axis=0)


def by_owner(rows, dp_count):
    count = -(-rows.shape[1] // 2048) * 16
    padded = jnp.pad(rows, ((0, 0), (0, count * 128 - rows.shape[1])))
    return padded.reshape(dp_count, count, 128)


def body(
    hidden_in,
    triple_projection_weight,
    triple_projection_bias,
    attention_out_weight,
    b_dense,
    feedforward_in_weight,
    feedforward_in_bias,
    feedforward_out_weight,
    b_fc2,
    ln1_gain,
    ln1_bias,
    ln2_gain,
    ln2_bias,
    grad_out,
):
    _, piece_len, width = hidden_in.shape
    tp_count = lax.axis_size("tp")
    dp_count = lax.axis_size("dp")
    length = piece_len * tp_count
    cosine, sine = rotary_tables(length)
    small = pack_small(
        [b_dense, b_fc2, ln1_gain, ln1_bias, ln2_gain, ln2_bias],
        [triple_projection_bias, feedforward_in_bias],
    )
    n_q = -(-triple_projection_bias.size // 128)
    n_b = -(-feedforward_in_bias.size // 128)
    outs = head(
        small,
        triple_projection_weight.transpose(1, 0, 2),
        feedforward_in_weight,
        attention_out_weight,
        feedforward_out_weight,
        hidden_in[0],
        grad_out[0],
        cosine,
        sine,
        n_q,
        n_b,
        dp_count,
        tp_count,
        0,
    )
    _, cot_seq, norm_one, norm_two = outs[:4]
    act, head_out, d_fc = outs[7], outs[10], outs[14]
    d_qkv, e_sum, hidden_out, vectors, sum_bfc1, sum_bqkv, ln_sums = outs[17:]
    e_piece = lax.psum_scatter(e_sum, "tp", scatter_dimension=0, tiled=True).astype(jnp.float32)

    cot_piece = grad_out[0].astype(jnp.float32)
    line_sums = ln_sums[:5].reshape(5, dp_count, -1).transpose(1, 0, 2).reshape(dp_count, -1)
    flat_sums = jnp.concatenate([sum_bqkv, sum_bfc1], axis=1).reshape(-1, dp_count).T
    line_rows, flat_rows = by_owner(line_sums, dp_count), by_owner(flat_sums, dp_count)
    own_fc2, own_dense, own_fc1, own_qkv, own_small = tail(
        act, head_out, cot_seq, norm_one, norm_two, d_fc, d_qkv, line_rows, flat_rows,
        dp_count, tp_count, 1,
    )
    e_piece, own_small = lax.optimization_barrier((e_piece, own_small))
    own_line = own_small[: line_rows.shape[1]].reshape(-1)[: line_sums.shape[1]].reshape(5, -1)
    own_flat = own_small[line_rows.shape[1] :].reshape(-1)[: flat_sums.shape[1]]
    split = sum_bqkv.size // dp_count

    x_own = hidden_in[0].astype(jnp.float32)
    mean = jnp.mean(x_own, axis=-1, keepdims=True)
    centered = x_own - mean
    rstd = lax.rsqrt(jnp.mean(centered * centered, axis=-1, keepdims=True) + EPSILON)
    xhat = centered * rstd
    back = (
        e_piece
        - jnp.mean(e_piece, axis=-1, keepdims=True)
        - xhat * jnp.mean(e_piece * xhat, axis=-1, keepdims=True)
    ) * rstd
    grad_in = (cot_piece + back)[None]
    return (
        hidden_out[None],
        grad_in,
        own_qkv.transpose(1, 0, 2),
        own_flat[:split].reshape(triple_projection_bias.shape),
        own_dense,
        own_line[4],
        own_fc1,
        own_flat[split:].reshape(feedforward_in_bias.shape),
        own_fc2,
        own_line[4],
        own_line[0],
        own_line[1],
        own_line[2],
        own_line[3],
    )


def solution(mesh):
    return jax.shard_map(
        body,
        mesh=mesh,
        in_specs=(
            P("dp", "tp", None),
            P("dp", None, "tp"),
            P(None, "tp", "dp"),
            P("tp", "dp"),
            P("dp"),
            P("dp", "tp"),
            P("tp", "dp"),
            P("tp", "dp"),
            P("dp"),
            P("dp"),
            P("dp"),
            P("dp"),
            P("dp"),
            P("dp", "tp", None),
        ),
        out_specs=(
            P("dp", "tp", None),
            P("dp", "tp", None),
            P("dp", None, "tp"),
            P(None, "tp", "dp"),
            P("tp", "dp"),
            P("dp"),
            P("dp", "tp"),
            P("tp", "dp"),
            P("tp", "dp"),
            P("dp"),
            P("dp"),
            P("dp"),
            P("dp"),
            P("dp"),
        ),
        check_vma=False,
    )
```

```python
import functools
import math

import jax
import jax.numpy as jnp
import numpy as np
from jax import lax
from jax.experimental import pallas as pl
from jax.experimental.pallas import tpu as pltpu
from jax.sharding import PartitionSpec as P

MESH = pl.DeviceIdType.MESH
EPSILON = 1e-05
MASKED = -1e30
HD = 256
ROT = 64
VMEM_LIMIT = 60 * 1024 * 1024
LOG2E = 1.4426950408889634


def low(value):
    return value.astype(jnp.bfloat16)


def dot_nn(a, b):
    return lax.dot_general(a, b, (((1,), (0,)), ((), ())), preferred_element_type=jnp.float32)


def dot_nt(a, b):
    return lax.dot_general(a, b, (((1,), (1,)), ((), ())), preferred_element_type=jnp.float32)


def dot_tn(a, b):
    return lax.dot_general(a, b, (((0,), (0,)), ((), ())), preferred_element_type=jnp.float32)


def rotary_tables(length):
    half = ROT // 2
    exponent = np.arange(half, dtype=np.float32) * np.float32(2.0 / ROT)
    inverse = np.exp(exponent * np.float32(-math.log(10000.0)), dtype=np.float32)
    angle = np.arange(length, dtype=np.float32)[:, None] * inverse[None, :]
    cosine = np.ones((length, 128), np.float32)
    sine = np.zeros((length, 128), np.float32)
    cosine[:, :half] = cosine[:, half:ROT] = np.cos(angle)
    sine[:, :half] = -np.sin(angle)
    sine[:, half:ROT] = np.sin(angle)
    return jnp.asarray(cosine), jnp.asarray(sine)


def turned(part):
    half = ROT // 2
    lane = lax.broadcasted_iota(jnp.int32, part.shape, 1)
    return jnp.where(
        lane < half, pltpu.roll(part, 128 - half, 1), pltpu.roll(part, half, 1)
    )


def ring_place(chip, chips):
    half = chips // 2
    return jnp.where(chip < half, chip, 3 * half - 1 - chip)


def shard_view(ref, kind, owner, part, extent):
    axis = 1 if kind == "mid" else 0
    rows = extent[axis]
    first, size = (0, rows) if part == 0 else ((part - 1) * (rows // 2), rows // 2)
    if kind == "row":
        return ref.at[pl.ds(owner * rows + first, size)]
    if kind == "mid":
        return ref.at[:, pl.ds(owner * rows + first, size)]
    return ref.at[pl.ds(first, size), pl.ds(owner * extent[1], extent[1])]


def own_view(ref, kind, part, extent):
    if part == 0:
        return ref
    axis = 1 if kind == "mid" else 0
    half = extent[axis] // 2
    at = pl.ds((part - 1) * half, half)
    return ref.at[:, at] if kind == "mid" else ref.at[at]


def picked(tp, values):
    out = values[0]
    for i in range(1, len(values)):
        out = jnp.where(tp == i, values[i], out)
    return out


def order_of(line):
    return [sorted(range(line), key=lambda p: (abs(p - z), p)) for z in range(line)]


def head_kernel(cfg, *refs):
    chips, line, heads, n_q, n_b = cfg
    hops = chips // 2
    refs = list(refs)

    def take(n):
        out, refs[:n] = refs[:n], []
        return out

    shards = take(5)
    x_ref, cot_ref, cos_ref, sin_ref = take(4)
    (x_all, cot_all, n1_out, n2_out, q_out, k_out, v_out, act_out, slope_out,
     stat_out, head_out, lse_out, part_out, dh_out, dfc_out, land_out, acc_out, dqkv_out, e_out,
     hidden_out, vec_out, sfc_out, sq_out, ln_out) = take(24)
    fulls = take(5)
    small_ref, wq_ref, w1_ref, wd_ref, w2_ref = fulls
    kvec, bq_ref, b1_ref, k_buf, v_buf, sq_ref, ln_ref = take(7)
    (ring_send, ring_recv, pair_send, pair_recv, line_send, line_recv, local,
     sum_send, sum_recv, keep) = refs
    kinds = ["row", "mid", "row", "col", "col"]
    extents = [s.shape for s in shards]
    count = 5
    dp = lax.axis_index("dp")
    tp = lax.axis_index("tp")
    dp_count = 2 * chips
    core = lax.rem(dp, 2)
    place = ring_place(lax.div(dp, 2), chips)
    length = x_ref.shape[0]
    total_len = length * line
    width = x_ref.shape[1]

    def device(ring_pos):
        return ring_place(lax.rem(ring_pos + chips, chips), chips) * 2 + core

    right, left = device(place + 1), device(place - 1)
    sibling = dp + 1 - 2 * core
    barrier = pltpu.get_barrier_semaphore()
    for partner in (right, left, sibling):
        pl.semaphore_signal(barrier, 1, device_id={"dp": partner}, device_id_type=MESH)

    @pl.when(tp > 0)
    def _():
        pl.semaphore_signal(barrier, 1, device_id={"tp": tp - 1}, device_id_type=MESH)

    @pl.when(tp < line - 1)
    def _():
        pl.semaphore_signal(barrier, 1, device_id={"tp": tp + 1}, device_id_type=MESH)

    pl.semaphore_wait(barrier, 3 + jnp.where(tp > 0, 1, 0) + jnp.where(tp < line - 1, 1, 0))

    def ring_copy(a, way, hop, arriving=False):
        back = hop + 1 if arriving else hop
        owner = device(place - back) if way == 0 else device(place + back)
        part = 0 if hop < hops - 1 else 1 + way
        view = shard_view(fulls[a], kinds[a], owner, part, extents[a])
        own = hop == 0 and not arriving
        return pltpu.make_async_remote_copy(
            src_ref=own_view(shards[a], kinds[a], part, extents[a]) if own else view,
            dst_ref=view,
            send_sem=ring_send.at[a, way, hop],
            recv_sem=ring_recv.at[a, way, hop],
            device_id={"dp": right if way == 0 else left},
            device_id_type=MESH,
        )

    def pair_copy(a, slot, arriving=False):
        if slot == 0:
            owner, part = dp, 0
        else:
            hop, way = divmod(slot - 1, 2)
            owner = device(place - 1 - hop) if way == 0 else device(place + 1 + hop)
            part = 0 if hop < hops - 1 else 1 + way
        if arriving:
            owner = owner + 1 - 2 * core
        view = shard_view(fulls[a], kinds[a], owner, part, extents[a])
        return pltpu.make_async_remote_copy(
            src_ref=shards[a] if slot == 0 and not arriving else view,
            dst_ref=view,
            send_sem=pair_send.at[a, slot],
            recv_sem=pair_recv.at[a, slot],
            device_id={"dp": sibling},
            device_id_type=MESH,
        )

    def rows_of(piece):
        return pl.ds(pl.multiple_of(piece * length, length), length)

    def line_copy(b, way, hop, arriving=False):
        back = hop + 1 if arriving else hop
        piece = tp - back if way == 0 else tp + back
        view = (x_all, cot_all)[b].at[rows_of(piece)]
        to = tp + 1 if way == 0 else tp - 1
        if arriving:
            to = tp - 1 if way == 0 else tp + 1
        return pltpu.make_async_remote_copy(
            src_ref=(x_ref, cot_ref)[b] if hop == 0 and not arriving else view,
            dst_ref=view,
            send_sem=line_send.at[b, way, hop],
            recv_sem=line_recv.at[b, way, hop],
            device_id={"tp": to},
            device_id_type=MESH,
        )

    def sends(way, hop):
        return (tp < line - 1) & (tp >= hop) if way == 0 else (tp > 0) & (tp + hop < line)

    def arrives(way, hop):
        return tp - 1 - hop >= 0 if way == 0 else tp + 1 + hop < line

    def start_line(b, hop):
        for way in range(2):
            @pl.when(sends(way, hop))
            def _():
                line_copy(b, way, hop).start()

    def step_line(b, hop):
        for way in range(2):
            @pl.when(arrives(way, hop))
            def _():
                line_copy(b, way, hop, True).wait_recv()

            if hop + 1 < line - 1:
                @pl.when(sends(way, hop + 1))
                def _():
                    line_copy(b, way, hop + 1).start()

    early, late = range(3), range(3, count)
    locals_ = [
        pltpu.make_async_copy(
            shards[a], shard_view(fulls[a], kinds[a], dp, 0, extents[a]), local.at[a])
        for a in range(count)
    ]
    locals_.append(pltpu.make_async_copy(x_ref, x_all.at[rows_of(tp)], local.at[count]))
    locals_.append(pltpu.make_async_copy(cot_ref, cot_all.at[rows_of(tp)], local.at[count + 1]))

    def start_ring(group):
        for a in group:
            for way in range(2):
                ring_copy(a, way, 0).start()
            pair_copy(a, 0).start()

    def step_ring(group, hop):
        for a in group:
            for way in range(2):
                ring_copy(a, way, hop, True).wait_recv()
                if hop + 1 < hops:
                    ring_copy(a, way, hop + 1).start()
                pair_copy(a, 1 + 2 * hop + way).start()

    def end_ring(group):
        for a in group:
            locals_[a].wait()
            for slot in range(1 + 2 * hops):
                pair_copy(a, slot, True).wait_recv()

    start_line(0, 0)
    start_ring(early)
    for copy in locals_:
        copy.start()
    step_ring(early, 0)
    start_ring(late)
    step_line(0, 0)
    for hop in range(1, hops):
        step_ring(early, hop)
    end_ring(early)

    small_rows = extents[0][0]
    per = width // dp_count // 128
    for d in range(dp_count):
        block = small_ref[d * small_rows : (d + 1) * small_rows].astype(jnp.float32)
        for vec in range(6):
            for r in range(per):
                at = (d * per + r) * 128
                row = vec * per + r
                kvec[vec : vec + 1, at : at + 128] = block[row : row + 1]
    span = 128 * dp_count
    lane = lax.broadcasted_iota(jnp.int32, (128, span), 0)
    col = lax.broadcasted_iota(jnp.int32, (128, span), 1)
    mixed = jnp.zeros((16, span), jnp.float32)
    for d in range(dp_count):
        hot = jnp.where(col == lane * dp_count + d, 1.0, 0.0).astype(jnp.bfloat16)
        mixed += dot_nn(small_ref[d * small_rows + 16 : d * small_rows + 32], hot)
    for ref, first, n in ((bq_ref, 0, n_q), (b1_ref, n_q, n_b)):
        for r in range(n):
            wide = min(span, ref.shape[1] - r * span)
            ref[0:1, r * span : r * span + wide] = mixed[first + r : first + r + 1, :wide]

    def front_body(x_blk, cos_blk, sin_blk, n1, n2, q, k, v, act, slope, stat):
        x = x_blk[...].astype(jnp.float32)
        mean = jnp.mean(x, axis=1, keepdims=True)
        centered = x - mean
        rstd = lax.rsqrt(jnp.mean(centered * centered, axis=1, keepdims=True) + EPSILON)
        xhat = centered * rstd
        n1[...] = low(xhat * kvec[2:3] + kvec[3:4])
        n2[...] = low(xhat * kvec[4:5] + kvec[5:6])
        lanes = lax.broadcasted_iota(jnp.int32, stat.shape, 1)
        stat[...] = jnp.where(lanes == 0, mean, rstd)
        cosine, sine = cos_blk[...], sin_blk[...]
        qw = heads * HD
        for which, out in enumerate((q, k, v)):
            for head in range(heads):
                cols = slice(head * HD, (head + 1) * HD)
                bias = slice(which * qw + head * HD, which * qw + (head + 1) * HD)
                raw = dot_nn(n1[...], wq_ref[which, :, cols]) + bq_ref[:, bias]
                if which < 2:
                    first = raw[:, :128]
                    first = first * cosine + turned(first) * sine
                    out[:, head * HD : head * HD + 128] = low(first)
                    out[:, head * HD + 128 : (head + 1) * HD] = low(raw[:, 128:])
                else:
                    out[:, cols] = low(raw)
        step = 256
        for at in range(0, w1_ref.shape[1], step):
            u = dot_nn(n2[...], w1_ref[:, at : at + step]) + b1_ref[:, at : at + step]
            cdf = 0.5 * (1.0 + lax.erf(u * (1.0 / math.sqrt(2.0))))
            pdf = jnp.exp(-0.5 * u * u) * (1.0 / math.sqrt(2.0 * math.pi))
            act[:, at : at + step] = low(u * cdf)
            slope[:, at : at + step] = low(cdf + u * pdf)

    block = min(256, length)
    wblock = min(512, length)

    def spec(n):
        return pl.BlockSpec((block, n), lambda i: (i, 0))

    qw, ff = heads * HD, w1_ref.shape[1]
    front_outs = (n1_out, n2_out, q_out, k_out, v_out, act_out, slope_out, stat_out)
    front_pipe = pltpu.emit_pipeline(
        front_body,
        grid=(length // block,),
        in_specs=[spec(width), spec(128), spec(128)],
        out_specs=[spec(ref.shape[1]) for ref in front_outs],
    )
    table = order_of(line)

    def piece_at(k):
        return picked(tp, [table[z][k] for z in range(line)])

    locals_[count].wait()
    for k in range(line):
        if k == 1:
            step_ring(late, 0)
        if k == line - 1:
            for hop in range(1, hops):
                step_ring(late, hop)
        if k > 1:
            step_line(0, k - 1)
        if k == line - 1:
            start_line(1, 0)
        at = rows_of(piece_at(k))
        front_pipe(
            x_all.at[at], cos_ref.at[at], sin_ref.at[at], *[ref.at[at] for ref in front_outs])

    end_ring(late)

    kv_copies = [
        pltpu.make_async_copy(k_out, k_buf, local.at[0]),
        pltpu.make_async_copy(v_out, v_buf, local.at[1]),
    ]
    for copy in kv_copies:
        copy.start()
    for copy in kv_copies:
        copy.wait()
    qblock = min(512, total_len)
    scale = LOG2E * HD ** -0.5

    def attend_body(q_blk, o_blk, lse_blk):
        i = pl.program_id(0)
        qs = [q_blk[:, h * HD : (h + 1) * HD] for h in range(heads)]

        def one(h, j, state, diagonal):
            top, total, acc = state
            rows = pl.ds(pl.multiple_of(j * qblock, qblock), qblock)
            key = k_buf[rows, h * HD : (h + 1) * HD]
            value = v_buf[rows, h * HD : (h + 1) * HD]
            s = dot_nt(key, qs[h]) * scale
            if diagonal:
                kp = lax.broadcasted_iota(jnp.int32, s.shape, 0)
                qp = lax.broadcasted_iota(jnp.int32, s.shape, 1)
                s = jnp.where(kp <= qp, s, MASKED)
            new_top = jnp.maximum(top, jnp.max(s, axis=0, keepdims=True))
            p = jnp.exp2(s - new_top)
            shrink = jnp.exp2(top - new_top)
            total = total * shrink + jnp.sum(p, axis=0, keepdims=True)
            acc = acc * shrink + dot_tn(value, low(p))
            return new_top, total, acc

        def start():
            return (
                jnp.full((1, qblock), MASKED, jnp.float32),
                jnp.zeros((1, qblock), jnp.float32),
                jnp.zeros((HD, qblock), jnp.float32),
            )

        def step(j, states):
            return tuple(one(h, j, states[h], False) for h in range(heads))

        states = lax.fori_loop(0, i, step, tuple(start() for _ in range(heads)))
        states = [one(h, i, states[h], True) for h in range(heads)]
        for h in range(heads):
            top, total, acc = states[h]
            o_blk[:, h * HD : (h + 1) * HD] = low((acc / total).T)
            lse_blk[h : h + 1, :] = top + jnp.log2(total)

    pltpu.emit_pipeline(
        attend_body,
        grid=(total_len // qblock,),
        in_specs=[pl.BlockSpec((qblock, qw), lambda i: (i, 0))],
        out_specs=[
            pl.BlockSpec((qblock, qw), lambda i: (i, 0)),
            pl.BlockSpec((heads, qblock), lambda i: (0, i)),
        ],
    )(q_out, head_out, lse_out)
    step_line(1, 0)
    cot_hop = 1

    def out_body(h_blk, a_blk, o_blk):
        step = 512
        for at in range(0, o_blk.shape[1], step):
            o_blk[:, at : at + step] = low(
                dot_nn(h_blk[...], wd_ref[:, at : at + step])
                + dot_nn(a_blk[...], w2_ref[:, at : at + step]))

    out_pipe = pltpu.emit_pipeline(
        out_body, grid=(length // block,), in_specs=[spec(qw), spec(ff)], out_specs=[spec(width)])

    def sum_copy(way, step, from_acc):
        dist = line - step
        piece = tp + dist if way == 0 else tp - dist
        src = acc_out.at[way, step - 2] if from_acc else part_out.at[rows_of(piece)]
        return pltpu.make_async_remote_copy(
            src_ref=src,
            dst_ref=land_out.at[way, step - 1],
            send_sem=sum_send.at[way, step - 1],
            recv_sem=sum_recv.at[way, step - 1],
            device_id={"tp": tp + 1 if way == 0 else tp - 1},
            device_id_type=MESH,
        )

    def sum_sends(way, step):
        dist = line - step
        return tp + dist < line if way == 0 else tp - dist >= 0

    def sum_first(way):
        return tp == 0 if way == 0 else tp == line - 1

    def sum_arrival(way, step):
        view = land_out.at[way, step - 1]
        return pltpu.make_async_remote_copy(
            src_ref=view, dst_ref=view,
            send_sem=sum_send.at[way, step - 1], recv_sem=sum_recv.at[way, step - 1],
            device_id={"tp": tp - 1 if way == 0 else tp + 1}, device_id_type=MESH)

    def sum_arrives(way, step):
        dist = line - step
        if way == 0:
            return (tp >= 1) & (tp - 1 + dist < line)
        return (tp + 1 < line) & (tp + 1 - dist >= 0)

    def add_body(a_blk, b_blk, o_blk):
        o_blk[...] = low(a_blk[...].astype(jnp.float32) + b_blk[...].astype(jnp.float32))

    add_pipe = pltpu.emit_pipeline(
        add_body, grid=(length // 128,), in_specs=[pl.BlockSpec((128, width), lambda i: (i, 0))] * 2,
        out_specs=[pl.BlockSpec((128, width), lambda i: (i, 0))])

    def start_sum(step):
        for way in range(2):
            dist = line - step
            piece = tp + dist if way == 0 else tp - dist

            @pl.when(sum_sends(way, step) & sum_first(way))
            def _():
                sum_copy(way, step, False).start()

            if step > 1:
                @pl.when(sum_arrives(way, step - 1))
                def _():
                    sum_arrival(way, step - 1).wait_recv()

                @pl.when(sum_sends(way, step) & jnp.logical_not(sum_first(way)))
                def _():
                    add_pipe(
                        part_out.at[rows_of(piece)], land_out.at[way, step - 2],
                        acc_out.at[way, step - 2])
                    sum_copy(way, step, True).start()

    for k in range(line - 1, -1, -1):
        at = rows_of(piece_at(k))
        out_pipe(head_out.at[at], act_out.at[at], part_out.at[at])
        if k == line - 1:
            start_sum(1)

    sfc_ref = b1_ref
    for row in range(1):
        sfc_ref[...] = jnp.zeros_like(sfc_ref)

    def back_body(c_blk, slope_blk, dh_blk, dfc_blk):
        dh_blk[...] = low(dot_nt(c_blk[...], wd_ref[...]))
        step = 512
        for at in range(0, ff, step):
            d = low(dot_nt(c_blk[...], w2_ref[at : at + step, :])
                    * slope_blk[:, at : at + step].astype(jnp.float32))
            dfc_blk[:, at : at + step] = d
            sfc_ref[0:1, at : at + step] += jnp.sum(d.astype(jnp.float32), axis=0, keepdims=True)

    back_pipe = pltpu.emit_pipeline(
        back_body, grid=(length // block,), in_specs=[spec(width), spec(ff)],
        out_specs=[spec(qw), spec(ff)])
    locals_[count + 1].wait()
    ln_ref[...] = jnp.zeros_like(ln_ref)

    def cot_sum_body(c_blk):
        ln_ref[4:5] += jnp.sum(c_blk[...].astype(jnp.float32), axis=0, keepdims=True)

    pltpu.emit_pipeline(
        cot_sum_body, grid=(length // block,), in_specs=[spec(width)], out_specs=[])(cot_ref)
    for k in range(line):
        if 2 <= k < line - 1:
            start_sum(k)
        for hop in range(cot_hop, k):
            step_line(1, hop)
            cot_hop = hop + 1
        at = rows_of(piece_at(k))
        back_pipe(cot_all.at[at], slope_out.at[at], dh_out.at[at], dfc_out.at[at])
    def attend_back(q_buf, o_buf, do_buf, lse_buf, dq_acc, dk_acc, dv_acc, delta, loaded):
        copies = [
            pltpu.make_async_copy(q_out, q_buf, loaded.at[0]),
            pltpu.make_async_copy(head_out, o_buf, loaded.at[1]),
            pltpu.make_async_copy(dh_out, do_buf, loaded.at[2]),
            pltpu.make_async_copy(lse_out, lse_buf, loaded.at[3]),
        ]
        for copy in copies:
            copy.start()
        dq_acc[...] = jnp.zeros_like(dq_acc)
        for copy in copies:
            copy.wait()
        blocks = total_len // qblock
        scale = HD ** -0.5
        for i in range(blocks):
            rows = slice(i * qblock, (i + 1) * qblock)
            for h in range(heads):
                cols = slice(h * HD, (h + 1) * HD)
                inner = jnp.sum(
                    do_buf[rows, cols].astype(jnp.float32) * o_buf[rows, cols].astype(jnp.float32),
                    axis=1, keepdims=True)
                delta[h : h + 1, rows] = jnp.broadcast_to(inner, (qblock, 128)).T[0:1]

        def one(h, i, j, diagonal):
            cols = slice(h * HD, (h + 1) * HD)
            qrows = pl.ds(pl.multiple_of(i * qblock, qblock), qblock)
            krows = pl.ds(pl.multiple_of(j * qblock, qblock), qblock)
            query, grad = q_buf[qrows, cols], do_buf[qrows, cols]
            key, value = k_buf[krows, cols], v_buf[krows, cols]
            s = dot_nt(key, query) * (scale * LOG2E)
            p = jnp.exp2(s - lse_buf[h : h + 1, qrows])
            if diagonal:
                kp = lax.broadcasted_iota(jnp.int32, s.shape, 0)
                qp = lax.broadcasted_iota(jnp.int32, s.shape, 1)
                p = jnp.where(kp <= qp, p, 0.0)
            dp_blk = dot_nt(value, grad)
            ds = low(p * (dp_blk - delta[h : h + 1, qrows]))
            dv = dot_nn(low(p), grad)
            dk = dot_nn(ds, query)
            dq_acc[qrows, cols] += dot_tn(ds, key)
            if diagonal:
                dv_acc[krows, cols] = dv
                dk_acc[krows, cols] = dk
            else:
                dv_acc[krows, cols] += dv
                dk_acc[krows, cols] += dk

        def outer(j, carry):
            for h in range(heads):
                one(h, j, j, True)

            def inner(i, c):
                for h in range(heads):
                    one(h, i, j, False)
                return c

            lax.fori_loop(j + 1, blocks, inner, 0)
            return carry

        middle = blocks // 2
        lax.fori_loop(0, middle, outer, 0)
        start_sum(line - 1)
        lax.fori_loop(middle, blocks, outer, 0)
        sq_ref[...] = jnp.zeros_like(sq_ref)

        def finish_body(cos_blk, sin_blk, out_blk):
            rows = pl.ds(pl.multiple_of(pl.program_id(0) * block, block), block)
            cosine, sine = cos_blk[...], sin_blk[...]
            for which, acc in enumerate((dq_acc, dk_acc, dv_acc)):
                for h in range(heads):
                    at = which * qw + h * HD
                    g = acc[rows, h * HD : (h + 1) * HD]
                    if which < 2:
                        g = g * scale
                        first = g[:, :128]
                        first = first * cosine - turned(first) * sine
                        out_blk[:, at : at + 128] = low(first)
                        out_blk[:, at + 128 : at + HD] = low(g[:, 128:])
                    else:
                        out_blk[:, at : at + HD] = low(g)
                    sq_ref[:, at : at + HD] += jnp.sum(
                        out_blk[:, at : at + HD].astype(jnp.float32), axis=0, keepdims=True)

        pltpu.emit_pipeline(
            finish_body, grid=(total_len // block,), in_specs=[spec(128), spec(128)],
            out_specs=[spec(3 * qw)],
        )(cos_ref, sin_ref, dqkv_out)

    pl.run_scoped(
        attend_back,
        pltpu.VMEM((total_len, qw), jnp.bfloat16),
        pltpu.VMEM((total_len, qw), jnp.bfloat16),
        pltpu.VMEM((total_len, qw), jnp.bfloat16),
        pltpu.VMEM((heads, total_len), jnp.float32),
        pltpu.VMEM((total_len, qw), jnp.float32),
        pltpu.VMEM((total_len, qw), jnp.float32),
        pltpu.VMEM((total_len, qw), jnp.float32),
        pltpu.VMEM((heads, total_len), jnp.float32),
        pltpu.SemaphoreType.DMA((4,)),
    )

    def e_body(dqkv_blk, dfc_blk, x_blk, stat_blk, e_blk):
        mean, rstd = stat_blk[:, 0:1], stat_blk[:, 1:2]
        step = 512
        for at in range(0, width, step):
            cols = slice(at, at + step)
            d1 = dot_nt(dqkv_blk[:, :qw], wq_ref[0, cols, :])
            d1 += dot_nt(dqkv_blk[:, qw : 2 * qw], wq_ref[1, cols, :])
            d1 += dot_nt(dqkv_blk[:, 2 * qw :], wq_ref[2, cols, :])
            d2 = dot_nt(dfc_blk[...], w1_ref[cols, :])
            xhat = (x_blk[:, cols].astype(jnp.float32) - mean) * rstd
            e_blk[:, cols] = low(d1 * kvec[2:3, cols] + d2 * kvec[4:5, cols])
            ln_ref[0:1, cols] += jnp.sum(d1 * xhat, axis=0, keepdims=True)
            ln_ref[1:2, cols] += jnp.sum(d1, axis=0, keepdims=True)
            ln_ref[2:3, cols] += jnp.sum(d2 * xhat, axis=0, keepdims=True)
            ln_ref[3:4, cols] += jnp.sum(d2, axis=0, keepdims=True)

    wspec = lambda n: pl.BlockSpec((wblock, n), lambda i: (i, 0))
    pltpu.emit_pipeline(
        e_body, grid=(total_len // wblock,),
        in_specs=[wspec(3 * qw), wspec(ff), wspec(width), wspec(128)], out_specs=[wspec(width)],
    )(dqkv_out, dfc_out, x_all, stat_out, e_out)
    ends = [
        pltpu.make_async_copy(kvec, vec_out, keep.at[0]),
        pltpu.make_async_copy(sfc_ref, sfc_out, keep.at[1]),
        pltpu.make_async_copy(sq_ref, sq_out, keep.at[2]),
        pltpu.make_async_copy(ln_ref, ln_out, keep.at[3]),
    ]
    for copy in ends:
        copy.start()

    def hidden_body(ways):
        def run(x_blk, part_blk, *blks):
            total = x_blk[...].astype(jnp.float32) + part_blk[...].astype(jnp.float32)
            for blk in blks[:-1]:
                total = total + blk[...].astype(jnp.float32)
            blks[-1][...] = low(total + kvec[0:1] + kvec[1:2])

        pltpu.emit_pipeline(
            run, grid=(length // block,), in_specs=[spec(width)] * (2 + len(ways)),
            out_specs=[spec(width)],
        )(x_ref, part_out.at[rows_of(tp)], *[land_out.at[w, line - 2] for w in ways], hidden_out)

    for way in range(2):
        @pl.when(sum_arrives(way, line - 1))
        def _():
            sum_arrival(way, line - 1).wait_recv()

    @pl.when(tp == 0)
    def _():
        hidden_body([1])

    @pl.when(tp == line - 1)
    def _():
        hidden_body([0])

    @pl.when((tp > 0) & (tp < line - 1))
    def _():
        hidden_body([0, 1])

    for step in range(1, line):
        for way in range(2):
            @pl.when(sum_sends(way, step))
            def _():
                sum_copy(way, step, False).wait_send()

    for a in range(count):
        for slot in range(1 + 2 * hops):
            pair_copy(a, slot).wait_send()
        for hop in range(hops):
            for way in range(2):
                ring_copy(a, way, hop).wait_send()
    for b in range(2):
        for hop in range(line - 1):
            for way in range(2):
                @pl.when(sends(way, hop))
                def _():
                    line_copy(b, way, hop).wait_send()
    for copy in ends:
        copy.wait()


def head(small, wq, w1, wd, w2, x, cot, cosine, sine, n_q, n_b, dp_count, tp_count, collective_id):
    piece, width = x.shape
    length = piece * tp_count
    qw, ff = wd.shape[0], w2.shape[0]
    heads = qw // HD
    chips = dp_count // 2
    hops = chips // 2
    bf, f32 = jnp.bfloat16, jnp.float32
    sds = jax.ShapeDtypeStruct
    steps = max(tp_count - 1, 1)
    out_shape = [
        sds((length, width), bf), sds((length, width), bf),
        sds((length, width), bf), sds((length, width), bf),
        sds((length, qw), bf), sds((length, qw), bf), sds((length, qw), bf),
        sds((length, ff), bf), sds((length, ff), bf), sds((length, 128), f32),
        sds((length, qw), bf), sds((heads, length), f32), sds((length, width), bf),
        sds((length, qw), bf), sds((length, ff), bf),
        sds((2, steps, piece, width), bf), sds((2, steps, piece, width), bf),
        sds((length, 3 * qw), bf), sds((length, width), bf), sds((piece, width), bf),
        sds((8, width), f32), sds((1, ff), f32), sds((1, 3 * qw), f32), sds((8, width), f32),
    ]
    dma = pltpu.SemaphoreType.DMA
    hbm = pl.BlockSpec(memory_space=pl.ANY)
    line = max(tp_count - 1, 1)
    return pl.pallas_call(
        functools.partial(head_kernel, (chips, tp_count, heads, n_q, n_b)),
        out_shape=out_shape,
        in_specs=[hbm] * 9,
        out_specs=[hbm] * len(out_shape),
        scratch_shapes=[
            pltpu.VMEM((small.shape[0] * dp_count, 128), bf),
            pltpu.VMEM((3, width, qw), bf),
            pltpu.VMEM((width, ff), bf),
            pltpu.VMEM((qw, width), bf),
            pltpu.VMEM((ff, width), bf),
            pltpu.VMEM((8, width), f32),
            pltpu.VMEM((1, 3 * qw), f32),
            pltpu.VMEM((1, ff), f32),
            pltpu.VMEM((length, qw), bf),
            pltpu.VMEM((length, qw), bf),
            pltpu.VMEM((1, 3 * qw), f32),
            pltpu.VMEM((8, width), f32),
            dma((5, 2, hops)), dma((5, 2, hops)),
            dma((5, 1 + 2 * hops)), dma((5, 1 + 2 * hops)),
            dma((2, 2, line)), dma((2, 2, line)), dma((7,)),
            dma((2, line)), dma((2, line)), dma((4,)),
        ],
        compiler_params=pltpu.CompilerParams(
            collective_id=collective_id, has_side_effects=True,
            vmem_limit_bytes=62 * 1024 * 1024),
        name="head",
    )(small, wq, w1, wd, w2, x, cot, cosine, sine)


def tail_kernel(cfg, *refs):
    chips, line = cfg
    hops = chips // 2
    refs = list(refs)

    def take(n):
        out, refs[:n] = refs[:n], []
        return out

    act, heads_in, cot, n1, n2, dfc, dqkv, line_ref, flat_ref = take(9)
    own_fc2, own_dense, own_fc1, own_qkv, own_small = take(5)
    held, paired, landed, first_landed = take(4)
    small, s_held, s_paired, s_landed, line_land = take(5)
    (pair_send, pair_recv, ring_send, ring_recv, s_load, s_pair_send, s_pair_recv, s_ring_send,
     s_ring_recv, line_send, line_recv) = refs
    ff, qw = act.shape[1], heads_in.shape[1]
    length = act.shape[0]
    rows = held.shape[1]
    dp = lax.axis_index("dp")
    tp = lax.axis_index("tp")
    core = lax.rem(dp, 2)
    place = ring_place(lax.div(dp, 2), chips)

    def chip_at(ring_pos):
        return ring_place(lax.rem(ring_pos + chips, chips), chips)

    right, left = chip_at(place + 1) * 2 + core, chip_at(place - 1) * 2 + core
    sibling = dp + 1 - 2 * core
    barrier = pltpu.get_barrier_semaphore()
    for partner in (right, left, sibling):
        pl.semaphore_signal(barrier, 1, device_id={"dp": partner}, device_id_type=MESH)
    for n in range(1, line):
        pl.semaphore_signal(
            barrier, 1, device_id={"tp": lax.rem(tp + n, line)}, device_id_type=MESH)
    pl.semaphore_wait(barrier, 3 + line - 1)

    def line_copy(n):
        return pltpu.make_async_remote_copy(
            src_ref=line_ref, dst_ref=line_land.at[n - 1],
            send_sem=line_send.at[n - 1], recv_sem=line_recv.at[n - 1],
            device_id={"tp": lax.rem(tp + n, line)}, device_id_type=MESH)

    for n in range(1, line):
        line_copy(n).start()

    offsets = [hops]
    for near in range(hops - 1, 0, -1):
        offsets += [near, -near]
    offsets.append(0)
    own = chips - 1
    spans = [(0, ff), (ff, qw), (ff + qw, ff), (2 * ff + qw, 3 * qw)]

    def f32(value):
        return value.astype(jnp.float32)

    def over_rows(count, body):
        step = min(count, 32)

        def run(t, carry):
            body(pl.multiple_of(t * step, step), step)
            return carry

        lax.fori_loop(0, count // step, run, 0)

    def pair_arrival(slot, unit):
        at, wide = spans[unit]
        view = paired.at[slot, :, pl.ds(at, wide)]
        return pltpu.make_async_remote_copy(
            src_ref=view, dst_ref=view,
            send_sem=pair_send.at[slot, unit], recv_sem=pair_recv.at[slot, unit],
            device_id={"dp": sibling}, device_id_type=MESH)

    def pair_sum(slot, unit):
        at, wide = spans[unit]
        cols = slice(at, at + wide)
        pair_arrival(slot, unit).wait_recv()

        def body(r, n):
            r = pl.ds(r, n)
            held[slot, r, cols] = low(f32(held[slot, r, cols]) + f32(paired[slot, r, cols]))

        over_rows(rows, body)

    def slot_of(way, step):
        return offsets.index((hops - step) * (1 if way == 0 or step == 0 else -1))

    def ring_rows(way, step):
        return (way * (rows // 2), rows // 2) if step == 0 else (0, rows)

    def ring_copy(way, step, unit):
        at, wide = spans[unit]
        first, n = ring_rows(way, step)
        view = held.at[slot_of(way, step), pl.ds(first, n), pl.ds(at, wide)]
        if step == 0:
            dst = first_landed.at[pl.ds(first, n), pl.ds(at, wide)]
        else:
            dst = landed.at[way, step - 1, :, pl.ds(at, wide)]
        return pltpu.make_async_remote_copy(
            src_ref=view, dst_ref=dst,
            send_sem=ring_send.at[way, step, unit], recv_sem=ring_recv.at[way, step, unit],
            device_id={"dp": right if way == 0 else left}, device_id_type=MESH)

    def add_landed(way, step, unit):
        at, wide = spans[unit]
        cols = slice(at, at + wide)
        slot = slot_of(way, step + 1)
        first, n = ring_rows(way, step)
        ring_copy(way, step, unit).wait_recv()

        def body(r, size):
            r = pl.ds(pl.multiple_of(r + first, 16), size)
            if step == 0:
                moved = first_landed[r, cols]
            else:
                moved = landed[way, step - 1, r, cols]
            held[slot, r, cols] = low(f32(held[slot, r, cols]) + f32(moved))

        over_rows(n, body)

    def ring_after(slot, units):
        for step in range(hops):
            for way in range(2):
                if slot_of(way, step) != slot or slot == own:
                    continue
                for unit in units:
                    if step > 0:
                        add_landed(way, step - 1, unit)
                    ring_copy(way, step, unit).start()

    def compute(big, mid, lhs, turn, out, lhs_sem, big_sem, mid_sem):
        loads = [(cot, 0, slot) for slot in range(chips)]
        loads += [(src, 2, slot) for slot in range(chips) for src in (n2, n1)]

        def lhs_load(i):
            src, _, slot = loads[i]
            chip = chip_at(place + offsets[slot])
            cols = pl.ds(pl.multiple_of(chip * 2 * rows, 128), 2 * rows)
            return pltpu.make_async_copy(src.at[:, cols], lhs.at[i % 2], lhs_sem.at[i % 2])

        phase_loads = (
            (pltpu.make_async_copy(act, big, big_sem.at[0]),
             pltpu.make_async_copy(heads_in, mid.at[:, pl.ds(0, qw)], mid_sem.at[0])),
            (pltpu.make_async_copy(dfc, big, big_sem.at[1]),
             pltpu.make_async_copy(dqkv, mid, mid_sem.at[1])),
        )
        lhs_load(0).start()
        for copy in phase_loads[0]:
            copy.start()
        busy = [None, None]
        counter = 0
        pending = []

        def product(i, slot, unit, rhs):
            nonlocal counter
            at, wide = spans[unit]
            which = counter % 2
            counter += 1
            if busy[which] is not None:
                busy[which].wait_send()
            step = 512 if wide % 512 == 0 else 256
            for col in range(0, wide, step):
                out[which, :, col : col + step] = low(
                    dot_nn(turn[...], rhs[:, col : col + step]))
            mine = pl.ds(pl.multiple_of(core * rows, 16), rows)
            held[slot, :, at : at + wide] = out[which, mine, :wide]
            theirs = pl.ds(pl.multiple_of((1 - core) * rows, 16), rows)
            copy = pltpu.make_async_remote_copy(
                src_ref=out.at[which, theirs, pl.ds(0, wide)],
                dst_ref=paired.at[slot, :, pl.ds(at, wide)],
                send_sem=pair_send.at[slot, unit], recv_sem=pair_recv.at[slot, unit],
                device_id={"dp": sibling}, device_id_type=MESH)
            copy.start()
            busy[which] = copy
            while pending:
                pair_sum(*pending.pop(0))
            pending.append((slot, unit))

        def settle():
            while pending:
                pair_sum(*pending.pop(0))

        def left_side(i):
            lhs_load(i).wait()
            if i + 1 < len(loads):
                lhs_load(i + 1).start()
            turn[...] = lhs[i % 2].T

        for phase in range(2):
            units = (0, 1) if phase == 0 else (2, 3)
            for slot in range(chips):
                if phase == 0:
                    left_side(slot)
                    if slot == 0:
                        for copy in phase_loads[0]:
                            copy.wait()
                    product(slot, slot, 0, big)
                    product(slot, slot, 1, mid)
                else:
                    i = chips + 2 * slot
                    left_side(i)
                    if slot == 0:
                        phase_loads[1][0].wait()
                    product(i, slot, 2, big)
                    left_side(i + 1)
                    if slot == 0:
                        phase_loads[1][1].wait()
                    product(i + 1, slot, 3, mid)
                if slot == 0:
                    settle()
                    ring_after(0, units)
                elif slot == chips - 2:
                    settle()
                    for ready in range(1, chips - 1):
                        ring_after(ready, units)
            if phase == 0:
                for copy in phase_loads[1]:
                    copy.start()
        settle()
        for copy in busy:
            copy.wait_send()

    pl.run_scoped(
        compute,
        pltpu.VMEM((length, ff), jnp.bfloat16),
        pltpu.VMEM((length, 3 * qw), jnp.bfloat16),
        pltpu.VMEM((2, length, 2 * rows), jnp.bfloat16),
        pltpu.VMEM((2 * rows, length), jnp.bfloat16),
        pltpu.VMEM((2, 2 * rows, max(ff, 3 * qw)), jnp.bfloat16),
        pltpu.SemaphoreType.DMA((2,)),
        pltpu.SemaphoreType.DMA((2,)),
        pltpu.SemaphoreType.DMA((2,)),
    )

    for n in range(1, line):
        line_copy(n).wait_recv()
    total = line_ref[...]
    for n in range(1, line):
        total = total + line_land[n - 1]
    rows_z = line_ref.shape[1]
    small[:, :rows_z] = total
    small[:, rows_z:] = flat_ref[...]
    s_rows = small.shape[1]

    def s_pair(slot):
        chip = chip_at(place + offsets[slot])
        return pltpu.make_async_remote_copy(
            src_ref=small.at[chip * 2 + 1 - core], dst_ref=s_paired.at[slot],
            send_sem=s_pair_send.at[slot], recv_sem=s_pair_recv.at[slot],
            device_id={"dp": sibling}, device_id_type=MESH)

    def s_keep(slot):
        chip = chip_at(place + offsets[slot])
        return pltpu.make_async_copy(small.at[chip * 2 + core], s_held.at[slot], s_load.at[slot])

    def s_ring(way, step):
        n = s_rows // 2 if step == 0 else s_rows
        first = way * n if step == 0 else 0
        return pltpu.make_async_remote_copy(
            src_ref=s_held.at[slot_of(way, step), pl.ds(first, n)],
            dst_ref=s_landed.at[way, step, pl.ds(first, n)],
            send_sem=s_ring_send.at[way, step], recv_sem=s_ring_recv.at[way, step],
            device_id={"dp": right if way == 0 else left}, device_id_type=MESH)

    for slot in range(chips):
        s_keep(slot).start()
        s_pair(slot).start()
    for slot in range(chips):
        s_keep(slot).wait()
        s_pair(slot).wait_recv()
        s_held[slot] += s_paired[slot]
        for step in range(hops):
            for way in range(2):
                if slot_of(way, step) != slot or slot == own:
                    continue
                if step > 0:
                    n = s_rows // 2 if step == 1 else s_rows
                    first = way * n if step == 1 else 0
                    s_ring(way, step - 1).wait_recv()
                    s_held[slot, first : first + n] += s_landed[way, step - 1, first : first + n]
                s_ring(way, step).start()
    for way in range(2):
        s_ring(way, hops - 1).wait_recv()
    own_small[...] = s_held[own] + s_landed[0, hops - 1] + s_landed[1, hops - 1]

    def finish(wide_buf, tall_buf, done):
        targets = [
            (0, [own_fc2]), (1, [own_dense]), (2, [own_fc1]),
            (3, [own_qkv.at[w] for w in range(3)]),
        ]
        last = {}

        def total_at(unit, at, size):
            cols = slice(at, at + size)
            value = f32(held[own, :, cols])
            if hops == 1:
                return value + f32(first_landed[:, cols])
            return value + f32(landed[0, hops - 2, :, cols]) + f32(landed[1, hops - 2, :, cols])

        for unit, outs in targets:
            at, wide = spans[unit]
            for way in range(2):
                ring_copy(way, hops - 1, unit).wait_recv()
            if unit < 2:
                if "tall" in last:
                    last["tall"].wait()
                for col in range(0, wide, 256):
                    tall_buf[col : col + 256, :] = total_at(unit, at + col, 256).T
                copy = pltpu.make_async_copy(tall_buf.at[pl.ds(0, wide)], outs[0], done.at[0])
                copy.start()
                last["tall"] = copy
            else:
                if "wide" in last:
                    for copy in last["wide"]:
                        copy.wait()
                for col in range(0, wide, 256):
                    wide_buf[:, col : col + 256] = total_at(unit, at + col, 256)
                each = wide // len(outs)
                copies = [
                    pltpu.make_async_copy(
                        wide_buf.at[:, pl.ds(w * each, each)], out, done.at[1 + w])
                    for w, out in enumerate(outs)
                ]
                for copy in copies:
                    copy.start()
                last["wide"] = copies
        last["tall"].wait()
        for copy in last["wide"]:
            copy.wait()

    pl.run_scoped(
        finish,
        pltpu.VMEM((rows, max(ff, 3 * qw)), jnp.float32),
        pltpu.VMEM((max(ff, qw), rows), jnp.float32),
        pltpu.SemaphoreType.DMA((4,)),
    )
    for way in range(2):
        for step in range(hops):
            for unit in range(4):
                ring_copy(way, step, unit).wait_send()
            s_ring(way, step).wait_send()
    for slot in range(chips):
        s_pair(slot).wait_send()
    for n in range(1, line):
        line_copy(n).wait_send()


def tail(act, heads_in, cot, n1, n2, dfc, dqkv, line_sums, flat_sums, dp_count, tp_count, collective_id):
    chips = dp_count // 2
    hops = chips // 2
    length, ff = act.shape
    qw = heads_in.shape[1]
    rows = cot.shape[1] // dp_count
    cols = 2 * ff + 4 * qw
    rows_s = line_sums.shape[1] + flat_sums.shape[1]
    bf, f32 = jnp.bfloat16, jnp.float32
    dma = pltpu.SemaphoreType.DMA
    hbm = pl.BlockSpec(memory_space=pl.ANY)
    vm = pl.BlockSpec(memory_space=pltpu.VMEM)
    line = max(tp_count - 1, 1)
    sds = jax.ShapeDtypeStruct
    return pl.pallas_call(
        functools.partial(tail_kernel, (chips, tp_count)),
        out_shape=[
            sds((ff, rows), f32), sds((qw, rows), f32), sds((rows, ff), f32),
            sds((3, rows, qw), f32), sds((rows_s, 128), f32),
        ],
        in_specs=[hbm] * 7 + [vm, vm],
        out_specs=[hbm] * 4 + [vm],
        scratch_shapes=[
            pltpu.VMEM((chips, rows, cols), bf),
            pltpu.VMEM((chips, rows, cols), bf),
            pltpu.VMEM((2, max(hops - 1, 1), rows, cols), bf),
            pltpu.VMEM((rows, cols), bf),
            pltpu.VMEM((dp_count, rows_s, 128), f32),
            pltpu.VMEM((chips, rows_s, 128), f32),
            pltpu.VMEM((chips, rows_s, 128), f32),
            pltpu.VMEM((2, hops, rows_s, 128), f32),
            pltpu.VMEM((line,) + line_sums.shape, f32),
            dma((chips, 4)), dma((chips, 4)), dma((2, hops, 4)), dma((2, hops, 4)),
            dma((chips,)), dma((chips,)), dma((chips,)), dma((2, hops)), dma((2, hops)),
            dma((line,)), dma((line,)),
        ],
        compiler_params=pltpu.CompilerParams(
            collective_id=collective_id, has_side_effects=True,
            vmem_limit_bytes=62 * 1024 * 1024),
        cost_estimate=pl.CostEstimate(
            flops=2 * length * cot.shape[1] * cols, bytes_accessed=400_000_000, transcendentals=0),
        name="tail",
    )(act, heads_in, cot, n1, n2, dfc, dqkv, line_sums, flat_sums)


def pack_small(wide, narrow):
    rows = []
    first = jnp.concatenate([part.reshape(-1, 128) for part in wide], axis=0)
    rows.append(jnp.pad(first, ((0, 16 - first.shape[0]), (0, 0))))
    count = 0
    for part in narrow:
        flat = part.reshape(-1)
        need = -(-flat.size // 128)
        rows.append(jnp.pad(flat, (0, need * 128 - flat.size)).reshape(need, 128))
        count += need
    rows.append(jnp.zeros((16 - count, 128), jnp.bfloat16))
    return jnp.concatenate(rows, axis=0)


def by_owner(rows, dp_count):
    count = -(-rows.shape[1] // 2048) * 16
    padded = jnp.pad(rows, ((0, 0), (0, count * 128 - rows.shape[1])))
    return padded.reshape(dp_count, count, 128)


def body(
    hidden_in,
    triple_projection_weight,
    triple_projection_bias,
    attention_out_weight,
    b_dense,
    feedforward_in_weight,
    feedforward_in_bias,
    feedforward_out_weight,
    b_fc2,
    ln1_gain,
    ln1_bias,
    ln2_gain,
    ln2_bias,
    grad_out,
):
    _, piece_len, width = hidden_in.shape
    tp_count = lax.axis_size("tp")
    dp_count = lax.axis_size("dp")
    length = piece_len * tp_count
    cosine, sine = rotary_tables(length)
    small = pack_small(
        [b_dense, b_fc2, ln1_gain, ln1_bias, ln2_gain, ln2_bias],
        [triple_projection_bias, feedforward_in_bias],
    )
    n_q = -(-triple_projection_bias.size // 128)
    n_b = -(-feedforward_in_bias.size // 128)
    outs = head(
        small,
        triple_projection_weight.transpose(1, 0, 2),
        feedforward_in_weight,
        attention_out_weight,
        feedforward_out_weight,
        hidden_in[0],
        grad_out[0],
        cosine,
        sine,
        n_q,
        n_b,
        dp_count,
        tp_count,
        0,
    )
    _, cot_seq, norm_one, norm_two = outs[:4]
    act, head_out, d_fc = outs[7], outs[10], outs[14]
    d_qkv, e_sum, hidden_out, vectors, sum_bfc1, sum_bqkv, ln_sums = outs[17:]
    e_piece = lax.psum_scatter(e_sum, "tp", scatter_dimension=0, tiled=True).astype(jnp.float32)

    cot_piece = grad_out[0].astype(jnp.float32)
    line_sums = ln_sums[:5].reshape(5, dp_count, -1).transpose(1, 0, 2).reshape(dp_count, -1)
    flat_sums = jnp.concatenate([sum_bqkv, sum_bfc1], axis=1).reshape(-1, dp_count).T
    line_rows, flat_rows = by_owner(line_sums, dp_count), by_owner(flat_sums, dp_count)
    own_fc2, own_dense, own_fc1, own_qkv, own_small = tail(
        act, head_out, cot_seq, norm_one, norm_two, d_fc, d_qkv, line_rows, flat_rows,
        dp_count, tp_count, 1,
    )
    e_piece, own_small = lax.optimization_barrier((e_piece, own_small))
    own_line = own_small[: line_rows.shape[1]].reshape(-1)[: line_sums.shape[1]].reshape(5, -1)
    own_flat = own_small[line_rows.shape[1] :].reshape(-1)[: flat_sums.shape[1]]
    split = sum_bqkv.size // dp_count

    x_own = hidden_in[0].astype(jnp.float32)
    mean = jnp.mean(x_own, axis=-1, keepdims=True)
    centered = x_own - mean
    rstd = lax.rsqrt(jnp.mean(centered * centered, axis=-1, keepdims=True) + EPSILON)
    xhat = centered * rstd
    back = (
        e_piece
        - jnp.mean(e_piece, axis=-1, keepdims=True)
        - xhat * jnp.mean(e_piece * xhat, axis=-1, keepdims=True)
    ) * rstd
    grad_in = (cot_piece + back)[None]
    return (
        hidden_out[None],
        grad_in,
        own_qkv.transpose(1, 0, 2),
        own_flat[:split].reshape(triple_projection_bias.shape),
        own_dense,
        own_line[4],
        own_fc1,
        own_flat[split:].reshape(feedforward_in_bias.shape),
        own_fc2,
        own_line[4],
        own_line[0],
        own_line[1],
        own_line[2],
        own_line[3],
    )


def solution(mesh):
    return jax.shard_map(
        body,
        mesh=mesh,
        in_specs=(
            P("dp", "tp", None),
            P("dp", None, "tp"),
            P(None, "tp", "dp"),
            P("tp", "dp"),
            P("dp"),
            P("dp", "tp"),
            P("tp", "dp"),
            P("tp", "dp"),
            P("dp"),
            P("dp"),
            P("dp"),
            P("dp"),
            P("dp"),
            P("dp", "tp", None),
        ),
        out_specs=(
            P("dp", "tp", None),
            P("dp", "tp", None),
            P("dp", None, "tp"),
            P(None, "tp", "dp"),
            P("tp", "dp"),
            P("dp"),
            P("dp", "tp"),
            P("tp", "dp"),
            P("tp", "dp"),
            P("dp"),
            P("dp"),
            P("dp"),
            P("dp"),
            P("dp"),
        ),
        check_vma=False,
    )
```

```python
import functools
import math

import jax
import jax.numpy as jnp
import numpy as np
from jax import lax
from jax.experimental import pallas as pl
from jax.experimental.pallas import tpu as pltpu
from jax.sharding import PartitionSpec as P

MESH = pl.DeviceIdType.MESH
EPSILON = 1e-05
MASKED = -1e30
HD = 256
ROT = 64
VMEM_LIMIT = 60 * 1024 * 1024
LOG2E = 1.4426950408889634


def low(value):
    return value.astype(jnp.bfloat16)


def dot_nn(a, b):
    return lax.dot_general(a, b, (((1,), (0,)), ((), ())), preferred_element_type=jnp.float32)


def dot_nt(a, b):
    return lax.dot_general(a, b, (((1,), (1,)), ((), ())), preferred_element_type=jnp.float32)


def dot_tn(a, b):
    return lax.dot_general(a, b, (((0,), (0,)), ((), ())), preferred_element_type=jnp.float32)


def rotary_tables(length):
    half = ROT // 2
    exponent = np.arange(half, dtype=np.float32) * np.float32(2.0 / ROT)
    inverse = np.exp(exponent * np.float32(-math.log(10000.0)), dtype=np.float32)
    angle = np.arange(length, dtype=np.float32)[:, None] * inverse[None, :]
    cosine = np.ones((length, 128), np.float32)
    sine = np.zeros((length, 128), np.float32)
    cosine[:, :half] = cosine[:, half:ROT] = np.cos(angle)
    sine[:, :half] = -np.sin(angle)
    sine[:, half:ROT] = np.sin(angle)
    return jnp.asarray(cosine), jnp.asarray(sine)


def turned(part):
    half = ROT // 2
    lane = lax.broadcasted_iota(jnp.int32, part.shape, 1)
    return jnp.where(
        lane < half, pltpu.roll(part, 128 - half, 1), pltpu.roll(part, half, 1)
    )


def ring_place(chip, chips):
    half = chips // 2
    return jnp.where(chip < half, chip, 3 * half - 1 - chip)


def shard_view(ref, kind, owner, part, extent):
    axis = 1 if kind == "mid" else 0
    rows = extent[axis]
    first, size = (0, rows) if part == 0 else ((part - 1) * (rows // 2), rows // 2)
    if kind == "row":
        return ref.at[pl.ds(owner * rows + first, size)]
    if kind == "mid":
        return ref.at[:, pl.ds(owner * rows + first, size)]
    return ref.at[pl.ds(first, size), pl.ds(owner * extent[1], extent[1])]


def own_view(ref, kind, part, extent):
    if part == 0:
        return ref
    axis = 1 if kind == "mid" else 0
    half = extent[axis] // 2
    at = pl.ds((part - 1) * half, half)
    return ref.at[:, at] if kind == "mid" else ref.at[at]


def picked(tp, values):
    out = values[0]
    for i in range(1, len(values)):
        out = jnp.where(tp == i, values[i], out)
    return out


def order_of(line):
    return [sorted(range(line), key=lambda p: (abs(p - z), p)) for z in range(line)]


def head_kernel(cfg, *refs):
    chips, line, heads, n_q, n_b = cfg
    hops = chips // 2
    refs = list(refs)

    def take(n):
        out, refs[:n] = refs[:n], []
        return out

    shards = take(5)
    x_ref, cot_ref, cos_ref, sin_ref = take(4)
    (x_all, cot_all, n1_out, n2_out, q_out, k_out, v_out, act_out, slope_out,
     stat_out, head_out, lse_out, part_out, dh_out, dfc_out, land_out, acc_out, dqkv_out, e_out,
     hidden_out, vec_out, sfc_out, sq_out, ln_out) = take(24)
    fulls = take(5)
    small_ref, wq_ref, w1_ref, wd_ref, w2_ref = fulls
    kvec, bq_ref, b1_ref, k_buf, v_buf, sq_ref, ln_ref = take(7)
    (ring_send, ring_recv, pair_send, pair_recv, line_send, line_recv, local,
     sum_send, sum_recv, keep) = refs
    kinds = ["row", "mid", "row", "col", "col"]
    extents = [s.shape for s in shards]
    count = 5
    dp = lax.axis_index("dp")
    tp = lax.axis_index("tp")
    dp_count = 2 * chips
    core = lax.rem(dp, 2)
    place = ring_place(lax.div(dp, 2), chips)
    length = x_ref.shape[0]
    total_len = length * line
    width = x_ref.shape[1]

    def device(ring_pos):
        return ring_place(lax.rem(ring_pos + chips, chips), chips) * 2 + core

    right, left = device(place + 1), device(place - 1)
    sibling = dp + 1 - 2 * core
    barrier = pltpu.get_barrier_semaphore()
    for partner in (right, left, sibling):
        pl.semaphore_signal(barrier, 1, device_id={"dp": partner}, device_id_type=MESH)

    @pl.when(tp > 0)
    def _():
        pl.semaphore_signal(barrier, 1, device_id={"tp": tp - 1}, device_id_type=MESH)

    @pl.when(tp < line - 1)
    def _():
        pl.semaphore_signal(barrier, 1, device_id={"tp": tp + 1}, device_id_type=MESH)

    pl.semaphore_wait(barrier, 3 + jnp.where(tp > 0, 1, 0) + jnp.where(tp < line - 1, 1, 0))

    def ring_copy(a, way, hop, arriving=False):
        back = hop + 1 if arriving else hop
        owner = device(place - back) if way == 0 else device(place + back)
        part = 0 if hop < hops - 1 else 1 + way
        view = shard_view(fulls[a], kinds[a], owner, part, extents[a])
        own = hop == 0 and not arriving
        return pltpu.make_async_remote_copy(
            src_ref=own_view(shards[a], kinds[a], part, extents[a]) if own else view,
            dst_ref=view,
            send_sem=ring_send.at[a, way, hop],
            recv_sem=ring_recv.at[a, way, hop],
            device_id={"dp": right if way == 0 else left},
            device_id_type=MESH,
        )

    def pair_copy(a, slot, arriving=False):
        if slot == 0:
            owner, part = dp, 0
        else:
            hop, way = divmod(slot - 1, 2)
            owner = device(place - 1 - hop) if way == 0 else device(place + 1 + hop)
            part = 0 if hop < hops - 1 else 1 + way
        if arriving:
            owner = owner + 1 - 2 * core
        view = shard_view(fulls[a], kinds[a], owner, part, extents[a])
        return pltpu.make_async_remote_copy(
            src_ref=shards[a] if slot == 0 and not arriving else view,
            dst_ref=view,
            send_sem=pair_send.at[a, slot],
            recv_sem=pair_recv.at[a, slot],
            device_id={"dp": sibling},
            device_id_type=MESH,
        )

    def rows_of(piece):
        return pl.ds(pl.multiple_of(piece * length, length), length)

    def line_copy(b, way, hop, arriving=False):
        back = hop + 1 if arriving else hop
        piece = tp - back if way == 0 else tp + back
        view = (x_all, cot_all)[b].at[rows_of(piece)]
        to = tp + 1 if way == 0 else tp - 1
        if arriving:
            to = tp - 1 if way == 0 else tp + 1
        return pltpu.make_async_remote_copy(
            src_ref=(x_ref, cot_ref)[b] if hop == 0 and not arriving else view,
            dst_ref=view,
            send_sem=line_send.at[b, way, hop],
            recv_sem=line_recv.at[b, way, hop],
            device_id={"tp": to},
            device_id_type=MESH,
        )

    def sends(way, hop):
        return (tp < line - 1) & (tp >= hop) if way == 0 else (tp > 0) & (tp + hop < line)

    def arrives(way, hop):
        return tp - 1 - hop >= 0 if way == 0 else tp + 1 + hop < line

    def start_line(b, hop):
        for way in range(2):
            @pl.when(sends(way, hop))
            def _():
                line_copy(b, way, hop).start()

    def step_line(b, hop):
        for way in range(2):
            @pl.when(arrives(way, hop))
            def _():
                line_copy(b, way, hop, True).wait_recv()

            if hop + 1 < line - 1:
                @pl.when(sends(way, hop + 1))
                def _():
                    line_copy(b, way, hop + 1).start()

    early, late = range(3), range(3, count)
    locals_ = [
        pltpu.make_async_copy(
            shards[a], shard_view(fulls[a], kinds[a], dp, 0, extents[a]), local.at[a])
        for a in range(count)
    ]
    locals_.append(pltpu.make_async_copy(x_ref, x_all.at[rows_of(tp)], local.at[count]))
    locals_.append(pltpu.make_async_copy(cot_ref, cot_all.at[rows_of(tp)], local.at[count + 1]))

    def start_ring(group):
        for a in group:
            for way in range(2):
                ring_copy(a, way, 0).start()
            pair_copy(a, 0).start()

    def step_ring(group, hop):
        for a in group:
            for way in range(2):
                ring_copy(a, way, hop, True).wait_recv()
                if hop + 1 < hops:
                    ring_copy(a, way, hop + 1).start()
                pair_copy(a, 1 + 2 * hop + way).start()

    def end_ring(group):
        for a in group:
            locals_[a].wait()
            for slot in range(1 + 2 * hops):
                pair_copy(a, slot, True).wait_recv()

    start_line(0, 0)
    start_ring(early)
    for copy in locals_:
        copy.start()
    step_ring(early, 0)
    start_ring(late)
    step_line(0, 0)
    for hop in range(1, hops):
        step_ring(early, hop)
    end_ring(early)

    small_rows = extents[0][0]
    per = width // dp_count // 128
    for d in range(dp_count):
        block = small_ref[d * small_rows : (d + 1) * small_rows].astype(jnp.float32)
        for vec in range(6):
            for r in range(per):
                at = (d * per + r) * 128
                row = vec * per + r
                kvec[vec : vec + 1, at : at + 128] = block[row : row + 1]
    span = 128 * dp_count
    lane = lax.broadcasted_iota(jnp.int32, (128, span), 0)
    col = lax.broadcasted_iota(jnp.int32, (128, span), 1)
    mixed = jnp.zeros((16, span), jnp.float32)
    for d in range(dp_count):
        hot = jnp.where(col == lane * dp_count + d, 1.0, 0.0).astype(jnp.bfloat16)
        mixed += dot_nn(small_ref[d * small_rows + 16 : d * small_rows + 32], hot)
    for ref, first, n in ((bq_ref, 0, n_q), (b1_ref, n_q, n_b)):
        for r in range(n):
            wide = min(span, ref.shape[1] - r * span)
            ref[0:1, r * span : r * span + wide] = mixed[first + r : first + r + 1, :wide]

    def front_body(x_blk, cos_blk, sin_blk, n1, n2, q, k, v, act, slope, stat):
        x = x_blk[...].astype(jnp.float32)
        mean = jnp.mean(x, axis=1, keepdims=True)
        centered = x - mean
        rstd = lax.rsqrt(jnp.mean(centered * centered, axis=1, keepdims=True) + EPSILON)
        xhat = centered * rstd
        n1[...] = low(xhat * kvec[2:3] + kvec[3:4])
        n2[...] = low(xhat * kvec[4:5] + kvec[5:6])
        lanes = lax.broadcasted_iota(jnp.int32, stat.shape, 1)
        stat[...] = jnp.where(lanes == 0, mean, rstd)
        cosine, sine = cos_blk[...], sin_blk[...]
        qw = heads * HD
        for which, out in enumerate((q, k, v)):
            for head in range(heads):
                cols = slice(head * HD, (head + 1) * HD)
                bias = slice(which * qw + head * HD, which * qw + (head + 1) * HD)
                raw = dot_nn(n1[...], wq_ref[which, :, cols]) + bq_ref[:, bias]
                if which < 2:
                    first = raw[:, :128]
                    first = first * cosine + turned(first) * sine
                    out[:, head * HD : head * HD + 128] = low(first)
                    out[:, head * HD + 128 : (head + 1) * HD] = low(raw[:, 128:])
                else:
                    out[:, cols] = low(raw)
        step = 256
        for at in range(0, w1_ref.shape[1], step):
            u = dot_nn(n2[...], w1_ref[:, at : at + step]) + b1_ref[:, at : at + step]
            cdf = 0.5 * (1.0 + lax.erf(u * (1.0 / math.sqrt(2.0))))
            pdf = jnp.exp(-0.5 * u * u) * (1.0 / math.sqrt(2.0 * math.pi))
            act[:, at : at + step] = low(u * cdf)
            slope[:, at : at + step] = low(cdf + u * pdf)

    block = min(256, length)
    wblock = min(512, length)

    def spec(n):
        return pl.BlockSpec((block, n), lambda i: (i, 0))

    qw, ff = heads * HD, w1_ref.shape[1]
    front_outs = (n1_out, n2_out, q_out, k_out, v_out, act_out, slope_out, stat_out)
    front_pipe = pltpu.emit_pipeline(
        front_body,
        grid=(length // block,),
        in_specs=[spec(width), spec(128), spec(128)],
        out_specs=[spec(ref.shape[1]) for ref in front_outs],
    )
    table = order_of(line)

    def piece_at(k):
        return picked(tp, [table[z][k] for z in range(line)])

    locals_[count].wait()
    for k in range(line):
        if k == 1:
            step_ring(late, 0)
        if k == line - 1:
            for hop in range(1, hops):
                step_ring(late, hop)
        if k > 1:
            step_line(0, k - 1)
        if k == line - 1:
            start_line(1, 0)
        at = rows_of(piece_at(k))
        front_pipe(
            x_all.at[at], cos_ref.at[at], sin_ref.at[at], *[ref.at[at] for ref in front_outs])

    end_ring(late)

    kv_copies = [
        pltpu.make_async_copy(k_out, k_buf, local.at[0]),
        pltpu.make_async_copy(v_out, v_buf, local.at[1]),
    ]
    for copy in kv_copies:
        copy.start()
    for copy in kv_copies:
        copy.wait()
    qblock = min(512, total_len)
    scale = LOG2E * HD ** -0.5

    def attend_body(q_blk, o_blk, lse_blk):
        i = pl.program_id(0)
        qs = [q_blk[:, h * HD : (h + 1) * HD] for h in range(heads)]

        def one(h, j, state, diagonal):
            top, total, acc = state
            rows = pl.ds(pl.multiple_of(j * qblock, qblock), qblock)
            key = k_buf[rows, h * HD : (h + 1) * HD]
            value = v_buf[rows, h * HD : (h + 1) * HD]
            s = dot_nt(key, qs[h]) * scale
            if diagonal:
                kp = lax.broadcasted_iota(jnp.int32, s.shape, 0)
                qp = lax.broadcasted_iota(jnp.int32, s.shape, 1)
                s = jnp.where(kp <= qp, s, MASKED)
            new_top = jnp.maximum(top, jnp.max(s, axis=0, keepdims=True))
            p = jnp.exp2(s - new_top)
            shrink = jnp.exp2(top - new_top)
            total = total * shrink + jnp.sum(p, axis=0, keepdims=True)
            acc = acc * shrink + dot_tn(value, low(p))
            return new_top, total, acc

        def start():
            return (
                jnp.full((1, qblock), MASKED, jnp.float32),
                jnp.zeros((1, qblock), jnp.float32),
                jnp.zeros((HD, qblock), jnp.float32),
            )

        def step(j, states):
            return tuple(one(h, j, states[h], False) for h in range(heads))

        states = lax.fori_loop(0, i, step, tuple(start() for _ in range(heads)))
        states = [one(h, i, states[h], True) for h in range(heads)]
        for h in range(heads):
            top, total, acc = states[h]
            o_blk[:, h * HD : (h + 1) * HD] = low((acc / total).T)
            lse_blk[h : h + 1, :] = top + jnp.log2(total)

    pltpu.emit_pipeline(
        attend_body,
        grid=(total_len // qblock,),
        in_specs=[pl.BlockSpec((qblock, qw), lambda i: (i, 0))],
        out_specs=[
            pl.BlockSpec((qblock, qw), lambda i: (i, 0)),
            pl.BlockSpec((heads, qblock), lambda i: (0, i)),
        ],
    )(q_out, head_out, lse_out)
    step_line(1, 0)
    cot_hop = 1

    def out_body(h_blk, a_blk, o_blk):
        step = 512
        for at in range(0, o_blk.shape[1], step):
            o_blk[:, at : at + step] = low(
                dot_nn(h_blk[...], wd_ref[:, at : at + step])
                + dot_nn(a_blk[...], w2_ref[:, at : at + step]))

    out_pipe = pltpu.emit_pipeline(
        out_body, grid=(length // block,), in_specs=[spec(qw), spec(ff)], out_specs=[spec(width)])

    def sum_copy(way, step, from_acc):
        dist = line - step
        piece = tp + dist if way == 0 else tp - dist
        src = acc_out.at[way, step - 2] if from_acc else part_out.at[rows_of(piece)]
        return pltpu.make_async_remote_copy(
            src_ref=src,
            dst_ref=land_out.at[way, step - 1],
            send_sem=sum_send.at[way, step - 1],
            recv_sem=sum_recv.at[way, step - 1],
            device_id={"tp": tp + 1 if way == 0 else tp - 1},
            device_id_type=MESH,
        )

    def sum_sends(way, step):
        dist = line - step
        return tp + dist < line if way == 0 else tp - dist >= 0

    def sum_first(way):
        return tp == 0 if way == 0 else tp == line - 1

    def sum_arrival(way, step):
        view = land_out.at[way, step - 1]
        return pltpu.make_async_remote_copy(
            src_ref=view, dst_ref=view,
            send_sem=sum_send.at[way, step - 1], recv_sem=sum_recv.at[way, step - 1],
            device_id={"tp": tp - 1 if way == 0 else tp + 1}, device_id_type=MESH)

    def sum_arrives(way, step):
        dist = line - step
        if way == 0:
            return (tp >= 1) & (tp - 1 + dist < line)
        return (tp + 1 < line) & (tp + 1 - dist >= 0)

    def add_body(a_blk, b_blk, o_blk):
        o_blk[...] = low(a_blk[...].astype(jnp.float32) + b_blk[...].astype(jnp.float32))

    add_pipe = pltpu.emit_pipeline(
        add_body, grid=(length // 128,), in_specs=[pl.BlockSpec((128, width), lambda i: (i, 0))] * 2,
        out_specs=[pl.BlockSpec((128, width), lambda i: (i, 0))])

    def start_sum(step):
        for way in range(2):
            dist = line - step
            piece = tp + dist if way == 0 else tp - dist

            @pl.when(sum_sends(way, step) & sum_first(way))
            def _():
                sum_copy(way, step, False).start()

            if step > 1:
                @pl.when(sum_arrives(way, step - 1))
                def _():
                    sum_arrival(way, step - 1).wait_recv()

                @pl.when(sum_sends(way, step) & jnp.logical_not(sum_first(way)))
                def _():
                    add_pipe(
                        part_out.at[rows_of(piece)], land_out.at[way, step - 2],
                        acc_out.at[way, step - 2])
                    sum_copy(way, step, True).start()

    for k in range(line - 1, -1, -1):
        at = rows_of(piece_at(k))
        out_pipe(head_out.at[at], act_out.at[at], part_out.at[at])
        if k == line - 1:
            start_sum(1)

    sfc_ref = b1_ref
    for row in range(1):
        sfc_ref[...] = jnp.zeros_like(sfc_ref)

    def back_body(c_blk, slope_blk, dh_blk, dfc_blk):
        dh_blk[...] = low(dot_nt(c_blk[...], wd_ref[...]))
        step = 512
        for at in range(0, ff, step):
            d = low(dot_nt(c_blk[...], w2_ref[at : at + step, :])
                    * slope_blk[:, at : at + step].astype(jnp.float32))
            dfc_blk[:, at : at + step] = d
            sfc_ref[0:1, at : at + step] += jnp.sum(d.astype(jnp.float32), axis=0, keepdims=True)

    back_pipe = pltpu.emit_pipeline(
        back_body, grid=(length // block,), in_specs=[spec(width), spec(ff)],
        out_specs=[spec(qw), spec(ff)])
    locals_[count + 1].wait()
    ln_ref[...] = jnp.zeros_like(ln_ref)

    def cot_sum_body(c_blk):
        ln_ref[4:5] += jnp.sum(c_blk[...].astype(jnp.float32), axis=0, keepdims=True)

    pltpu.emit_pipeline(
        cot_sum_body, grid=(length // block,), in_specs=[spec(width)], out_specs=[])(cot_ref)
    for k in range(line):
        if 2 <= k < line - 1:
            start_sum(k)
        for hop in range(cot_hop, k):
            step_line(1, hop)
            cot_hop = hop + 1
        at = rows_of(piece_at(k))
        back_pipe(cot_all.at[at], slope_out.at[at], dh_out.at[at], dfc_out.at[at])
    def attend_back(q_buf, o_buf, do_buf, lse_buf, dq_acc, dk_acc, dv_acc, delta, loaded):
        copies = [
            pltpu.make_async_copy(q_out, q_buf, loaded.at[0]),
            pltpu.make_async_copy(head_out, o_buf, loaded.at[1]),
            pltpu.make_async_copy(dh_out, do_buf, loaded.at[2]),
            pltpu.make_async_copy(lse_out, lse_buf, loaded.at[3]),
        ]
        for copy in copies:
            copy.start()
        dq_acc[...] = jnp.zeros_like(dq_acc)
        for copy in copies:
            copy.wait()
        blocks = total_len // qblock
        scale = HD ** -0.5
        for i in range(blocks):
            rows = slice(i * qblock, (i + 1) * qblock)
            for h in range(heads):
                cols = slice(h * HD, (h + 1) * HD)
                inner = jnp.sum(
                    do_buf[rows, cols].astype(jnp.float32) * o_buf[rows, cols].astype(jnp.float32),
                    axis=1, keepdims=True)
                delta[h : h + 1, rows] = jnp.broadcast_to(inner, (qblock, 128)).T[0:1]

        def one(h, i, j, diagonal):
            cols = slice(h * HD, (h + 1) * HD)
            qrows = pl.ds(pl.multiple_of(i * qblock, qblock), qblock)
            krows = pl.ds(pl.multiple_of(j * qblock, qblock), qblock)
            query, grad = q_buf[qrows, cols], do_buf[qrows, cols]
            key, value = k_buf[krows, cols], v_buf[krows, cols]
            s = dot_nt(key, query) * (scale * LOG2E)
            p = jnp.exp2(s - lse_buf[h : h + 1, qrows])
            if diagonal:
                kp = lax.broadcasted_iota(jnp.int32, s.shape, 0)
                qp = lax.broadcasted_iota(jnp.int32, s.shape, 1)
                p = jnp.where(kp <= qp, p, 0.0)
            dp_blk = dot_nt(value, grad)
            ds = low(p * (dp_blk - delta[h : h + 1, qrows]))
            dv = dot_nn(low(p), grad)
            dk = dot_nn(ds, query)
            dq_acc[qrows, cols] += dot_tn(ds, key)
            if diagonal:
                dv_acc[krows, cols] = dv
                dk_acc[krows, cols] = dk
            else:
                dv_acc[krows, cols] += dv
                dk_acc[krows, cols] += dk

        def outer(j, carry):
            for h in range(heads):
                one(h, j, j, True)

            def inner(i, c):
                for h in range(heads):
                    one(h, i, j, False)
                return c

            lax.fori_loop(j + 1, blocks, inner, 0)
            return carry

        middle = blocks // 2
        lax.fori_loop(0, middle, outer, 0)
        start_sum(line - 1)
        lax.fori_loop(middle, blocks, outer, 0)
        sq_ref[...] = jnp.zeros_like(sq_ref)

        def finish_body(cos_blk, sin_blk, out_blk):
            rows = pl.ds(pl.multiple_of(pl.program_id(0) * block, block), block)
            cosine, sine = cos_blk[...], sin_blk[...]
            for which, acc in enumerate((dq_acc, dk_acc, dv_acc)):
                for h in range(heads):
                    at = which * qw + h * HD
                    g = acc[rows, h * HD : (h + 1) * HD]
                    if which < 2:
                        g = g * scale
                        first = g[:, :128]
                        first = first * cosine - turned(first) * sine
                        out_blk[:, at : at + 128] = low(first)
                        out_blk[:, at + 128 : at + HD] = low(g[:, 128:])
                    else:
                        out_blk[:, at : at + HD] = low(g)
                    sq_ref[:, at : at + HD] += jnp.sum(
                        out_blk[:, at : at + HD].astype(jnp.float32), axis=0, keepdims=True)

        pltpu.emit_pipeline(
            finish_body, grid=(total_len // block,), in_specs=[spec(128), spec(128)],
            out_specs=[spec(3 * qw)],
        )(cos_ref, sin_ref, dqkv_out)

    pl.run_scoped(
        attend_back,
        pltpu.VMEM((total_len, qw), jnp.bfloat16),
        pltpu.VMEM((total_len, qw), jnp.bfloat16),
        pltpu.VMEM((total_len, qw), jnp.bfloat16),
        pltpu.VMEM((heads, total_len), jnp.float32),
        pltpu.VMEM((total_len, qw), jnp.float32),
        pltpu.VMEM((total_len, qw), jnp.float32),
        pltpu.VMEM((total_len, qw), jnp.float32),
        pltpu.VMEM((heads, total_len), jnp.float32),
        pltpu.SemaphoreType.DMA((4,)),
    )

    def e_body(dqkv_blk, dfc_blk, x_blk, stat_blk, e_blk):
        mean, rstd = stat_blk[:, 0:1], stat_blk[:, 1:2]
        step = 512
        for at in range(0, width, step):
            cols = slice(at, at + step)
            d1 = dot_nt(dqkv_blk[:, :qw], wq_ref[0, cols, :])
            d1 += dot_nt(dqkv_blk[:, qw : 2 * qw], wq_ref[1, cols, :])
            d1 += dot_nt(dqkv_blk[:, 2 * qw :], wq_ref[2, cols, :])
            d2 = dot_nt(dfc_blk[...], w1_ref[cols, :])
            xhat = (x_blk[:, cols].astype(jnp.float32) - mean) * rstd
            e_blk[:, cols] = low(d1 * kvec[2:3, cols] + d2 * kvec[4:5, cols])
            ln_ref[0:1, cols] += jnp.sum(d1 * xhat, axis=0, keepdims=True)
            ln_ref[1:2, cols] += jnp.sum(d1, axis=0, keepdims=True)
            ln_ref[2:3, cols] += jnp.sum(d2 * xhat, axis=0, keepdims=True)
            ln_ref[3:4, cols] += jnp.sum(d2, axis=0, keepdims=True)

    wspec = lambda n: pl.BlockSpec((wblock, n), lambda i: (i, 0))
    pltpu.emit_pipeline(
        e_body, grid=(total_len // wblock,),
        in_specs=[wspec(3 * qw), wspec(ff), wspec(width), wspec(128)], out_specs=[wspec(width)],
    )(dqkv_out, dfc_out, x_all, stat_out, e_out)
    ends = [
        pltpu.make_async_copy(kvec, vec_out, keep.at[0]),
        pltpu.make_async_copy(sfc_ref, sfc_out, keep.at[1]),
        pltpu.make_async_copy(sq_ref, sq_out, keep.at[2]),
        pltpu.make_async_copy(ln_ref, ln_out, keep.at[3]),
    ]
    for copy in ends:
        copy.start()

    def hidden_body(ways):
        def run(x_blk, part_blk, *blks):
            total = x_blk[...].astype(jnp.float32) + part_blk[...].astype(jnp.float32)
            for blk in blks[:-1]:
                total = total + blk[...].astype(jnp.float32)
            blks[-1][...] = low(total + kvec[0:1] + kvec[1:2])

        pltpu.emit_pipeline(
            run, grid=(length // block,), in_specs=[spec(width)] * (2 + len(ways)),
            out_specs=[spec(width)],
        )(x_ref, part_out.at[rows_of(tp)], *[land_out.at[w, line - 2] for w in ways], hidden_out)

    for way in range(2):
        @pl.when(sum_arrives(way, line - 1))
        def _():
            sum_arrival(way, line - 1).wait_recv()

    @pl.when(tp == 0)
    def _():
        hidden_body([1])

    @pl.when(tp == line - 1)
    def _():
        hidden_body([0])

    @pl.when((tp > 0) & (tp < line - 1))
    def _():
        hidden_body([0, 1])

    for step in range(1, line):
        for way in range(2):
            @pl.when(sum_sends(way, step))
            def _():
                sum_copy(way, step, False).wait_send()

    for a in range(count):
        for slot in range(1 + 2 * hops):
            pair_copy(a, slot).wait_send()
        for hop in range(hops):
            for way in range(2):
                ring_copy(a, way, hop).wait_send()
    for b in range(2):
        for hop in range(line - 1):
            for way in range(2):
                @pl.when(sends(way, hop))
                def _():
                    line_copy(b, way, hop).wait_send()
    for copy in ends:
        copy.wait()


def head(small, wq, w1, wd, w2, x, cot, cosine, sine, n_q, n_b, dp_count, tp_count, collective_id):
    piece, width = x.shape
    length = piece * tp_count
    qw, ff = wd.shape[0], w2.shape[0]
    heads = qw // HD
    chips = dp_count // 2
    hops = chips // 2
    bf, f32 = jnp.bfloat16, jnp.float32
    sds = jax.ShapeDtypeStruct
    steps = max(tp_count - 1, 1)
    out_shape = [
        sds((length, width), bf), sds((length, width), bf),
        sds((length, width), bf), sds((length, width), bf),
        sds((length, qw), bf), sds((length, qw), bf), sds((length, qw), bf),
        sds((length, ff), bf), sds((length, ff), bf), sds((length, 128), f32),
        sds((length, qw), bf), sds((heads, length), f32), sds((length, width), bf),
        sds((length, qw), bf), sds((length, ff), bf),
        sds((2, steps, piece, width), bf), sds((2, steps, piece, width), bf),
        sds((length, 3 * qw), bf), sds((length, width), bf), sds((piece, width), bf),
        sds((8, width), f32), sds((1, ff), f32), sds((1, 3 * qw), f32), sds((8, width), f32),
    ]
    dma = pltpu.SemaphoreType.DMA
    hbm = pl.BlockSpec(memory_space=pl.ANY)
    line = max(tp_count - 1, 1)
    return pl.pallas_call(
        functools.partial(head_kernel, (chips, tp_count, heads, n_q, n_b)),
        out_shape=out_shape,
        in_specs=[hbm] * 9,
        out_specs=[hbm] * len(out_shape),
        scratch_shapes=[
            pltpu.VMEM((small.shape[0] * dp_count, 128), bf),
            pltpu.VMEM((3, width, qw), bf),
            pltpu.VMEM((width, ff), bf),
            pltpu.VMEM((qw, width), bf),
            pltpu.VMEM((ff, width), bf),
            pltpu.VMEM((8, width), f32),
            pltpu.VMEM((1, 3 * qw), f32),
            pltpu.VMEM((1, ff), f32),
            pltpu.VMEM((length, qw), bf),
            pltpu.VMEM((length, qw), bf),
            pltpu.VMEM((1, 3 * qw), f32),
            pltpu.VMEM((8, width), f32),
            dma((5, 2, hops)), dma((5, 2, hops)),
            dma((5, 1 + 2 * hops)), dma((5, 1 + 2 * hops)),
            dma((2, 2, line)), dma((2, 2, line)), dma((7,)),
            dma((2, line)), dma((2, line)), dma((4,)),
        ],
        compiler_params=pltpu.CompilerParams(
            collective_id=collective_id, has_side_effects=True,
            vmem_limit_bytes=62 * 1024 * 1024),
        name="head",
    )(small, wq, w1, wd, w2, x, cot, cosine, sine)


def tail_kernel(cfg, *refs):
    chips, line = cfg
    hops = chips // 2
    refs = list(refs)

    def take(n):
        out, refs[:n] = refs[:n], []
        return out

    act, heads_in, cot, n1, n2, dfc, dqkv, line_ref, flat_ref = take(9)
    own_fc2, own_dense, own_fc1, own_qkv, own_small = take(5)
    held, paired, landed, first_landed = take(4)
    small, s_held, s_paired, s_landed, line_land = take(5)
    (pair_send, pair_recv, ring_send, ring_recv, s_load, s_pair_send, s_pair_recv, s_ring_send,
     s_ring_recv, line_send, line_recv) = refs
    ff, qw = act.shape[1], heads_in.shape[1]
    length = act.shape[0]
    rows = held.shape[1]
    dp = lax.axis_index("dp")
    tp = lax.axis_index("tp")
    core = lax.rem(dp, 2)
    place = ring_place(lax.div(dp, 2), chips)

    def chip_at(ring_pos):
        return ring_place(lax.rem(ring_pos + chips, chips), chips)

    right, left = chip_at(place + 1) * 2 + core, chip_at(place - 1) * 2 + core
    sibling = dp + 1 - 2 * core
    barrier = pltpu.get_barrier_semaphore()
    for partner in (right, left, sibling):
        pl.semaphore_signal(barrier, 1, device_id={"dp": partner}, device_id_type=MESH)
    for n in range(1, line):
        pl.semaphore_signal(
            barrier, 1, device_id={"tp": lax.rem(tp + n, line)}, device_id_type=MESH)
    pl.semaphore_wait(barrier, 3 + line - 1)

    def line_copy(n):
        return pltpu.make_async_remote_copy(
            src_ref=line_ref, dst_ref=line_land.at[n - 1],
            send_sem=line_send.at[n - 1], recv_sem=line_recv.at[n - 1],
            device_id={"tp": lax.rem(tp + n, line)}, device_id_type=MESH)

    for n in range(1, line):
        line_copy(n).start()

    offsets = [hops]
    for near in range(hops - 1, 0, -1):
        offsets += [near, -near]
    offsets.append(0)
    own = chips - 1
    spans = [(0, ff), (ff, qw), (ff + qw, ff), (2 * ff + qw, 3 * qw)]

    def f32(value):
        return value.astype(jnp.float32)

    def over_rows(count, body):
        step = min(count, 32)

        def run(t, carry):
            body(pl.multiple_of(t * step, step), step)
            return carry

        lax.fori_loop(0, count // step, run, 0)

    def pair_arrival(slot, unit):
        at, wide = spans[unit]
        view = paired.at[slot, :, pl.ds(at, wide)]
        return pltpu.make_async_remote_copy(
            src_ref=view, dst_ref=view,
            send_sem=pair_send.at[slot, unit], recv_sem=pair_recv.at[slot, unit],
            device_id={"dp": sibling}, device_id_type=MESH)

    def pair_sum(slot, unit):
        at, wide = spans[unit]
        cols = slice(at, at + wide)
        pair_arrival(slot, unit).wait_recv()

        def body(r, n):
            r = pl.ds(r, n)
            held[slot, r, cols] = low(f32(held[slot, r, cols]) + f32(paired[slot, r, cols]))

        over_rows(rows, body)

    def slot_of(way, step):
        return offsets.index((hops - step) * (1 if way == 0 or step == 0 else -1))

    def ring_rows(way, step):
        return (way * (rows // 2), rows // 2) if step == 0 else (0, rows)

    def ring_copy(way, step, unit):
        at, wide = spans[unit]
        first, n = ring_rows(way, step)
        view = held.at[slot_of(way, step), pl.ds(first, n), pl.ds(at, wide)]
        if step == 0:
            dst = first_landed.at[pl.ds(first, n), pl.ds(at, wide)]
        else:
            dst = landed.at[way, step - 1, :, pl.ds(at, wide)]
        return pltpu.make_async_remote_copy(
            src_ref=view, dst_ref=dst,
            send_sem=ring_send.at[way, step, unit], recv_sem=ring_recv.at[way, step, unit],
            device_id={"dp": right if way == 0 else left}, device_id_type=MESH)

    def add_landed(way, step, unit):
        at, wide = spans[unit]
        cols = slice(at, at + wide)
        slot = slot_of(way, step + 1)
        first, n = ring_rows(way, step)
        ring_copy(way, step, unit).wait_recv()

        def body(r, size):
            r = pl.ds(pl.multiple_of(r + first, 16), size)
            if step == 0:
                moved = first_landed[r, cols]
            else:
                moved = landed[way, step - 1, r, cols]
            held[slot, r, cols] = low(f32(held[slot, r, cols]) + f32(moved))

        over_rows(n, body)

    def ring_after(slot, units):
        for step in range(hops):
            for way in range(2):
                if slot_of(way, step) != slot or slot == own:
                    continue
                for unit in units:
                    if step > 0:
                        add_landed(way, step - 1, unit)
                    ring_copy(way, step, unit).start()

    def compute(big, mid, lhs, turn, out, lhs_sem, big_sem, mid_sem):
        loads = [(cot, 0, slot) for slot in range(chips)]
        loads += [(src, 2, slot) for slot in range(chips) for src in (n2, n1)]

        def lhs_load(i):
            src, _, slot = loads[i]
            chip = chip_at(place + offsets[slot])
            cols = pl.ds(pl.multiple_of(chip * 2 * rows, 128), 2 * rows)
            return pltpu.make_async_copy(src.at[:, cols], lhs.at[i % 2], lhs_sem.at[i % 2])

        phase_loads = (
            (pltpu.make_async_copy(act, big, big_sem.at[0]),
             pltpu.make_async_copy(heads_in, mid.at[:, pl.ds(0, qw)], mid_sem.at[0])),
            (pltpu.make_async_copy(dfc, big, big_sem.at[1]),
             pltpu.make_async_copy(dqkv, mid, mid_sem.at[1])),
        )
        lhs_load(0).start()
        for copy in phase_loads[0]:
            copy.start()
        busy = [None, None]
        counter = 0
        pending = []

        def product(i, slot, unit, rhs):
            nonlocal counter
            at, wide = spans[unit]
            which = counter % 2
            counter += 1
            if busy[which] is not None:
                busy[which].wait_send()
            step = 512 if wide % 512 == 0 else 256
            for col in range(0, wide, step):
                out[which, :, col : col + step] = low(
                    dot_nn(turn[...], rhs[:, col : col + step]))
            mine = pl.ds(pl.multiple_of(core * rows, 16), rows)
            held[slot, :, at : at + wide] = out[which, mine, :wide]
            theirs = pl.ds(pl.multiple_of((1 - core) * rows, 16), rows)
            copy = pltpu.make_async_remote_copy(
                src_ref=out.at[which, theirs, pl.ds(0, wide)],
                dst_ref=paired.at[slot, :, pl.ds(at, wide)],
                send_sem=pair_send.at[slot, unit], recv_sem=pair_recv.at[slot, unit],
                device_id={"dp": sibling}, device_id_type=MESH)
            copy.start()
            busy[which] = copy
            while pending:
                pair_sum(*pending.pop(0))
            pending.append((slot, unit))

        def settle():
            while pending:
                pair_sum(*pending.pop(0))

        def left_side(i):
            lhs_load(i).wait()
            if i + 1 < len(loads):
                lhs_load(i + 1).start()
            turn[...] = lhs[i % 2].T

        for phase in range(2):
            units = (0, 1) if phase == 0 else (2, 3)
            for slot in range(chips):
                if phase == 0:
                    left_side(slot)
                    if slot == 0:
                        for copy in phase_loads[0]:
                            copy.wait()
                    product(slot, slot, 0, big)
                    product(slot, slot, 1, mid)
                else:
                    i = chips + 2 * slot
                    left_side(i)
                    if slot == 0:
                        phase_loads[1][0].wait()
                    product(i, slot, 2, big)
                    left_side(i + 1)
                    if slot == 0:
                        phase_loads[1][1].wait()
                    product(i + 1, slot, 3, mid)
                if slot == 0:
                    settle()
                    ring_after(0, units)
                elif slot == chips - 2:
                    settle()
                    for ready in range(1, chips - 1):
                        ring_after(ready, units)
            if phase == 0:
                for copy in phase_loads[1]:
                    copy.start()
        settle()
        for copy in busy:
            copy.wait_send()

    pl.run_scoped(
        compute,
        pltpu.VMEM((length, ff), jnp.bfloat16),
        pltpu.VMEM((length, 3 * qw), jnp.bfloat16),
        pltpu.VMEM((2, length, 2 * rows), jnp.bfloat16),
        pltpu.VMEM((2 * rows, length), jnp.bfloat16),
        pltpu.VMEM((2, 2 * rows, max(ff, 3 * qw)), jnp.bfloat16),
        pltpu.SemaphoreType.DMA((2,)),
        pltpu.SemaphoreType.DMA((2,)),
        pltpu.SemaphoreType.DMA((2,)),
    )

    for n in range(1, line):
        line_copy(n).wait_recv()
    total = line_ref[...]
    for n in range(1, line):
        total = total + line_land[n - 1]
    rows_z = line_ref.shape[1]
    small[:, :rows_z] = total
    small[:, rows_z:] = flat_ref[...]
    s_rows = small.shape[1]

    def s_pair(slot):
        chip = chip_at(place + offsets[slot])
        return pltpu.make_async_remote_copy(
            src_ref=small.at[chip * 2 + 1 - core], dst_ref=s_paired.at[slot],
            send_sem=s_pair_send.at[slot], recv_sem=s_pair_recv.at[slot],
            device_id={"dp": sibling}, device_id_type=MESH)

    def s_keep(slot):
        chip = chip_at(place + offsets[slot])
        return pltpu.make_async_copy(small.at[chip * 2 + core], s_held.at[slot], s_load.at[slot])

    def s_ring(way, step):
        n = s_rows // 2 if step == 0 else s_rows
        first = way * n if step == 0 else 0
        return pltpu.make_async_remote_copy(
            src_ref=s_held.at[slot_of(way, step), pl.ds(first, n)],
            dst_ref=s_landed.at[way, step, pl.ds(first, n)],
            send_sem=s_ring_send.at[way, step], recv_sem=s_ring_recv.at[way, step],
            device_id={"dp": right if way == 0 else left}, device_id_type=MESH)

    for slot in range(chips):
        s_keep(slot).start()
        s_pair(slot).start()
    for slot in range(chips):
        s_keep(slot).wait()
        s_pair(slot).wait_recv()
        s_held[slot] += s_paired[slot]
        for step in range(hops):
            for way in range(2):
                if slot_of(way, step) != slot or slot == own:
                    continue
                if step > 0:
                    n = s_rows // 2 if step == 1 else s_rows
                    first = way * n if step == 1 else 0
                    s_ring(way, step - 1).wait_recv()
                    s_held[slot, first : first + n] += s_landed[way, step - 1, first : first + n]
                s_ring(way, step).start()
    for way in range(2):
        s_ring(way, hops - 1).wait_recv()
    own_small[...] = s_held[own] + s_landed[0, hops - 1] + s_landed[1, hops - 1]

    def finish(wide_buf, tall_buf, done):
        targets = [
            (0, [own_fc2]), (1, [own_dense]), (2, [own_fc1]),
            (3, [own_qkv.at[w] for w in range(3)]),
        ]
        last = {}

        def total_at(unit, at, size):
            cols = slice(at, at + size)
            value = f32(held[own, :, cols])
            if hops == 1:
                return value + f32(first_landed[:, cols])
            return value + f32(landed[0, hops - 2, :, cols]) + f32(landed[1, hops - 2, :, cols])

        for unit, outs in targets:
            at, wide = spans[unit]
            for way in range(2):
                ring_copy(way, hops - 1, unit).wait_recv()
            if unit < 2:
                if "tall" in last:
                    last["tall"].wait()
                for col in range(0, wide, 256):
                    tall_buf[col : col + 256, :] = total_at(unit, at + col, 256).T
                copy = pltpu.make_async_copy(tall_buf.at[pl.ds(0, wide)], outs[0], done.at[0])
                copy.start()
                last["tall"] = copy
            else:
                if "wide" in last:
                    for copy in last["wide"]:
                        copy.wait()
                for col in range(0, wide, 256):
                    wide_buf[:, col : col + 256] = total_at(unit, at + col, 256)
                each = wide // len(outs)
                copies = [
                    pltpu.make_async_copy(
                        wide_buf.at[:, pl.ds(w * each, each)], out, done.at[1 + w])
                    for w, out in enumerate(outs)
                ]
                for copy in copies:
                    copy.start()
                last["wide"] = copies
        last["tall"].wait()
        for copy in last["wide"]:
            copy.wait()

    pl.run_scoped(
        finish,
        pltpu.VMEM((rows, max(ff, 3 * qw)), jnp.float32),
        pltpu.VMEM((max(ff, qw), rows), jnp.float32),
        pltpu.SemaphoreType.DMA((4,)),
    )
    for way in range(2):
        for step in range(hops):
            for unit in range(4):
                ring_copy(way, step, unit).wait_send()
            s_ring(way, step).wait_send()
    for slot in range(chips):
        s_pair(slot).wait_send()
    for n in range(1, line):
        line_copy(n).wait_send()


def tail(act, heads_in, cot, n1, n2, dfc, dqkv, line_sums, flat_sums, dp_count, tp_count, collective_id):
    chips = dp_count // 2
    hops = chips // 2
    length, ff = act.shape
    qw = heads_in.shape[1]
    rows = cot.shape[1] // dp_count
    cols = 2 * ff + 4 * qw
    rows_s = line_sums.shape[1] + flat_sums.shape[1]
    bf, f32 = jnp.bfloat16, jnp.float32
    dma = pltpu.SemaphoreType.DMA
    hbm = pl.BlockSpec(memory_space=pl.ANY)
    vm = pl.BlockSpec(memory_space=pltpu.VMEM)
    line = max(tp_count - 1, 1)
    sds = jax.ShapeDtypeStruct
    return pl.pallas_call(
        functools.partial(tail_kernel, (chips, tp_count)),
        out_shape=[
            sds((ff, rows), f32), sds((qw, rows), f32), sds((rows, ff), f32),
            sds((3, rows, qw), f32), sds((rows_s, 128), f32),
        ],
        in_specs=[hbm] * 7 + [vm, vm],
        out_specs=[hbm] * 4 + [vm],
        scratch_shapes=[
            pltpu.VMEM((chips, rows, cols), bf),
            pltpu.VMEM((chips, rows, cols), bf),
            pltpu.VMEM((2, max(hops - 1, 1), rows, cols), bf),
            pltpu.VMEM((rows, cols), bf),
            pltpu.VMEM((dp_count, rows_s, 128), f32),
            pltpu.VMEM((chips, rows_s, 128), f32),
            pltpu.VMEM((chips, rows_s, 128), f32),
            pltpu.VMEM((2, hops, rows_s, 128), f32),
            pltpu.VMEM((line,) + line_sums.shape, f32),
            dma((chips, 4)), dma((chips, 4)), dma((2, hops, 4)), dma((2, hops, 4)),
            dma((chips,)), dma((chips,)), dma((chips,)), dma((2, hops)), dma((2, hops)),
            dma((line,)), dma((line,)),
        ],
        compiler_params=pltpu.CompilerParams(
            collective_id=collective_id, has_side_effects=True,
            vmem_limit_bytes=62 * 1024 * 1024),
        cost_estimate=pl.CostEstimate(
            flops=2 * length * cot.shape[1] * cols, bytes_accessed=400_000_000, transcendentals=0),
        name="tail",
    )(act, heads_in, cot, n1, n2, dfc, dqkv, line_sums, flat_sums)


def pack_small(wide, narrow):
    rows = []
    first = jnp.concatenate([part.reshape(-1, 128) for part in wide], axis=0)
    rows.append(jnp.pad(first, ((0, 16 - first.shape[0]), (0, 0))))
    count = 0
    for part in narrow:
        flat = part.reshape(-1)
        need = -(-flat.size // 128)
        rows.append(jnp.pad(flat, (0, need * 128 - flat.size)).reshape(need, 128))
        count += need
    rows.append(jnp.zeros((16 - count, 128), jnp.bfloat16))
    return jnp.concatenate(rows, axis=0)


def by_owner(rows, dp_count):
    count = -(-rows.shape[1] // 2048) * 16
    padded = jnp.pad(rows, ((0, 0), (0, count * 128 - rows.shape[1])))
    return padded.reshape(dp_count, count, 128)


def body(
    hidden_in,
    triple_projection_weight,
    triple_projection_bias,
    attention_out_weight,
    b_dense,
    feedforward_in_weight,
    feedforward_in_bias,
    feedforward_out_weight,
    b_fc2,
    ln1_gain,
    ln1_bias,
    ln2_gain,
    ln2_bias,
    grad_out,
):
    _, piece_len, width = hidden_in.shape
    tp_count = lax.axis_size("tp")
    dp_count = lax.axis_size("dp")
    length = piece_len * tp_count
    cosine, sine = rotary_tables(length)
    small = pack_small(
        [b_dense, b_fc2, ln1_gain, ln1_bias, ln2_gain, ln2_bias],
        [triple_projection_bias, feedforward_in_bias],
    )
    n_q = -(-triple_projection_bias.size // 128)
    n_b = -(-feedforward_in_bias.size // 128)
    outs = head(
        small,
        triple_projection_weight.transpose(1, 0, 2),
        feedforward_in_weight,
        attention_out_weight,
        feedforward_out_weight,
        hidden_in[0],
        grad_out[0],
        cosine,
        sine,
        n_q,
        n_b,
        dp_count,
        tp_count,
        0,
    )
    _, cot_seq, norm_one, norm_two = outs[:4]
    act, head_out, d_fc = outs[7], outs[10], outs[14]
    d_qkv, e_sum, hidden_out, vectors, sum_bfc1, sum_bqkv, ln_sums = outs[17:]
    e_piece = lax.psum_scatter(e_sum, "tp", scatter_dimension=0, tiled=True)

    cot_piece = grad_out[0].astype(jnp.float32)
    line_sums = ln_sums[:5].reshape(5, dp_count, -1).transpose(1, 0, 2).reshape(dp_count, -1)
    flat_sums = jnp.concatenate([sum_bqkv, sum_bfc1], axis=1).reshape(-1, dp_count).T
    line_rows, flat_rows = by_owner(line_sums, dp_count), by_owner(flat_sums, dp_count)
    own_fc2, own_dense, own_fc1, own_qkv, own_small = tail(
        act, head_out, cot_seq, norm_one, norm_two, d_fc, d_qkv, line_rows, flat_rows,
        dp_count, tp_count, 1,
    )
    nothing = own_small[-1, -1]
    own_fc2, own_dense, own_fc1, own_qkv = [
        own + nothing for own in (own_fc2, own_dense, own_fc1, own_qkv)
    ]
    e_piece, own_small = lax.optimization_barrier((e_piece, own_small))
    e_piece = e_piece.astype(jnp.float32)
    own_line = own_small[: line_rows.shape[1]].reshape(-1)[: line_sums.shape[1]].reshape(5, -1)
    own_flat = own_small[line_rows.shape[1] :].reshape(-1)[: flat_sums.shape[1]]
    split = sum_bqkv.size // dp_count

    x_own = hidden_in[0].astype(jnp.float32)
    mean = jnp.mean(x_own, axis=-1, keepdims=True)
    centered = x_own - mean
    rstd = lax.rsqrt(jnp.mean(centered * centered, axis=-1, keepdims=True) + EPSILON)
    xhat = centered * rstd
    back = (
        e_piece
        - jnp.mean(e_piece, axis=-1, keepdims=True)
        - xhat * jnp.mean(e_piece * xhat, axis=-1, keepdims=True)
    ) * rstd
    grad_in = (cot_piece + back)[None]
    return (
        hidden_out[None],
        grad_in,
        own_qkv.transpose(1, 0, 2),
        own_flat[:split].reshape(triple_projection_bias.shape),
        own_dense,
        own_line[4],
        own_fc1,
        own_flat[split:].reshape(feedforward_in_bias.shape),
        own_fc2,
        own_line[4],
        own_line[0],
        own_line[1],
        own_line[2],
        own_line[3],
    )


def solution(mesh):
    return jax.shard_map(
        body,
        mesh=mesh,
        in_specs=(
            P("dp", "tp", None),
            P("dp", None, "tp"),
            P(None, "tp", "dp"),
            P("tp", "dp"),
            P("dp"),
            P("dp", "tp"),
            P("tp", "dp"),
            P("tp", "dp"),
            P("dp"),
            P("dp"),
            P("dp"),
            P("dp"),
            P("dp"),
            P("dp", "tp", None),
        ),
        out_specs=(
            P("dp", "tp", None),
            P("dp", "tp", None),
            P("dp", None, "tp"),
            P(None, "tp", "dp"),
            P("tp", "dp"),
            P("dp"),
            P("dp", "tp"),
            P("tp", "dp"),
            P("tp", "dp"),
            P("dp"),
            P("dp"),
            P("dp"),
            P("dp"),
            P("dp"),
        ),
        check_vma=False,
    )
```
